32 devices in a mesh: dp: 8 (over y, x, core), seq: 4 (over z).
Axes of the slice: x: 2, y: 2, z: 4, core: 2. Of those that a mesh axis runs over, the one named last changes fastest.
Arguments:
- hidden_in: bfloat16 [64, 256, 768], P('dp', 'seq'), may hold values from -6 to 6
- patches: bfloat16 [64, 1024, 768], P('dp', 'seq'), may hold values from -6 to 6
- text_lengths: int32 [8, 8], P('dp'), may hold values from 1 to 256, 1024 in all within a row
- patch_counts: int32 [64], P('dp'), may hold values from 256 to 1024, as said below
- cotangent: bfloat16 [64, 256, 768], P('dp', 'seq'), may hold values from -6 to 6
- g_self: float32 [768], replicated, may hold values from 0.25 to 1.75
- g_cross: float32 [768], replicated, may hold values from 0.25 to 1.75
- g_mlp: float32 [768], replicated, may hold values from 0.25 to 1.75
- w_query: bfloat16 [768, 768], replicated, may hold values from -0.21875 to 0.21875
- w_key: bfloat16 [768, 768], replicated, may hold values from -0.21875 to 0.21875
- w_value: bfloat16 [768, 768], replicated, may hold values from -0.21875 to 0.21875
- w_out: bfloat16 [768, 768], replicated, may hold values from -0.875 to 0.875
- c_query: bfloat16 [768, 768], replicated, may hold values from -0.21875 to 0.21875
- c_key: bfloat16 [768, 768], replicated, may hold values from -0.21875 to 0.21875
- c_value: bfloat16 [768, 768], replicated, may hold values from -0.21875 to 0.21875
- c_out: bfloat16 [768, 768], replicated, may hold values from -1.75 to 1.75
- w_gate: bfloat16 [768, 2048], replicated, may hold values from -0.21875 to 0.21875
- w_up: bfloat16 [768, 2048], replicated, may hold values from -0.21875 to 0.21875
- w_down: bfloat16 [2048, 768], replicated, may hold values from -0.125 to 0.125
Outputs:
- layer_out: float32 [64, 256, 768], P('dp', 'seq')
- grad_x: float32 [64, 256, 768], P('dp', 'seq')
- grad_patches: float32 [64, 1024, 768], P('dp', 'seq')
- grad_g_self: float32 [768], P('dp')
- grad_g_cross: float32 [768], P('dp')
- grad_g_mlp: float32 [768], P('dp')
- grad_w_query: float32 [768, 768], P('dp', 'seq')
- grad_w_key: float32 [768, 768], P('dp', 'seq')
- grad_w_value: float32 [768, 768], P('dp', 'seq')
- grad_w_out: float32 [768, 768], P('dp', 'seq')
- grad_c_query: float32 [768, 768], P('dp', 'seq')
- grad_c_key: float32 [768, 768], P('dp', 'seq')
- grad_c_value: float32 [768, 768], P('dp', 'seq')
- grad_c_out: float32 [768, 768], P('dp', 'seq')
- grad_w_gate: float32 [768, 2048], P('dp', 'seq')
- grad_w_up: float32 [768, 2048], P('dp', 'seq')
- grad_w_down: float32 [2048, 768], P('dp', 'seq')
- rms_values: float32 [7], replicated
The draws below stay inside these ranges and needn't reach their ends.
Inputs may be any that keep to these rules, and one draw needn't show every extreme that they name: `text_lengths`: each row holds 8 lengths summing to 1024, one of them exactly 256. `patch_counts`: each count is 256 or 1024; both occur in every draw.
All inputs are finite; a program needn't handle non-finite values.
Results may differ from the reference program's by a relative error of at most 0.022.
Values may be sent and summed in bfloat16 or wider, within the bound.
A program may use at most 256 MiB of HBM per device.

```python
import math
import jax
import jax.numpy as jnp
import numpy as np
from jax import lax

D = 768
FF = 2048
HEADS = 12
HEAD_DIM = 64
TEXT = 256
PATCHES = 1024
EX_DEV = 8
GROUPS = 8
EXAMPLES = 64


def draw_patch_counts(key, part):
    key = jax.random.fold_in(key, 11)
    keys = jax.random.split(key, 4)
    shares = jax.random.randint(keys[0], (EXAMPLES // EX_DEV,), 0, 60)
    rolled = jax.random.randint(keys[1], (EXAMPLES,), 0, 100)
    example_idx = jnp.arange(EXAMPLES)
    group_idx = example_idx // EX_DEV
    large = rolled < shares[group_idx]
    first_big = jax.random.randint(keys[2], (), 0, EXAMPLES)
    first_small = (first_big + 1 + jax.random.randint(keys[3], (), 0, EXAMPLES - 1)) % EXAMPLES
    large = (large | (example_idx == first_big)) & (example_idx != first_small)
    return jnp.where(large, PATCHES, PATCHES // 4).astype(jnp.int32)


def strengthened(drawn, stream_key, source, target, blocks, factor):
    owner, partner = [(jnp.arange(drawn.shape[position]) // (drawn.shape[position] // blocks)).reshape([-1 if axis == position else 1 for axis in range(drawn.ndim)]) for position in (source, target)]
    chosen = jax.random.permutation(stream_key, blocks)[partner]
    strong = (owner == chosen) | (owner == (partner + blocks // 2) % blocks)
    return jnp.where(strong, factor * drawn, drawn)


def steps_of(key, extent, shards, low, high):
    gain, own = 1.0, jax.random.fold_in(key, 6)
    for dim, shards_of in shards:
        heights = jnp.exp(jax.random.uniform(jax.random.fold_in(own, dim), (shards_of,), jnp.float32, low / len(shards), high / len(shards)))
        gain = gain * jnp.repeat(heights, extent[dim] // shards_of).reshape([-1 if axis == dim else 1 for axis in range(len(extent))])
    return gain


def split_up(count, total, bound, lean):
    portions = [(1 << 20) // math.isqrt(standing ** lean) + 1 for standing in range(2, count + 1)]
    spare, counts = total - bound - (count - 1), [1] * (count - 1)
    while spare > 0:
        movable = [i for i in range(count - 1) if counts[i] < bound]
        pool, budget = sum([portions[i] for i in movable]), spare
        for i in movable:
            addition = min(bound - counts[i], max(1, budget * portions[i] // pool), spare)
            counts[i] = counts[i] + addition
            spare = spare - addition
    return np.array([bound] + counts)


def uneven(key, amount, total, reach, lean):
    if amount == 2:
        one = jax.random.randint(key, (), max(1, total - reach), min(reach, total - 1) + 1)
        return jnp.stack([one, total - one])
    lengths = jnp.asarray(split_up(amount, total, reach, lean), jnp.int32)
    couples = (amount - 1) // 2
    giver, sink = lengths[1:1 + 2 * couples:2], lengths[2:2 + 2 * couples:2]
    room = jnp.minimum(giver - 1, reach - sink)
    moved = jax.random.randint(jax.random.fold_in(key, 1), (couples,), 0, 1 << 20) % (room + 1)
    lengths = lengths.at[1:1 + 2 * couples:2].set(giver - moved).at[2:2 + 2 * couples:2].set(sink + moved)
    return lengths[jax.random.permutation(jax.random.fold_in(key, 2), amount)]


def gaussian(own_key, extent, scale, most, cuts=(), dtype=jnp.bfloat16):
    entries = scale * jax.random.normal(own_key, extent, jnp.float32)
    if cuts:
        entries = entries * steps_of(own_key, extent, cuts, -0.22, 0.18)
    return jnp.clip(entries, -most, most).astype(dtype)


def heavy_noise(own_key, dims, deviation, most, cuts, heavy, dtype=jnp.bfloat16):
    drawn = deviation * jax.random.normal(own_key, dims, jnp.float32)
    if cuts:
        drawn = drawn * steps_of(own_key, dims, cuts, -0.22, 0.18)
    return jnp.clip(strengthened(drawn, jax.random.fold_in(own_key, 3), *heavy), -most, most).astype(dtype)


def setup_inputs(seed: int = 0) -> dict:
    seeds = jax.random.split(jax.random.key(seed), 20)
    return {
        "hidden_in": heavy_noise(seeds[0], (EXAMPLES, TEXT, D), 1.0, 6.0, ((0, 8), (1, 4)), (0, 2, 8, 2.0)),
        "patches": heavy_noise(seeds[1], (EXAMPLES, PATCHES, D), 1.0, 6.0, ((0, 8), (1, 4)), (0, 2, 8, 2.0)),
        "text_lengths": jax.vmap(lambda own: uneven(own, EX_DEV, EX_DEV * TEXT // 2, TEXT, 1))(jax.random.split(seeds[2], GROUPS)).reshape((GROUPS, EX_DEV)).astype(jnp.int32),
        "patch_counts": draw_patch_counts(jax.random.fold_in(seeds[19], 71), 0),
        "cotangent": gaussian(seeds[4], (EXAMPLES, TEXT, D), 1.0, 6.0, ((0, 8), (1, 4))),
        "g_self": jnp.clip(1.0 + 0.15 * jax.random.normal(seeds[5], (D,), jnp.float32), 0.25, 1.75),
        "g_cross": jnp.clip(1.0 + 0.15 * jax.random.normal(seeds[6], (D,), jnp.float32), 0.25, 1.75),
        "g_mlp": jnp.clip(1.0 + 0.15 * jax.random.normal(seeds[7], (D,), jnp.float32), 0.25, 1.75),
        "w_query": gaussian(seeds[8], (D, D), D ** -0.5, 0.21875),
        "w_key": gaussian(seeds[9], (D, D), D ** -0.5, 0.21875),
        "w_value": gaussian(seeds[10], (D, D), D ** -0.5, 0.21875),
        "w_out": gaussian(seeds[11], (D, D), (D // 16) ** -0.5, 0.875),
        "c_query": gaussian(seeds[12], (D, D), D ** -0.5, 0.21875),
        "c_key": gaussian(seeds[13], (D, D), D ** -0.5, 0.21875),
        "c_value": gaussian(seeds[14], (D, D), D ** -0.5, 0.21875),
        "c_out": gaussian(seeds[15], (D, D), (D // 64) ** -0.5, 1.75),
        "w_gate": gaussian(seeds[16], (D, FF), D ** -0.5, 0.21875),
        "w_up": gaussian(seeds[17], (D, FF), D ** -0.5, 0.21875),
        "w_down": gaussian(seeds[18], (FF, D), FF ** -0.5, 0.125),
    }


NORM_EPS = 1e-06
NEG_FILL = -1e+30
GELU_CURVE = 0.7978845608028654
HIGHEST_PREC = lax.Precision.HIGHEST

@jax.custom_vjp
def low(v):
    return lax.optimization_barrier(v.astype(jnp.bfloat16)).astype(jnp.float32)

@jax.custom_vjp
def low_back(v):
    return v

def low_keep(v):
    return (low(v), None)

def low_pass(kept, grad):
    return (grad,)

def back_keep(v):
    return (v, None)

def back_low(kept, grad):
    return (low(grad),)
low.defvjp(low_keep, low_pass)
low_back.defvjp(back_keep, back_low)

def gelu_tanh(value_in):
    return 0.5 * value_in * (1.0 + jnp.tanh(GELU_CURVE * (value_in + 0.044715 * value_in * value_in * value_in)))

def rms_norm(value_in, gain_vec):
    return value_in * lax.rsqrt(lax.optimization_barrier(jnp.mean(value_in * value_in, axis=-1, keepdims=True)) + NORM_EPS) * gain_vec

def project(rows_in, weight):
    return jnp.einsum('btd,de->bte', rows_in, weight, precision=HIGHEST_PREC)

def attend_example(queries, key_rows, value_rows, allowed):
    query_heads = queries.reshape(queries.shape[0], HEADS, HEAD_DIM)
    key_heads = key_rows.reshape(key_rows.shape[0], HEADS, HEAD_DIM)
    value_heads = value_rows.reshape(value_rows.shape[0], HEADS, HEAD_DIM)
    scores = low_back(0.125 * jnp.einsum('qhd,khd->hqk', query_heads, key_heads, precision=HIGHEST_PREC))
    scores = jnp.where(allowed[None], scores, NEG_FILL)
    row_top = lax.optimization_barrier(jnp.max(scores, axis=-1, keepdims=True))
    exp_scores = jnp.exp(scores - row_top)
    probs_all = exp_scores / lax.optimization_barrier(jnp.sum(exp_scores, axis=-1, keepdims=True))
    mixed = jnp.einsum('hqk,khd->qhd', low(probs_all), value_heads, precision=HIGHEST_PREC)
    return mixed.reshape(queries.shape[0], D)

def attend_checked(entry):
    return jax.checkpoint(attend_example)(entry[0], entry[1], entry[2], entry[3])

def attention(queries, key_rows, value_rows, masks):
    return lax.map(attend_checked, (queries, key_rows, value_rows, masks))

def layer_block(x_group, patch_group, len_group, count_group, weights):
    g_self, g_cross, g_mlp, w_query, w_key, w_value, w_out, c_query, c_key, c_value, c_out, w_gate, w_up, w_down = weights
    text_pos = jnp.arange(TEXT)
    patch_pos = jnp.arange(PATCHES)
    key_ok = text_pos[None, None, :] < len_group[:, None, None]
    self_mask = key_ok & (text_pos[None, None, :] <= text_pos[None, :, None])
    cross_mask = jnp.broadcast_to((patch_pos[None, :] < count_group[:, None])[:, None, :], (EX_DEV, TEXT, PATCHES))
    text_valid = (text_pos[None, :] < len_group[:, None]).astype(jnp.float32)[..., None]
    normed_one = low(rms_norm(x_group, g_self))
    self_q = low(low_back(project(normed_one, w_query)))
    self_k = low(low_back(project(normed_one, w_key)))
    self_v = low(low_back(project(normed_one, w_value)))
    self_rows = low(low_back(attention(self_q, self_k, self_v, self_mask)))
    self_branch = low_back(project(self_rows, w_out))
    after_self = x_group + self_branch
    normed_two = low(rms_norm(after_self, g_cross))
    cross_q = low(low_back(project(normed_two, c_query)))
    cross_k = low(low_back(project(patch_group, c_key)))
    cross_v = low(low_back(project(patch_group, c_value)))
    cross_rows = low(low_back(attention(cross_q, cross_k, cross_v, cross_mask)))
    cross_branch = low_back(project(cross_rows, c_out))
    after_cross = after_self + cross_branch
    normed_three = low(rms_norm(after_cross, g_mlp))
    gate_pre = low_back(project(normed_three, w_gate))
    up_pre = low_back(project(normed_three, w_up))
    hidden_value = gelu_tanh(gate_pre) * up_pre
    mlp_branch = low_back(project(low(hidden_value), w_down))
    layer_out = after_cross + mlp_branch
    branch_sums = jnp.stack([jnp.sum(text_valid * self_branch * self_branch), jnp.sum(text_valid * cross_branch * cross_branch), jnp.sum(text_valid * mlp_branch * mlp_branch), jnp.sum(text_valid * hidden_value * hidden_value)])
    return (layer_out, branch_sums)

def reference(hidden_in, patches, text_lengths, patch_counts, cotangent, g_self, g_cross, g_mlp, w_query, w_key, w_value, w_out, c_query, c_key, c_value, c_out, w_gate, w_up, w_down):
    weights = tuple((weight.astype(jnp.float32) for weight in (g_self, g_cross, g_mlp, w_query, w_key, w_value, w_out, c_query, c_key, c_value, c_out, w_gate, w_up, w_down)))
    x_groups = hidden_in.astype(jnp.float32).reshape(GROUPS, EX_DEV, TEXT, D)
    patch_groups = patches.astype(jnp.float32).reshape(GROUPS, EX_DEV, PATCHES, D)
    len_groups = text_lengths.astype(jnp.int32).reshape(GROUPS, EX_DEV)
    count_groups = patch_counts.astype(jnp.int32).reshape(GROUPS, EX_DEV)

    def forward(x_all, patch_all, weight_all):

        def per_group(group_item):
            return jax.checkpoint(layer_block)(group_item[0], group_item[1], group_item[2], group_item[3], weight_all)
        return lax.map(per_group, (x_all, patch_all, len_groups, count_groups))
    outputs_y, pullback, branch_sums = jax.vjp(forward, x_groups, patch_groups, weights, has_aux=True)
    text_valid = (jnp.arange(TEXT)[None, None, :] < len_groups[:, :, None]).astype(jnp.float32)
    patch_valid = (jnp.arange(PATCHES)[None, None, :] < count_groups[:, :, None]).astype(jnp.float32)
    grad_y = cotangent.astype(jnp.float32).reshape(GROUPS, EX_DEV, TEXT, D) * text_valid[..., None]
    grad_in, grad_patch, grad_weights = pullback(grad_y)
    n_text = jnp.sum(text_valid)
    n_patch = jnp.sum(patch_valid)
    totals = lax.optimization_barrier(jnp.sum(branch_sums, axis=0))
    out_sq = jnp.sum(text_valid[..., None] * outputs_y * outputs_y)
    grad_sq = jnp.sum(text_valid[..., None] * grad_in * grad_in)
    patch_sq = jnp.sum(patch_valid[..., None] * grad_patch * grad_patch)
    rms_values = jnp.sqrt(jnp.stack([out_sq / (n_text * D), totals[0] / (n_text * D), totals[1] / (n_text * D), totals[2] / (n_text * D), totals[3] / (n_text * FF), grad_sq / (n_text * D), patch_sq / (n_patch * D)]))
    return (outputs_y.reshape(EXAMPLES, TEXT, D), grad_in.reshape(EXAMPLES, TEXT, D), grad_patch.reshape(EXAMPLES, PATCHES, D), grad_weights[0], grad_weights[1], grad_weights[2], grad_weights[3], grad_weights[4], grad_weights[5], grad_weights[6], grad_weights[7], grad_weights[8], grad_weights[9], grad_weights[10], grad_weights[11], grad_weights[12], grad_weights[13], rms_values)
```

```python
from functools import partial

import jax
import jax.numpy as jnp
from jax import lax
from jax.experimental import pallas as pl
from jax.experimental.pallas import tpu as pltpu
from jax.sharding import PartitionSpec as P

HEAD_DIM = 64
LANES = 128
PAIR = LANES // HEAD_DIM
NORM_EPS = 1e-06
NEG_FILL = -1e30
GELU_CURVE = 0.7978845608028654
F32 = jnp.float32
BF16 = jnp.bfloat16
MESH = pl.DeviceIdType.MESH
VMEM_LIMIT = 48 * 1024 * 1024


def dot_nn(a, b):
    return lax.dot_general(a, b, (((1,), (0,)), ((), ())), preferred_element_type=F32)


def dot_nt(a, b):
    return lax.dot_general(a, b, (((1,), (1,)), ((), ())), preferred_element_type=F32)


def dot_tn(a, b):
    return lax.dot_general(a, b, (((0,), (0,)), ((), ())), preferred_element_type=F32)


def head_mask(h, dtype):
    lane = lax.broadcasted_iota(jnp.int32, (1, LANES), 1)
    return ((lane // HEAD_DIM) == h).astype(F32).astype(dtype)


def causal_scores(raw, limit):
    key_pos = lax.broadcasted_iota(jnp.int32, raw.shape, 0)
    query_pos = lax.broadcasted_iota(jnp.int32, raw.shape, 1)
    return jnp.where((key_pos <= query_pos) & (key_pos < limit), raw, NEG_FILL)


def forward_pair(q, k, v, limit, causal):
    v_t = v.T
    mixes, norms = [], []
    for h in range(PAIR):
        q_h = q * (head_mask(h, BF16) * 0.125)
        scores = dot_nt(k, q_h)
        if causal:
            scores = causal_scores(scores, limit)
        top = jnp.max(scores, axis=0, keepdims=True)
        exps = jnp.exp(scores - top)
        total = jnp.sum(exps, axis=0, keepdims=True)
        mixed = dot_nn(v_t[h * HEAD_DIM : (h + 1) * HEAD_DIM], exps.astype(BF16))
        mixes.append(mixed / total)
        norms.append(top + jnp.log(total))
    return jnp.concatenate(mixes, axis=0).T.astype(BF16), jnp.concatenate(norms, axis=0)


def backward_pair(q, k, v, grad_mix, norms, limit, causal):
    k_t = k.T * 0.125
    grad_q, grad_k, grad_v = [], 0.0, 0.0
    for h in range(PAIR):
        mask = head_mask(h, BF16)
        q_h = q * (mask * 0.125)
        scores = dot_nt(k, q_h)
        if causal:
            scores = causal_scores(scores, limit)
        probs = jnp.exp(scores - norms[h : h + 1])
        grad_h = grad_mix * mask
        grad_v = grad_v + dot_nn(probs.astype(BF16), grad_h)
        grad_p = dot_nt(v, grad_h)
        inner = jnp.sum(probs * grad_p, axis=0, keepdims=True)
        grad_s = (probs * (grad_p - inner)).astype(BF16)
        grad_k = grad_k + dot_nn(grad_s, q_h)
        grad_q.append(dot_nn(k_t[h * HEAD_DIM : (h + 1) * HEAD_DIM], grad_s))
    grad_q = jnp.concatenate(grad_q, axis=0).T
    return grad_q.astype(BF16), grad_k.astype(BF16), grad_v.astype(BF16)


def self_forward_kernel(limit_ref, q_ref, k_ref, v_ref, mix_ref, norm_ref):
    limit = limit_ref[pl.program_id(0)]
    mix, norms = forward_pair(q_ref[...], k_ref[...], v_ref[...], limit, True)
    mix_ref[...] = mix
    norm_ref[0, 0, 0:PAIR] = norms


def self_backward_kernel(
    limit_ref, q_ref, k_ref, v_ref, grad_ref, norm_ref, dq_ref, dk_ref, dv_ref
):
    limit = limit_ref[pl.program_id(0)]
    dq, dk, dv = backward_pair(
        q_ref[...], k_ref[...], v_ref[...], grad_ref[...], norm_ref[0, 0, 0:PAIR], limit, True
    )
    dq_ref[...] = dq
    dk_ref[...] = dk
    dv_ref[...] = dv


def cross_forward_kernel(limit_ref, q_ref, k_ref, v_ref, mix_ref, norm_ref):
    limit = limit_ref[pl.program_id(0)]
    keys = k_ref.shape[0]
    short = keys // 4

    def run(count):
        mix, norms = forward_pair(q_ref[...], k_ref[0:count], v_ref[0:count], None, False)
        mix_ref[...] = mix
        norm_ref[0, 0, 0:PAIR] = norms

    pl.when(limit > short)(lambda: run(keys))
    pl.when(limit <= short)(lambda: run(short))


def cross_backward_kernel(
    limit_ref, q_ref, k_ref, v_ref, grad_ref, norm_ref, dq_ref, dk_ref, dv_ref
):
    limit = limit_ref[pl.program_id(0)]
    keys = k_ref.shape[0]
    short = keys // 4

    def run(count):
        dq, dk, dv = backward_pair(
            q_ref[...],
            k_ref[0:count],
            v_ref[0:count],
            grad_ref[...],
            norm_ref[0, 0, 0:PAIR],
            None,
            False,
        )
        dq_ref[...] = dq
        dk_ref[0:count] = dk
        dv_ref[0:count] = dv
        if count < keys:
            dk_ref[count:] = jnp.zeros((keys - count, LANES), BF16)
            dv_ref[count:] = jnp.zeros((keys - count, LANES), BF16)

    pl.when(limit > short)(lambda: run(keys))
    pl.when(limit <= short)(lambda: run(short))


def attend(kernel, limits, arrays, norms, examples, flops):
    width = arrays[0].shape[1]
    pairs = width // LANES
    queries = arrays[0].shape[0] // examples

    def rows_spec(array):
        return pl.BlockSpec((array.shape[0] // examples, LANES), lambda e, p: (e, p))

    norm_spec = pl.BlockSpec((1, 1, 8, queries), lambda e, p: (e, p, 0, 0))
    norm_shape = jax.ShapeDtypeStruct((examples, pairs, 8, queries), F32)
    in_specs = [pl.BlockSpec(memory_space=pltpu.SMEM)] + [rows_spec(a) for a in arrays]
    args = (limits,) + tuple(arrays)
    if norms is None:
        out_shape = (jax.ShapeDtypeStruct(arrays[0].shape, BF16), norm_shape)
        out_specs = (rows_spec(arrays[0]), norm_spec)
    else:
        in_specs.append(norm_spec)
        args = args + (norms,)
        out_shape = tuple(jax.ShapeDtypeStruct(a.shape, BF16) for a in arrays[:3])
        out_specs = tuple(rows_spec(a) for a in arrays[:3])
    return pl.pallas_call(
        kernel,
        grid=(examples, pairs),
        in_specs=in_specs,
        out_specs=out_specs,
        out_shape=out_shape,
        compiler_params=pltpu.CompilerParams(vmem_limit_bytes=VMEM_LIMIT),
        cost_estimate=pl.CostEstimate(
            flops=flops, bytes_accessed=sum(a.size * 2 for a in arrays), transcendentals=0
        ),
    )(*args)


def sum_small_kernel(n_dp, n_seq, own_ref, out_ref, slots, send_sem, recv_sem):
    n = n_dp * n_seq
    me = lax.axis_index("dp") * n_seq + lax.axis_index("seq")

    def place(index):
        return (index // n_seq, lax.rem(index, n_seq))

    barrier = pltpu.get_barrier_semaphore()

    def greet(off, carry):
        pl.semaphore_signal(
            barrier, inc=1, device_id=place(lax.rem(me + off, n)), device_id_type=MESH
        )
        return carry

    lax.fori_loop(1, n, greet, 0)
    pl.semaphore_wait(barrier, n - 1)

    def copy_to(off):
        return pltpu.make_async_remote_copy(
            src_ref=own_ref,
            dst_ref=slots.at[me],
            send_sem=send_sem.at[off],
            recv_sem=recv_sem.at[off],
            device_id=place(lax.rem(me + off, n)),
            device_id_type=MESH,
        )

    def start(off, carry):
        copy_to(off).start()
        return carry

    def finish(off, carry):
        copy_to(off).wait()
        return carry

    lax.fori_loop(1, n, start, 0)
    slots[me] = own_ref[...]
    lax.fori_loop(1, n, finish, 0)
    out_ref[...] = lax.fori_loop(
        1, n, lambda i, total: total + slots[i], slots[0]
    )


def sum_small(vector, n_dp, n_seq):
    n = n_dp * n_seq
    return pl.pallas_call(
        partial(sum_small_kernel, n_dp, n_seq),
        out_shape=jax.ShapeDtypeStruct(vector.shape, F32),
        in_specs=[pl.BlockSpec(memory_space=pltpu.VMEM)],
        out_specs=pl.BlockSpec(memory_space=pltpu.VMEM),
        scratch_shapes=[
            pltpu.VMEM((n,) + vector.shape, F32),
            pltpu.SemaphoreType.DMA((n,)),
            pltpu.SemaphoreType.DMA((n,)),
        ],
        compiler_params=pltpu.CompilerParams(
            collective_id=0, has_side_effects=True, vmem_limit_bytes=VMEM_LIMIT
        ),
    )(vector)


def norm_forward(u, gain):
    r = lax.rsqrt(jnp.mean(u * u, axis=-1, keepdims=True) + NORM_EPS)
    return (u * r * gain).astype(BF16)


def norm_backward(u, gain, w):
    r = lax.rsqrt(jnp.mean(u * u, axis=-1, keepdims=True) + NORM_EPS)
    gw = gain * w
    grad = r * gw - u * (r * r * r) * jnp.mean(gw * u, axis=-1, keepdims=True)
    return grad, jnp.sum(w * u * r, axis=0)


def to_examples(rows):
    n = lax.axis_size("seq")
    examples, part, width = rows.shape
    parts = lax.all_to_all(rows.reshape(n, examples // n, part, width), "seq", 0, 0)
    return parts.transpose(1, 0, 2, 3).reshape(examples // n, n * part, width)


def to_positions(rows):
    n = lax.axis_size("seq")
    own, positions, width = rows.shape
    parts = rows.reshape(own, n, positions // n, width).transpose(1, 0, 2, 3)
    return lax.all_to_all(parts, "seq", 0, 0).reshape(n * own, positions // n, width)


def halve_over_dp(matrix, bits):
    n = lax.axis_size("dp")
    count = n.bit_length() - 1
    rows, width = matrix.shape[0] // n, matrix.shape[1]
    place = lax.axis_index("dp")
    left = list(range(count))[::-1]
    current = matrix.reshape((2,) * count + (rows, width))
    for bit in bits:
        axis = left.index(bit)
        mine = (place >> bit) & 1
        keep = lax.dynamic_index_in_dim(current, mine, axis, keepdims=False)
        give = lax.dynamic_index_in_dim(current, 1 - mine, axis, keepdims=False)
        got = lax.ppermute(give, "dp", [(i, i ^ (1 << bit)) for i in range(n)])
        current = (keep.astype(F32) + got.astype(F32)).astype(BF16)
        left.remove(bit)
    return current


def scatter_over_seq(matrix):
    n = lax.axis_size("seq")
    rows, width = matrix.shape
    parts = matrix.reshape(rows, n, width // n).transpose(1, 0, 2)
    return jnp.sum(lax.all_to_all(parts, "seq", 0, 0).astype(F32), axis=0)


def reduce_grad(matrix, order):
    n = lax.axis_size("dp")
    bits = list(range(n.bit_length() - 1))
    if order:
        bits = bits[:1] + bits[1:][::-1]
    return scatter_over_seq(halve_over_dp(matrix, bits))


def local(
    hidden_in,
    patches,
    text_lengths,
    patch_counts,
    cotangent,
    g_self,
    g_cross,
    g_mlp,
    w_query,
    w_key,
    w_value,
    w_out,
    c_query,
    c_key,
    c_value,
    c_out,
    w_gate,
    w_up,
    w_down,
):
    n_seq = lax.axis_size("seq")
    n_dp = lax.axis_size("dp")
    seq_place = lax.axis_index("seq")
    dp_place = lax.axis_index("dp")
    width = hidden_in.shape[2]
    ff_width = w_gate.shape[1]
    own = hidden_in.shape[0] // n_seq
    lengths = lax.dynamic_slice_in_dim(text_lengths[0], seq_place * own, own)
    counts = lax.dynamic_slice_in_dim(patch_counts, seq_place * own, own)

    hidden = to_examples(hidden_in)
    patch = to_examples(patches)
    cot = to_examples(cotangent)
    text = hidden.shape[1]
    slots = patch.shape[1]
    text_valid = (jnp.arange(text)[None, :] < lengths[:, None]).astype(F32).reshape(-1, 1)
    patch_valid = (jnp.arange(slots)[None, :] < counts[:, None]).astype(F32).reshape(-1, 1)
    x = hidden.reshape(-1, width).astype(F32)
    patch = patch.reshape(-1, width)
    self_flops = 4 * own * text * text * width
    cross_flops = 4 * own * text * slots * width

    normed_one = norm_forward(x, g_self)
    self_q = dot_nn(normed_one, w_query).astype(BF16)
    self_k = dot_nn(normed_one, w_key).astype(BF16)
    self_v = dot_nn(normed_one, w_value).astype(BF16)
    self_mix, self_norms = attend(
        self_forward_kernel, lengths, (self_q, self_k, self_v), None, own, self_flops
    )
    self_branch = dot_nn(self_mix, w_out)
    after_self = x + self_branch
    normed_two = norm_forward(after_self, g_cross)
    cross_q = dot_nn(normed_two, c_query).astype(BF16)
    cross_k = dot_nn(patch, c_key).astype(BF16)
    cross_v = dot_nn(patch, c_value).astype(BF16)
    cross_mix, cross_norms = attend(
        cross_forward_kernel, counts, (cross_q, cross_k, cross_v), None, own, cross_flops
    )
    cross_branch = dot_nn(cross_mix, c_out)
    after_cross = after_self + cross_branch
    normed_three = norm_forward(after_cross, g_mlp)
    gate = dot_nn(normed_three, w_gate)
    up = dot_nn(normed_three, w_up)
    tanh_part = jnp.tanh(GELU_CURVE * (gate + 0.044715 * gate * gate * gate))
    gelu = 0.5 * gate * (1.0 + tanh_part)
    gelu_slope = 0.5 * (1.0 + tanh_part) + 0.5 * gate * (1.0 - tanh_part * tanh_part) * (
        GELU_CURVE * (1.0 + 3.0 * 0.044715 * gate * gate)
    )
    hidden_value = gelu * up
    hidden_low = hidden_value.astype(BF16)
    mlp_branch = dot_nn(hidden_low, w_down)
    layer_rows = after_cross + mlp_branch
    layer_out = to_positions(layer_rows.astype(BF16).reshape(own, text, width)).astype(F32)

    grad_y = cot.reshape(-1, width).astype(F32) * text_valid
    grad_mlp = grad_y.astype(BF16)
    grad_w_down = dot_tn(hidden_low, grad_mlp).astype(BF16)
    grad_hidden = dot_nt(grad_mlp, w_down)
    grad_gate = (grad_hidden * up * gelu_slope).astype(BF16)
    grad_up = (grad_hidden * gelu).astype(BF16)
    grad_w_gate = dot_tn(normed_three, grad_gate).astype(BF16)
    grad_w_up = dot_tn(normed_three, grad_up).astype(BF16)
    grad_w_down = reduce_grad(grad_w_down, 0)
    grad_w_gate = reduce_grad(grad_w_gate, 1)
    grad_w_up = reduce_grad(grad_w_up, 0)
    grad_three = dot_nt(grad_gate, w_gate) + dot_nt(grad_up, w_up)
    norm_grad, grad_g_mlp = norm_backward(after_cross, g_mlp, grad_three)
    grad_after_cross = grad_y + norm_grad

    grad_cbranch = grad_after_cross.astype(BF16)
    grad_c_out = reduce_grad(dot_tn(cross_mix, grad_cbranch).astype(BF16), 1)
    grad_cmix = dot_nt(grad_cbranch, c_out).astype(BF16)
    grad_cq, grad_ck, grad_cv = attend(
        cross_backward_kernel,
        counts,
        (cross_q, cross_k, cross_v, grad_cmix),
        cross_norms,
        own,
        cross_flops * 5 // 2,
    )
    grad_patch_rows = dot_nt(grad_ck, c_key) + dot_nt(grad_cv, c_value)
    grad_patches = to_positions(
        grad_patch_rows.astype(BF16).reshape(own, slots, width)
    ).astype(F32)
    grad_c_query = reduce_grad(dot_tn(normed_two, grad_cq).astype(BF16), 0)
    grad_c_key = reduce_grad(dot_tn(patch, grad_ck).astype(BF16), 1)
    grad_c_value = reduce_grad(dot_tn(patch, grad_cv).astype(BF16), 0)
    grad_two = dot_nt(grad_cq, c_query)
    norm_grad, grad_g_cross = norm_backward(after_self, g_cross, grad_two)
    grad_after_self = grad_after_cross + norm_grad

    grad_sbranch = grad_after_self.astype(BF16)
    grad_w_out = reduce_grad(dot_tn(self_mix, grad_sbranch).astype(BF16), 1)
    grad_smix = dot_nt(grad_sbranch, w_out).astype(BF16)
    grad_sq, grad_sk, grad_sv = attend(
        self_backward_kernel,
        lengths,
        (self_q, self_k, self_v, grad_smix),
        self_norms,
        own,
        self_flops * 5 // 2,
    )
    grad_w_query = reduce_grad(dot_tn(normed_one, grad_sq).astype(BF16), 0)
    grad_w_key = reduce_grad(dot_tn(normed_one, grad_sk).astype(BF16), 1)
    grad_w_value = reduce_grad(dot_tn(normed_one, grad_sv).astype(BF16), 0)
    grad_one = dot_nt(grad_sq, w_query) + dot_nt(grad_sk, w_key) + dot_nt(grad_sv, w_value)
    norm_grad, grad_g_self = norm_backward(x, g_self, grad_one)
    grad_x_rows = grad_after_self + norm_grad
    grad_x = to_positions(grad_x_rows.astype(BF16).reshape(own, text, width)).astype(F32)

    stats = jnp.stack(
        [
            jnp.sum(text_valid * layer_rows * layer_rows),
            jnp.sum(text_valid * self_branch * self_branch),
            jnp.sum(text_valid * cross_branch * cross_branch),
            jnp.sum(text_valid * mlp_branch * mlp_branch),
            jnp.sum(text_valid * hidden_value * hidden_value),
            jnp.sum(text_valid * grad_x_rows * grad_x_rows),
            jnp.sum(patch_valid * grad_patch_rows * grad_patch_rows),
            jnp.sum(text_valid),
            jnp.sum(patch_valid),
        ]
    )
    small = jnp.concatenate([grad_g_self, grad_g_cross, grad_g_mlp, stats])
    padded = -(-small.shape[0] // (8 * LANES)) * 8 * LANES
    small = jnp.pad(small, (0, padded - small.shape[0])).reshape(-1, LANES)
    total = sum_small(small, n_dp, n_seq).reshape(-1)
    part = width // n_dp
    gains = [
        lax.dynamic_slice_in_dim(total, i * width + dp_place * part, part) for i in range(3)
    ]
    stats = total[3 * width : 3 * width + 9]
    per_text = stats[7] * width
    rms_values = jnp.sqrt(
        stats[:7]
        / jnp.stack(
            [per_text, per_text, per_text, per_text, stats[7] * ff_width, per_text, stats[8] * width]
        )
    )
    return (
        layer_out,
        grad_x,
        grad_patches,
        gains[0],
        gains[1],
        gains[2],
        grad_w_query,
        grad_w_key,
        grad_w_value,
        grad_w_out,
        grad_c_query,
        grad_c_key,
        grad_c_value,
        grad_c_out,
        grad_w_gate,
        grad_w_up,
        grad_w_down,
        rms_values,
    )


def solution(mesh):
    rows = P("dp", "seq", None)
    tile = P("dp", "seq")
    in_specs = (rows, rows, P("dp", None), P("dp"), rows) + (P(),) * 14
    out_specs = (rows,) * 3 + (P("dp"),) * 3 + (tile,) * 11 + (P(),)
    return jax.shard_map(local, mesh=mesh, in_specs=in_specs, out_specs=out_specs, check_vma=False)
```

```python
from functools import partial

import jax
import jax.numpy as jnp
from jax import lax
from jax.experimental import pallas as pl
from jax.experimental.pallas import tpu as pltpu
from jax.sharding import PartitionSpec as P

HEAD_DIM = 64
LANES = 128
PAIR = LANES // HEAD_DIM
NORM_EPS = 1e-06
NEG_FILL = -1e30
GELU_CURVE = 0.7978845608028654
F32 = jnp.float32
BF16 = jnp.bfloat16
MESH = pl.DeviceIdType.MESH
VMEM_LIMIT = 48 * 1024 * 1024


def dot_nn(a, b):
    return lax.dot_general(a, b, (((1,), (0,)), ((), ())), preferred_element_type=F32)


def dot_nt(a, b):
    return lax.dot_general(a, b, (((1,), (1,)), ((), ())), preferred_element_type=F32)


def dot_tn(a, b):
    return lax.dot_general(a, b, (((0,), (0,)), ((), ())), preferred_element_type=F32)


def head_mask(h, dtype):
    lane = lax.broadcasted_iota(jnp.int32, (1, LANES), 1)
    return ((lane // HEAD_DIM) == h).astype(F32).astype(dtype)


def causal_scores(raw, limit):
    key_pos = lax.broadcasted_iota(jnp.int32, raw.shape, 0)
    query_pos = lax.broadcasted_iota(jnp.int32, raw.shape, 1)
    return jnp.where((key_pos <= query_pos) & (key_pos < limit), raw, NEG_FILL)


def forward_pair(q, k, v, limit, causal):
    v_t = v.T
    mixes, norms = [], []
    for h in range(PAIR):
        q_h = q * (head_mask(h, BF16) * 0.125)
        scores = dot_nt(k, q_h)
        if causal:
            scores = causal_scores(scores, limit)
        top = jnp.max(scores, axis=0, keepdims=True)
        exps = jnp.exp(scores - top)
        total = jnp.sum(exps, axis=0, keepdims=True)
        mixed = dot_nn(v_t[h * HEAD_DIM : (h + 1) * HEAD_DIM], exps.astype(BF16))
        mixes.append(mixed / total)
        norms.append(top + jnp.log(total))
    return jnp.concatenate(mixes, axis=0).T.astype(BF16), jnp.concatenate(norms, axis=0)


def backward_pair(q, k, v, grad_mix, norms, limit, causal):
    k_t = k.T * 0.125
    grad_q, grad_k, grad_v = [], 0.0, 0.0
    for h in range(PAIR):
        mask = head_mask(h, BF16)
        q_h = q * (mask * 0.125)
        scores = dot_nt(k, q_h)
        if causal:
            scores = causal_scores(scores, limit)
        probs = jnp.exp(scores - norms[h : h + 1])
        grad_h = grad_mix * mask
        grad_v = grad_v + dot_nn(probs.astype(BF16), grad_h)
        grad_p = dot_nt(v, grad_h)
        inner = jnp.sum(probs * grad_p, axis=0, keepdims=True)
        grad_s = (probs * (grad_p - inner)).astype(BF16)
        grad_k = grad_k + dot_nn(grad_s, q_h)
        grad_q.append(dot_nn(k_t[h * HEAD_DIM : (h + 1) * HEAD_DIM], grad_s))
    grad_q = jnp.concatenate(grad_q, axis=0).T
    return grad_q.astype(BF16), grad_k.astype(BF16), grad_v.astype(BF16)


def self_forward_kernel(limit_ref, q_ref, k_ref, v_ref, mix_ref, norm_ref):
    limit = limit_ref[pl.program_id(0)]
    mix, norms = forward_pair(q_ref[...], k_ref[...], v_ref[...], limit, True)
    mix_ref[...] = mix
    norm_ref[0, 0, 0:PAIR] = norms


def self_backward_kernel(
    limit_ref, q_ref, k_ref, v_ref, grad_ref, norm_ref, dq_ref, dk_ref, dv_ref
):
    limit = limit_ref[pl.program_id(0)]
    dq, dk, dv = backward_pair(
        q_ref[...], k_ref[...], v_ref[...], grad_ref[...], norm_ref[0, 0, 0:PAIR], limit, True
    )
    dq_ref[...] = dq
    dk_ref[...] = dk
    dv_ref[...] = dv


def cross_forward_kernel(limit_ref, q_ref, k_ref, v_ref, mix_ref, norm_ref):
    limit = limit_ref[pl.program_id(0)]
    keys = k_ref.shape[0]
    short = keys // 4

    def run(count):
        mix, norms = forward_pair(q_ref[...], k_ref[0:count], v_ref[0:count], None, False)
        mix_ref[...] = mix
        norm_ref[0, 0, 0:PAIR] = norms

    pl.when(limit > short)(lambda: run(keys))
    pl.when(limit <= short)(lambda: run(short))


def cross_backward_kernel(
    limit_ref, q_ref, k_ref, v_ref, grad_ref, norm_ref, dq_ref, dk_ref, dv_ref
):
    limit = limit_ref[pl.program_id(0)]
    keys = k_ref.shape[0]
    short = keys // 4

    def run(count):
        dq, dk, dv = backward_pair(
            q_ref[...],
            k_ref[0:count],
            v_ref[0:count],
            grad_ref[...],
            norm_ref[0, 0, 0:PAIR],
            None,
            False,
        )
        dq_ref[...] = dq
        dk_ref[0:count] = dk
        dv_ref[0:count] = dv
        if count < keys:
            dk_ref[count:] = jnp.zeros((keys - count, LANES), BF16)
            dv_ref[count:] = jnp.zeros((keys - count, LANES), BF16)

    pl.when(limit > short)(lambda: run(keys))
    pl.when(limit <= short)(lambda: run(short))


def attend(kernel, limits, arrays, norms, examples, flops):
    width = arrays[0].shape[1]
    pairs = width // LANES
    queries = arrays[0].shape[0] // examples

    def rows_spec(array):
        return pl.BlockSpec((array.shape[0] // examples, LANES), lambda e, p: (e, p))

    norm_spec = pl.BlockSpec((1, 1, 8, queries), lambda e, p: (e, p, 0, 0))
    norm_shape = jax.ShapeDtypeStruct((examples, pairs, 8, queries), F32)
    in_specs = [pl.BlockSpec(memory_space=pltpu.SMEM)] + [rows_spec(a) for a in arrays]
    args = (limits,) + tuple(arrays)
    if norms is None:
        out_shape = (jax.ShapeDtypeStruct(arrays[0].shape, BF16), norm_shape)
        out_specs = (rows_spec(arrays[0]), norm_spec)
    else:
        in_specs.append(norm_spec)
        args = args + (norms,)
        out_shape = tuple(jax.ShapeDtypeStruct(a.shape, BF16) for a in arrays[:3])
        out_specs = tuple(rows_spec(a) for a in arrays[:3])
    return pl.pallas_call(
        kernel,
        grid=(examples, pairs),
        in_specs=in_specs,
        out_specs=out_specs,
        out_shape=out_shape,
        compiler_params=pltpu.CompilerParams(vmem_limit_bytes=VMEM_LIMIT),
        cost_estimate=pl.CostEstimate(
            flops=flops, bytes_accessed=sum(a.size * 2 for a in arrays), transcendentals=0
        ),
    )(*args)


def ordered(value, *before):
    return lax.optimization_barrier((value,) + before)[0]


def reduce_kernel(count, groups, *refs):
    n_seq = lax.axis_size("seq")
    ins, small_in = refs[:count], refs[count]
    parts, small_out = refs[count + 1 : count + 3], refs[count + 3]
    scratch = refs[count + 4 :]
    own, got_core = scratch[:count], scratch[count : 2 * count]
    got_two, got_three = scratch[2 * count : 3 * count], scratch[3 * count : 4 * count]
    cut = scratch[4 * count : 4 * count + 2]
    small_own, small_got, small_seq = scratch[4 * count + 2 : 4 * count + 5]
    load_sem, send_sem, recv_sem, small_send, small_recv, cut_send, cut_recv = scratch[
        4 * count + 5 :
    ]
    dp = lax.axis_index("dp")
    seq = lax.axis_index("seq")
    core, x, y = dp % 2, (dp // 2) % 2, dp // 4
    to_core = (dp + 1 - 2 * core, seq)
    to_x = (dp + 2 - 4 * x, seq)
    to_y = (dp + 4 - 8 * y, seq)
    seq_peers = [(seq + off) % n_seq for off in range(1, n_seq)]

    barrier = pltpu.get_barrier_semaphore()
    for peer in [to_core, to_x, to_y] + [(dp, z) for z in seq_peers]:
        pl.semaphore_signal(barrier, inc=1, device_id=peer, device_id_type=MESH)
    pl.semaphore_wait(barrier, 3 + len(seq_peers))

    def remote(src, dst, send, recv, device):
        copy = pltpu.make_async_remote_copy(
            src_ref=src,
            dst_ref=dst,
            send_sem=send,
            recv_sem=recv,
            device_id=device,
            device_id_type=MESH,
        )
        copy.start()
        return copy

    def add(out, got):
        rows = out.shape[0]
        step = 32 if rows % 32 == 0 else rows

        def body(i, carry):
            at = pl.ds(pl.multiple_of(i * step, step), step)
            out[at, :] = (out[at, :].astype(F32) + got[at, :].astype(F32)).astype(BF16)
            return carry

        lax.fori_loop(0, rows // step, body, 0)

    loads, first = [], []
    for u in range(count):
        load = pltpu.make_async_copy(ins[u].at[:, :, core], own[u], load_sem.at[u])
        load.start()
        loads.append(load)
        first.append(
            remote(
                ins[u].at[:, :, 1 - core], got_core[u], send_sem.at[0, u], recv_sem.at[0, u], to_core
            )
        )
    small = [remote(small_in, small_got.at[0], small_send.at[0], small_recv.at[0], to_core)]

    second = []
    for u in range(count):
        loads[u].wait()
        first[u].wait_recv()
        for i in range(2):
            for j in range(2):
                add(own[u].at[i, j], got_core[u].at[i, j])
        src, device = (own[u].at[1 - y], to_y) if u % 2 else (own[u].at[:, 1 - x], to_x)
        second.append(remote(src, got_two[u], send_sem.at[1, u], recv_sem.at[1, u], device))
    small[0].wait_recv()
    small_own[0] = small_in[...] + small_got[0]
    small.append(
        remote(small_own.at[0], small_got.at[1], small_send.at[1], small_recv.at[1], to_x)
    )

    third = []
    for u in range(count):
        second[u].wait_recv()
        for i in range(2):
            add(own[u].at[y, i] if u % 2 else own[u].at[i, x], got_two[u].at[i])
        src, device = (own[u].at[y, 1 - x], to_x) if u % 2 else (own[u].at[1 - y, x], to_y)
        third.append(remote(src, got_three[u], send_sem.at[2, u], recv_sem.at[2, u], device))
    small[1].wait_recv()
    small_own[1] = small_own[0] + small_got[1]
    small.append(
        remote(small_own.at[1], small_got.at[2], small_send.at[2], small_recv.at[2], to_y)
    )

    cuts = []
    for number, (buffer, row, rows, members) in enumerate(groups):
        for u in members:
            third[u].wait_recv()
        halves = [own[u][y, x].astype(F32) + got_three[u][...].astype(F32) for u in members]
        if len(members) == 1:
            halves = [halves[0][:rows], halves[0][rows:]]
        part = halves[0].shape[1] // n_seq
        at = pl.ds(row, rows)
        for z in range(n_seq):
            block = [h[:, z * part : (z + 1) * part] for h in halves]
            cut[buffer][z, at] = jnp.concatenate(block, axis=1).astype(BF16)
        parts[buffer][seq, at] = cut[buffer][seq, at]
        for k, z in enumerate(seq_peers):
            cuts.append(
                remote(
                    cut[buffer].at[z, at],
                    parts[buffer].at[seq, at],
                    cut_send.at[number, k],
                    cut_recv.at[number, k],
                    (dp, z),
                )
            )
    small[2].wait_recv()
    small_own[2] = small_own[1] + small_got[2]
    small_seq[seq] = small_own[2]
    for k, z in enumerate(seq_peers):
        small.append(
            remote(
                small_own.at[2], small_seq.at[seq], small_send.at[3 + k], small_recv.at[3 + k], (dp, z)
            )
        )
    for copy in cuts + small[3:]:
        copy.wait_recv()
    total = small_seq[0]
    for z in range(1, n_seq):
        total = total + small_seq[z]
    small_out[...] = total
    for copy in first + second + third + cuts + small:
        copy.wait_send()


def finish_kernel(groups, narrow_ref, wide_ref, *out_refs):
    for buffer, row, rows, members in groups:
        ref = (narrow_ref, wide_ref)[buffer]
        total = ref[0, row : row + rows].astype(F32)
        for z in range(1, ref.shape[0]):
            total = total + ref[z, row : row + rows].astype(F32)
        part = total.shape[1] // 2
        if len(members) == 2:
            out_refs[members[0]][...] = total[:, :part]
            out_refs[members[1]][...] = total[:, part:]
        else:
            out_refs[members[0]][0:rows] = total[:, :part]
            out_refs[members[0]][rows:] = total[:, part:]


def reduce_all(grads, small, n_dp, n_seq):
    count = len(grads)
    width = grads[0].shape[1]
    rows, part = width // n_dp, width // n_seq
    if n_dp != 8 or rows % 16 or (2 * part) % LANES:
        return tuple(reduce_grad(g, u % 2) for u, g in enumerate(grads)), lax.psum(
            small, ("dp", "seq")
        )
    square = count - 3
    gate, up, down = square, square + 1, square + 2
    half = grads[down].shape[0] // n_dp // 2
    narrow_rows = square // 2 * rows + half
    wide_lanes = 2 * grads[gate].shape[1] // n_seq
    groups = ((1, 0, rows, (gate, up)), (0, square // 2 * rows, half, (down,))) + tuple(
        (0, i * rows, rows, (2 * i, 2 * i + 1)) for i in range(square // 2)
    )
    order = [gate, up, down] + list(range(square))
    place = {u: i for i, u in enumerate(order)}
    sent = tuple((b, r, n, tuple(place[u] for u in m)) for b, r, n, m in groups)
    ins = []
    for u in order:
        r, c = grads[u].shape
        ins.append(grads[u].reshape(2, 2, 2, r // n_dp, c))
    slices = [g.shape[3:] for g in ins]
    buffers = (
        jax.ShapeDtypeStruct((n_seq, narrow_rows, 2 * part), BF16),
        jax.ShapeDtypeStruct((n_seq, rows, wide_lanes), BF16),
    )
    vmem = pl.BlockSpec(memory_space=pltpu.VMEM)
    narrow, wide, total = pl.pallas_call(
        partial(reduce_kernel, count, sent),
        out_shape=buffers + (jax.ShapeDtypeStruct(small.shape, F32),),
        in_specs=[pl.BlockSpec(memory_space=pl.ANY)] * count + [vmem],
        out_specs=(vmem,) * 3,
        scratch_shapes=[pltpu.VMEM((2, 2) + s, BF16) for s in slices]
        + [pltpu.VMEM((2, 2) + s, BF16) for s in slices]
        + [pltpu.VMEM((2,) + s, BF16) for s in slices]
        + [pltpu.VMEM(s, BF16) for s in slices]
        + [pltpu.VMEM(b.shape, BF16) for b in buffers]
        + [pltpu.VMEM((3,) + small.shape, F32)] * 2
        + [
            pltpu.VMEM((n_seq,) + small.shape, F32),
            pltpu.SemaphoreType.DMA((count,)),
            pltpu.SemaphoreType.DMA((3, count)),
            pltpu.SemaphoreType.DMA((3, count)),
            pltpu.SemaphoreType.DMA((3 + n_seq,)),
            pltpu.SemaphoreType.DMA((3 + n_seq,)),
            pltpu.SemaphoreType.DMA((len(sent), n_seq)),
            pltpu.SemaphoreType.DMA((len(sent), n_seq)),
        ],
        compiler_params=pltpu.CompilerParams(
            collective_id=0, has_side_effects=True, vmem_limit_bytes=VMEM_LIMIT
        ),
    )(*ins, small)
    results = pl.pallas_call(
        partial(finish_kernel, groups),
        out_shape=tuple(
            jax.ShapeDtypeStruct((g.shape[0] // n_dp, g.shape[1] // n_seq), F32) for g in grads
        ),
        in_specs=[vmem] * 2,
        out_specs=(vmem,) * count,
        compiler_params=pltpu.CompilerParams(vmem_limit_bytes=VMEM_LIMIT),
    )(narrow, wide)
    return tuple(results), total


def norm_forward(u, gain):
    r = lax.rsqrt(jnp.mean(u * u, axis=-1, keepdims=True) + NORM_EPS)
    return (u * r * gain).astype(BF16)


def norm_backward(u, gain, w):
    r = lax.rsqrt(jnp.mean(u * u, axis=-1, keepdims=True) + NORM_EPS)
    gw = gain * w
    grad = r * gw - u * (r * r * r) * jnp.mean(gw * u, axis=-1, keepdims=True)
    return grad, jnp.sum(w * u * r, axis=0)


def to_examples(rows):
    n = lax.axis_size("seq")
    examples, part, width = rows.shape
    parts = lax.all_to_all(rows.reshape(n, examples // n, part, width), "seq", 0, 0)
    return parts.transpose(1, 0, 2, 3).reshape(examples // n, n * part, width)


def to_positions(rows):
    n = lax.axis_size("seq")
    own, positions, width = rows.shape
    parts = rows.reshape(own, n, positions // n, width).transpose(1, 0, 2, 3)
    return lax.all_to_all(parts, "seq", 0, 0).reshape(n * own, positions // n, width)


def halve_over_dp(matrix, bits):
    n = lax.axis_size("dp")
    count = n.bit_length() - 1
    rows, width = matrix.shape[0] // n, matrix.shape[1]
    place = lax.axis_index("dp")
    left = list(range(count))[::-1]
    current = matrix.reshape((2,) * count + (rows, width))
    for bit in bits:
        axis = left.index(bit)
        mine = (place >> bit) & 1
        keep = lax.dynamic_index_in_dim(current, mine, axis, keepdims=False)
        give = lax.dynamic_index_in_dim(current, 1 - mine, axis, keepdims=False)
        got = lax.ppermute(give, "dp", [(i, i ^ (1 << bit)) for i in range(n)])
        current = (keep.astype(F32) + got.astype(F32)).astype(BF16)
        left.remove(bit)
    return current


def scatter_over_seq(matrix):
    n = lax.axis_size("seq")
    rows, width = matrix.shape
    parts = matrix.reshape(rows, n, width // n).transpose(1, 0, 2)
    return jnp.sum(lax.all_to_all(parts, "seq", 0, 0).astype(F32), axis=0)


def reduce_grad(matrix, order):
    n = lax.axis_size("dp")
    bits = list(range(n.bit_length() - 1))
    if order:
        bits = bits[:1] + bits[1:][::-1]
    return scatter_over_seq(halve_over_dp(matrix, bits))


def local(
    hidden_in,
    patches,
    text_lengths,
    patch_counts,
    cotangent,
    g_self,
    g_cross,
    g_mlp,
    w_query,
    w_key,
    w_value,
    w_out,
    c_query,
    c_key,
    c_value,
    c_out,
    w_gate,
    w_up,
    w_down,
):
    n_seq = lax.axis_size("seq")
    n_dp = lax.axis_size("dp")
    seq_place = lax.axis_index("seq")
    dp_place = lax.axis_index("dp")
    width = hidden_in.shape[2]
    ff_width = w_gate.shape[1]
    own = hidden_in.shape[0] // n_seq
    lengths = lax.dynamic_slice_in_dim(text_lengths[0], seq_place * own, own)
    counts = lax.dynamic_slice_in_dim(patch_counts, seq_place * own, own)

    hidden = to_examples(hidden_in)
    patch = to_examples(patches)
    text = hidden.shape[1]
    slots = patch.shape[1]
    text_valid = (jnp.arange(text)[None, :] < lengths[:, None]).astype(F32).reshape(-1, 1)
    patch_valid = (jnp.arange(slots)[None, :] < counts[:, None]).astype(F32).reshape(-1, 1)
    x = hidden.reshape(-1, width).astype(F32)
    patch = patch.reshape(-1, width)
    self_flops = 4 * own * text * text * width
    cross_flops = 4 * own * text * slots * width

    normed_one = norm_forward(x, g_self)
    self_q = dot_nn(normed_one, w_query).astype(BF16)
    self_k = dot_nn(normed_one, w_key).astype(BF16)
    self_v = dot_nn(normed_one, w_value).astype(BF16)
    self_mix, self_norms = attend(
        self_forward_kernel, lengths, (self_q, self_k, self_v), None, own, self_flops
    )
    cot = to_examples(ordered(cotangent, self_mix))
    self_branch = dot_nn(self_mix, w_out)
    after_self = x + self_branch
    normed_two = norm_forward(after_self, g_cross)
    cross_q = dot_nn(normed_two, c_query).astype(BF16)
    cross_k = dot_nn(patch, c_key).astype(BF16)
    cross_v = dot_nn(patch, c_value).astype(BF16)
    cross_mix, cross_norms = attend(
        cross_forward_kernel, counts, (cross_q, cross_k, cross_v), None, own, cross_flops
    )
    cross_branch = dot_nn(cross_mix, c_out)
    after_cross = after_self + cross_branch
    normed_three = norm_forward(after_cross, g_mlp)
    gate = dot_nn(normed_three, w_gate)
    up = dot_nn(normed_three, w_up)
    tanh_part = jnp.tanh(GELU_CURVE * (gate + 0.044715 * gate * gate * gate))
    gelu = 0.5 * gate * (1.0 + tanh_part)
    gelu_slope = 0.5 * (1.0 + tanh_part) + 0.5 * gate * (1.0 - tanh_part * tanh_part) * (
        GELU_CURVE * (1.0 + 3.0 * 0.044715 * gate * gate)
    )
    hidden_value = gelu * up
    hidden_low = hidden_value.astype(BF16)
    mlp_branch = dot_nn(hidden_low, w_down)
    layer_rows = after_cross + mlp_branch
    layer_out = to_positions(layer_rows.astype(BF16).reshape(own, text, width)).astype(F32)

    grad_y = cot.reshape(-1, width).astype(F32) * text_valid
    grad_mlp = grad_y.astype(BF16)
    grad_w_down = dot_tn(hidden_low, grad_mlp).astype(BF16)
    grad_hidden = dot_nt(grad_mlp, w_down)
    grad_gate = (grad_hidden * up * gelu_slope).astype(BF16)
    grad_up = (grad_hidden * gelu).astype(BF16)
    grad_w_gate = dot_tn(normed_three, grad_gate).astype(BF16)
    grad_w_up = dot_tn(normed_three, grad_up).astype(BF16)
    grad_three = dot_nt(grad_gate, w_gate) + dot_nt(grad_up, w_up)
    norm_grad, grad_g_mlp = norm_backward(after_cross, g_mlp, grad_three)
    grad_after_cross = grad_y + norm_grad

    grad_cbranch = grad_after_cross.astype(BF16)
    grad_c_out = dot_tn(cross_mix, grad_cbranch).astype(BF16)
    grad_cmix = dot_nt(grad_cbranch, c_out).astype(BF16)
    grad_cq, grad_ck, grad_cv = attend(
        cross_backward_kernel,
        counts,
        (cross_q, cross_k, cross_v, grad_cmix),
        cross_norms,
        own,
        cross_flops * 5 // 2,
    )
    grad_patch_rows = dot_nt(grad_ck, c_key) + dot_nt(grad_cv, c_value)
    grad_patches = to_positions(
        grad_patch_rows.astype(BF16).reshape(own, slots, width)
    ).astype(F32)
    grad_c_query = dot_tn(normed_two, grad_cq).astype(BF16)
    grad_c_key = dot_tn(patch, grad_ck).astype(BF16)
    grad_c_value = dot_tn(patch, grad_cv).astype(BF16)
    grad_two = dot_nt(grad_cq, c_query)
    norm_grad, grad_g_cross = norm_backward(after_self, g_cross, grad_two)
    grad_after_self = grad_after_cross + norm_grad

    grad_sbranch = grad_after_self.astype(BF16)
    grad_w_out = dot_tn(self_mix, grad_sbranch).astype(BF16)
    grad_smix = dot_nt(grad_sbranch, w_out).astype(BF16)
    grad_sq, grad_sk, grad_sv = attend(
        self_backward_kernel,
        lengths,
        (self_q, self_k, self_v, grad_smix),
        self_norms,
        own,
        self_flops * 5 // 2,
    )
    grad_w_query = dot_tn(normed_one, grad_sq).astype(BF16)
    grad_w_key = dot_tn(normed_one, grad_sk).astype(BF16)
    grad_w_value = dot_tn(normed_one, grad_sv).astype(BF16)
    grad_one = dot_nt(grad_sq, w_query) + dot_nt(grad_sk, w_key) + dot_nt(grad_sv, w_value)
    norm_grad, grad_g_self = norm_backward(x, g_self, grad_one)
    grad_x_rows = grad_after_self + norm_grad
    grad_x = to_positions(grad_x_rows.astype(BF16).reshape(own, text, width)).astype(F32)

    stats = jnp.stack(
        [
            jnp.sum(text_valid * layer_rows * layer_rows),
            jnp.sum(text_valid * self_branch * self_branch),
            jnp.sum(text_valid * cross_branch * cross_branch),
            jnp.sum(text_valid * mlp_branch * mlp_branch),
            jnp.sum(text_valid * hidden_value * hidden_value),
            jnp.sum(text_valid * grad_x_rows * grad_x_rows),
            jnp.sum(patch_valid * grad_patch_rows * grad_patch_rows),
            jnp.sum(text_valid),
            jnp.sum(patch_valid),
        ]
    )
    small = jnp.concatenate([grad_g_self, grad_g_cross, grad_g_mlp, stats])
    padded = -(-small.shape[0] // (8 * LANES)) * 8 * LANES
    small = jnp.pad(small, (0, padded - small.shape[0])).reshape(-1, LANES)
    summed, total = reduce_all(
        (
            grad_w_query,
            grad_w_key,
            grad_w_value,
            grad_w_out,
            grad_c_query,
            grad_c_key,
            grad_c_value,
            grad_c_out,
            grad_w_gate,
            grad_w_up,
            grad_w_down,
        ),
        small,
        n_dp,
        n_seq,
    )
    total = total.reshape(-1)
    part = width // n_dp
    gains = [
        lax.dynamic_slice_in_dim(total, i * width + dp_place * part, part) for i in range(3)
    ]
    stats = total[3 * width : 3 * width + 9]
    per_text = stats[7] * width
    rms_values = jnp.sqrt(
        stats[:7]
        / jnp.stack(
            [per_text, per_text, per_text, per_text, stats[7] * ff_width, per_text, stats[8] * width]
        )
    )
    return (
        layer_out,
        grad_x,
        grad_patches,
        gains[0],
        gains[1],
        gains[2],
        *summed,
        rms_values,
    )


def solution(mesh):
    rows = P("dp", "seq", None)
    tile = P("dp", "seq")
    in_specs = (rows, rows, P("dp", None), P("dp"), rows) + (P(),) * 14
    out_specs = (rows,) * 3 + (P("dp"),) * 3 + (tile,) * 11 + (P(),)
    return jax.shard_map(local, mesh=mesh, in_specs=in_specs, out_specs=out_specs, check_vma=False)
```

```python
from functools import partial

import jax
import jax.numpy as jnp
from jax import lax
from jax.experimental import pallas as pl
from jax.experimental.pallas import tpu as pltpu
from jax.sharding import PartitionSpec as P

HEAD_DIM = 64
LANES = 128
PAIR = LANES // HEAD_DIM
NORM_EPS = 1e-06
NEG_FILL = -1e30
GELU_CURVE = 0.7978845608028654
F32 = jnp.float32
BF16 = jnp.bfloat16
MESH = pl.DeviceIdType.MESH
VMEM_LIMIT = 48 * 1024 * 1024
TAIL_VMEM = 62 * 1024 * 1024


def dot_nn(a, b):
    return lax.dot_general(a, b, (((1,), (0,)), ((), ())), preferred_element_type=F32)


def dot_nt(a, b):
    return lax.dot_general(a, b, (((1,), (1,)), ((), ())), preferred_element_type=F32)


def dot_tn(a, b):
    return lax.dot_general(a, b, (((0,), (0,)), ((), ())), preferred_element_type=F32)


def head_mask(h, dtype):
    lane = lax.broadcasted_iota(jnp.int32, (1, LANES), 1)
    return ((lane // HEAD_DIM) == h).astype(F32).astype(dtype)


def causal_scores(raw, limit):
    key_pos = lax.broadcasted_iota(jnp.int32, raw.shape, 0)
    query_pos = lax.broadcasted_iota(jnp.int32, raw.shape, 1)
    return jnp.where((key_pos <= query_pos) & (key_pos < limit), raw, NEG_FILL)


def forward_pair(q, k, v, limit, causal):
    v_t = v.T
    mixes, norms = [], []
    for h in range(PAIR):
        q_h = q * (head_mask(h, BF16) * 0.125)
        scores = dot_nt(k, q_h)
        if causal:
            scores = causal_scores(scores, limit)
        elif limit is not None:
            key_pos = lax.broadcasted_iota(jnp.int32, scores.shape, 0)
            scores = jnp.where(key_pos < limit, scores, NEG_FILL)
        top = jnp.max(scores, axis=0, keepdims=True)
        exps = jnp.exp(scores - top)
        total = jnp.sum(exps, axis=0, keepdims=True)
        mixed = dot_nn(v_t[h * HEAD_DIM : (h + 1) * HEAD_DIM], exps.astype(BF16))
        mixes.append(mixed / total)
        norms.append(top + jnp.log(total))
    return jnp.concatenate(mixes, axis=0).T.astype(BF16), jnp.concatenate(norms, axis=0)


def backward_pair(q, k, v, grad_mix, norms, limit, causal):
    k_t = k.T * 0.125
    grad_q, grad_k, grad_v = [], 0.0, 0.0
    for h in range(PAIR):
        mask = head_mask(h, BF16)
        q_h = q * (mask * 0.125)
        scores = dot_nt(k, q_h)
        if causal:
            scores = causal_scores(scores, limit)
        elif limit is not None:
            key_pos = lax.broadcasted_iota(jnp.int32, scores.shape, 0)
            scores = jnp.where(key_pos < limit, scores, NEG_FILL)
        probs = jnp.exp(scores - norms[h : h + 1])
        grad_h = grad_mix * mask
        grad_v = grad_v + dot_nn(probs.astype(BF16), grad_h)
        grad_p = dot_nt(v, grad_h)
        inner = jnp.sum(probs * grad_p, axis=0, keepdims=True)
        grad_s = (probs * (grad_p - inner)).astype(BF16)
        grad_k = grad_k + dot_nn(grad_s, q_h)
        grad_q.append(dot_nn(k_t[h * HEAD_DIM : (h + 1) * HEAD_DIM], grad_s))
    grad_q = jnp.concatenate(grad_q, axis=0).T
    return grad_q.astype(BF16), grad_k.astype(BF16), grad_v.astype(BF16)


def self_forward_kernel(limit_ref, q_ref, k_ref, v_ref, mix_ref, norm_ref):
    limit = limit_ref[pl.program_id(0)]
    mix, norms = forward_pair(q_ref[...], k_ref[...], v_ref[...], limit, True)
    mix_ref[...] = mix
    norm_ref[0, 0, 0:PAIR] = norms


def self_backward_kernel(
    limit_ref, q_ref, k_ref, v_ref, grad_ref, norm_ref, dq_ref, dk_ref, dv_ref
):
    limit = limit_ref[pl.program_id(0)]
    dq, dk, dv = backward_pair(
        q_ref[...], k_ref[...], v_ref[...], grad_ref[...], norm_ref[0, 0, 0:PAIR], limit, True
    )
    dq_ref[...] = dq
    dk_ref[...] = dk
    dv_ref[...] = dv


def cross_forward_kernel(limit_ref, q_ref, k_ref, v_ref, mix_ref, norm_ref):
    limit = limit_ref[pl.program_id(0)]
    keys = k_ref.shape[0]
    short = keys // 4

    def run(count):
        mix, norms = forward_pair(q_ref[...], k_ref[0:count], v_ref[0:count], None, False)
        mix_ref[...] = mix
        norm_ref[0, 0, 0:PAIR] = norms

    pl.when(limit > short)(lambda: run(keys))
    pl.when(limit <= short)(lambda: run(short))


def cross_backward_kernel(
    limit_ref, q_ref, k_ref, v_ref, grad_ref, norm_ref, dq_ref, dk_ref, dv_ref
):
    limit = limit_ref[pl.program_id(0)]
    keys = k_ref.shape[0]
    short = keys // 4

    def run(count):
        dq, dk, dv = backward_pair(
            q_ref[...],
            k_ref[0:count],
            v_ref[0:count],
            grad_ref[...],
            norm_ref[0, 0, 0:PAIR],
            None,
            False,
        )
        dq_ref[...] = dq
        dk_ref[0:count] = dk
        dv_ref[0:count] = dv
        if count < keys:
            dk_ref[count:] = jnp.zeros((keys - count, LANES), BF16)
            dv_ref[count:] = jnp.zeros((keys - count, LANES), BF16)

    pl.when(limit > short)(lambda: run(keys))
    pl.when(limit <= short)(lambda: run(short))


def attend(kernel, limits, arrays, norms, examples, flops):
    width = arrays[0].shape[1]
    pairs = width // LANES
    queries = arrays[0].shape[0] // examples

    def rows_spec(array):
        return pl.BlockSpec((array.shape[0] // examples, LANES), lambda e, p: (e, p))

    norm_spec = pl.BlockSpec((1, 1, 8, queries), lambda e, p: (e, p, 0, 0))
    norm_shape = jax.ShapeDtypeStruct((examples, pairs, 8, queries), F32)
    in_specs = [pl.BlockSpec(memory_space=pltpu.SMEM)] + [rows_spec(a) for a in arrays]
    args = (limits,) + tuple(arrays)
    if norms is None:
        out_shape = (jax.ShapeDtypeStruct(arrays[0].shape, BF16), norm_shape)
        out_specs = (rows_spec(arrays[0]), norm_spec)
    else:
        in_specs.append(norm_spec)
        args = args + (norms,)
        out_shape = tuple(jax.ShapeDtypeStruct(a.shape, BF16) for a in arrays[:3])
        out_specs = tuple(rows_spec(a) for a in arrays[:3])
    return pl.pallas_call(
        kernel,
        grid=(examples, pairs),
        in_specs=in_specs,
        out_specs=out_specs,
        out_shape=out_shape,
        compiler_params=pltpu.CompilerParams(vmem_limit_bytes=VMEM_LIMIT),
        cost_estimate=pl.CostEstimate(
            flops=flops, bytes_accessed=sum(a.size * 2 for a in arrays), transcendentals=0
        ),
    )(*args)


HEAD_STATE = (
    "self_q self_k self_v self_mix normed_one hidden after_self grad_after_cross grad_cross_q normed_three "
    "grad_mlp mlp_hidden grad_gate grad_up self_norms patch_late layer_late dw_c_out dw_c_query dw_c_key dw_c_value"
).split()


def head_kernel(*refs):
    lengths_ref, counts_ref, g_self_ref, g_cross_ref, g_mlp_ref = refs[:5]
    hidden_in, patches_in, cot_in = refs[5:8]
    weights_in = refs[8:19]
    refs = refs[19:]
    small, patch_out, layer_out = refs[:3]
    kept = dict(zip(HEAD_STATE, refs[3 : 3 + len(HEAD_STATE)]))
    (
        hidden,
        cot,
        patch,
        normed_one,
        self_rows,
        after_self,
        normed_two,
        queries,
        keys,
        values,
        cmix,
        normed_three,
        mlp_rows,
        grad_after,
        cbranch,
        grad_mix,
        patch_send,
        layer,
        after_cross,
        mlp_sum,
        grad_three,
        squares,
        w_gate,
        w_up,
        w_down,
        self_norms,
        cross_norms,
        weight_sem,
        in_send,
        in_recv,
        in_local,
        out_send,
        out_recv,
        out_local,
        keep_sem,
    ) = refs[3 + len(HEAD_STATE) :]
    own = 2
    rows, width = hidden.shape
    text = rows // own
    slots = patch.shape[0] // own
    part, patch_part = text // 4, slots // 4
    pairs = width // LANES
    dp = lax.axis_index("dp")
    seq = lax.axis_index("seq")
    near_seq = seq + 1 - 2 * (seq % 2)
    far_seq = seq + 2 - 4 * (seq // 2)
    seq_peers = [far_seq, near_seq, 3 - seq]
    lengths = [lengths_ref[own * seq + e] for e in range(own)]
    counts = [counts_ref[own * seq + e] for e in range(own)]

    barrier = pltpu.get_barrier_semaphore()
    for z in seq_peers:
        pl.semaphore_signal(barrier, inc=1, device_id=(dp, z), device_id_type=MESH)
    pl.semaphore_wait(barrier, len(seq_peers))

    incoming = {}

    def receive(name, number, src, dst, size, e):
        first = pl.multiple_of(e * 4 * size + seq * size, size)
        copies = []
        for k, z in enumerate(seq_peers):
            copy = pltpu.make_async_remote_copy(
                src_ref=src.at[own * z + e],
                dst_ref=dst.at[pl.ds(first, size)],
                send_sem=in_send.at[number, k],
                recv_sem=in_recv.at[number, k],
                device_id=(dp, z),
                device_id_type=MESH,
            )
            copy.start()
            copies.append(copy)
        local_copy = pltpu.make_async_copy(
            src.at[own * seq + e], dst.at[pl.ds(first, size)], in_local.at[number]
        )
        local_copy.start()
        incoming[name] = (copies, local_copy)

    def arrived(name):
        copies, local_copy = incoming[name]
        local_copy.wait()
        for copy in copies:
            copy.wait_recv()

    receive("x0", 0, hidden_in, hidden, part, 0)
    receive("x1", 1, hidden_in, hidden, part, 1)

    loads = []
    targets = [squares.at[i] for i in range(8)] + [w_gate, w_up, w_down]
    for i, (src, dst) in enumerate(zip(weights_in, targets)):
        copy = pltpu.make_async_copy(src, dst, weight_sem.at[i])
        copy.start()
        loads.append(copy)
    WQ, WK, WV, WO, CQ, CK, CV, CO = range(8)

    keeping = []

    def keep(name, src):
        copy = pltpu.make_async_copy(src, kept[name], keep_sem.at[len(keeping)])
        copy.start()
        keeping.append(copy)

    small[...] = jnp.zeros(small.shape, F32)
    lane = lax.broadcasted_iota(jnp.int32, (1, width), 1)
    small[10:11] = jnp.where(
        lane == 0, lengths[0] + lengths[1], jnp.where(lane == 1, counts[0] + counts[1], 0)
    ).astype(F32)

    def add_row(i, value):
        small[i : i + 1, 0 : value.shape[1]] += value

    def valid_rows(e):
        position = lax.broadcasted_iota(jnp.int32, (text, 1), 0)
        return (position < lengths[e]).astype(F32)

    def squared(valid, value):
        return jnp.sum(valid * value * value, axis=0, keepdims=True)

    def norm(u, gain):
        r = lax.rsqrt(jnp.mean(u * u, axis=-1, keepdims=True) + NORM_EPS)
        return (u * r * gain).astype(BF16)

    for e in range(own):
        at = slice(e * text, (e + 1) * text)
        arrived("x%d" % e)
        if e == 0:
            for i in (WQ, WK, WV):
                loads[i].wait()
        else:
            receive("p0", 2, patches_in, patch, patch_part, 0)
        normed_one[at] = norm(hidden[at].astype(F32), g_self_ref[...])
        for i in (WQ, WK, WV):
            self_rows[i, at] = dot_nn(normed_one[at], squares[i]).astype(BF16)

    def self_pair(step, carry):
        e, p = step // pairs, step % pairs
        at = pl.ds(pl.multiple_of(e * text, text), text)
        lanes = pl.ds(pl.multiple_of(p * LANES, LANES), LANES)
        limit = lengths_ref[own * seq + e]
        mix, norms = forward_pair(
            self_rows[0, at, lanes], self_rows[1, at, lanes], self_rows[2, at, lanes], limit, True
        )
        self_rows[3, at, lanes] = mix
        self_norms[e, p, 0:PAIR] = norms
        return carry

    lax.fori_loop(0, own * pairs, self_pair, 0)
    receive("c0", 4, cot_in, cot, part, 0)
    receive("c1", 5, cot_in, cot, part, 1)
    loads[WO].wait()
    loads[CQ].wait()
    for e in range(own):
        at = slice(e * text, (e + 1) * text)
        branch = dot_nn(self_rows[3, at], squares[WO])
        add_row(4, squared(valid_rows(e), branch))
        after = hidden[at].astype(F32) + branch
        after_self[at] = after
        normed_two[at] = norm(after, g_cross_ref[...])
        queries[at] = dot_nn(normed_two[at], squares[CQ]).astype(BF16)
    for i, name in enumerate(("self_q", "self_k", "self_v", "self_mix")):
        keep(name, self_rows.at[i])
    keep("normed_one", normed_one)
    keep("hidden", hidden)
    keep("after_self", after_self)
    keep("self_norms", self_norms)

    def project_patches(e):
        def body(i, carry):
            at = pl.ds(pl.multiple_of(e * slots + i * patch_part, patch_part), patch_part)
            keys[at] = dot_nn(patch[at], squares[CK]).astype(BF16)
            values[at] = dot_nn(patch[at], squares[CV]).astype(BF16)
            return carry

        lax.fori_loop(0, 4, body, 0)

    def cross_forward(e):
        at, key_at = slice(e * text, (e + 1) * text), slice(e * slots, (e + 1) * slots)

        def body(p, carry):
            lanes = pl.ds(pl.multiple_of(p * LANES, LANES), LANES)
            mix, norms = forward_pair(
                queries[at, lanes], keys[key_at, lanes], values[key_at, lanes], counts[e], False
            )
            cmix[at, lanes] = mix
            cross_norms[e, p, 0:PAIR] = norms
            return carry

        lax.fori_loop(0, pairs, body, 0)

    def feed_forward(e):
        at = slice(e * text, (e + 1) * text)
        valid = valid_rows(e)
        branch = dot_nn(cmix[at], squares[CO])
        add_row(5, squared(valid, branch))
        after = after_self[at] + branch
        after_cross[...] = after
        normed_three[at] = norm(after, g_mlp_ref[...])
        arrived("c%d" % e)
        cot[at] = (cot[at].astype(F32) * valid).astype(BF16)
        mlp_sum[...] = jnp.zeros((text, width), F32)
        grad_three[...] = jnp.zeros((text, width), F32)
        step = w_gate.shape[1] // 4

        def body(i, total):
            columns = pl.ds(pl.multiple_of(i * step, step), step)
            gate = dot_nn(normed_three[at], w_gate[:, columns])
            up = dot_nn(normed_three[at], w_up[:, columns])
            tanh_part = jnp.tanh(GELU_CURVE * (gate + 0.044715 * gate * gate * gate))
            gelu = 0.5 * gate * (1.0 + tanh_part)
            slope = 0.5 * (1.0 + tanh_part) + 0.5 * gate * (1.0 - tanh_part * tanh_part) * (
                GELU_CURVE * (1.0 + 3.0 * 0.044715 * gate * gate)
            )
            value = gelu * up
            low_value = value.astype(BF16)
            mlp_rows[0, at, columns] = low_value
            mlp_sum[...] += dot_nn(low_value, w_down[columns, :])
            grad_value = dot_nt(cot[at], w_down[columns, :])
            grad_gate = (grad_value * up * slope).astype(BF16)
            grad_up = (grad_value * gelu).astype(BF16)
            mlp_rows[1, at, columns] = grad_gate
            mlp_rows[2, at, columns] = grad_up
            grad_three[...] += dot_nt(grad_gate, w_gate[:, columns]) + dot_nt(
                grad_up, w_up[:, columns]
            )
            return total + squared(valid, value)

        add_row(7, lax.fori_loop(0, 4, body, jnp.zeros((1, step), F32)))
        mlp_branch = mlp_sum[...]
        add_row(6, squared(valid, mlp_branch))
        after = after_cross[...]
        out = after + mlp_branch
        add_row(3, squared(valid, out))
        layer[at] = out.astype(BF16)
        w = grad_three[...]
        r = lax.rsqrt(jnp.mean(after * after, axis=-1, keepdims=True) + NORM_EPS)
        gw = g_mlp_ref[...] * w
        add_row(2, jnp.sum(w * after * r, axis=0, keepdims=True))
        grad = r * gw - after * (r * r * r) * jnp.mean(gw * after, axis=-1, keepdims=True)
        grad = cot[at].astype(F32) + grad
        grad_after[at] = grad
        cbranch[at] = grad.astype(BF16)
        grad_mix[at] = dot_nt(cbranch[at], squares[CO]).astype(BF16)

    def cross_backward(e):
        at, key_at = slice(e * text, (e + 1) * text), slice(e * slots, (e + 1) * slots)

        def body(p, carry):
            lanes = pl.ds(pl.multiple_of(p * LANES, LANES), LANES)
            dq, dk, dv = backward_pair(
                queries[at, lanes],
                keys[key_at, lanes],
                values[key_at, lanes],
                grad_mix[at, lanes],
                cross_norms[e, p, 0:PAIR],
                counts[e],
                False,
            )
            queries[at, lanes] = dq
            keys[key_at, lanes] = dk
            values[key_at, lanes] = dv
            return carry

        lax.fori_loop(0, pairs, body, 0)

    def patch_grads(e):
        def body(d, total):
            first = pl.multiple_of(d * patch_part, patch_part)
            at = pl.ds(e * slots + first, patch_part)
            value = dot_nt(keys[at], squares[CK]) + dot_nt(values[at], squares[CV])
            position = lax.broadcasted_iota(jnp.int32, (patch_part, 1), 0) + first
            patch_send[e, d] = value.astype(BF16)
            return total + squared((position < counts[e]).astype(F32), value)

        add_row(9, lax.fori_loop(0, 4, body, jnp.zeros((1, width), F32)))

    outgoing = []

    def send_rows(src_of, dst, number):
        for k, z in enumerate(seq_peers):
            copy = pltpu.make_async_remote_copy(
                src_ref=src_of(z),
                dst_ref=dst.at[seq],
                send_sem=out_send.at[number, k],
                recv_sem=out_recv.at[number, k],
                device_id=(dp, z),
                device_id_type=MESH,
            )
            copy.start()
            outgoing.append(copy)
        local_copy = pltpu.make_async_copy(src_of(seq), dst.at[seq], out_local.at[number])
        local_copy.start()
        keeping.append(local_copy)

    arrived("p0")
    receive("p1", 3, patches_in, patch, patch_part, 1)
    for copy in loads[CK:]:
        copy.wait()
    project_patches(0)
    cross_forward(0)
    feed_forward(0)
    send_rows(lambda z: layer.at[pl.ds(pl.multiple_of(z * part, part), part)], layer_out, 0)
    cross_backward(0)
    patch_grads(0)
    send_rows(lambda z: patch_send.at[0, z], patch_out, 1)
    arrived("p1")
    project_patches(1)
    cross_forward(1)
    feed_forward(1)
    keep("layer_late", layer.at[text : 2 * text])
    keep("grad_after_cross", grad_after)
    keep("normed_three", normed_three)
    keep("grad_mlp", cot)
    for i, name in enumerate(("mlp_hidden", "grad_gate", "grad_up")):
        keep(name, mlp_rows.at[i])
    cross_backward(1)
    keep("grad_cross_q", queries)
    patch_grads(1)
    keep("patch_late", patch_send.at[1])

    for i, (name, left, right) in enumerate(
        (
            ("dw_c_out", cmix, cbranch),
            ("dw_c_query", normed_two, queries),
            ("dw_c_key", patch, keys),
            ("dw_c_value", patch, values),
        )
    ):
        for h in range(2):
            columns = slice(h * (width // 2), (h + 1) * (width // 2))
            squares[i, columns] = dot_tn(left[:, columns], right[...]).astype(BF16)
        keep(name, squares.at[i])
    for copies, local_copy in incoming.values():
        for copy in copies:
            copy.wait_send()
    for copy in outgoing:
        copy.wait()
    for copy in keeping:
        copy.wait()


def forward_head(lengths, counts, gains, rows, weights):
    examples, part, width = rows[0].shape
    patch_part = rows[1].shape[1]
    own = examples // 4
    text, slots = 4 * part, 4 * patch_part
    count, key_count = own * text, own * slots
    ff_width = weights[8].shape[1]
    pairs = width // LANES
    norms = (own, pairs, 8, text)
    vmem = pl.BlockSpec(memory_space=pltpu.VMEM)
    anywhere = pl.BlockSpec(memory_space=pl.ANY)
    smem = pl.BlockSpec(memory_space=pltpu.SMEM)
    low_shapes = dict(
        mlp_hidden=(count, ff_width),
        grad_gate=(count, ff_width),
        grad_up=(count, ff_width),
        patch_late=(4, patch_part, width),
        layer_late=(text, width),
        dw_c_out=(width, width),
        dw_c_query=(width, width),
        dw_c_key=(width, width),
        dw_c_value=(width, width),
    )
    wide_shapes = dict(
        after_self=(count, width), grad_after_cross=(count, width), self_norms=norms
    )
    state = []
    for name in HEAD_STATE:
        if name in wide_shapes:
            state.append(jax.ShapeDtypeStruct(wide_shapes[name], F32))
        else:
            state.append(jax.ShapeDtypeStruct(low_shapes.get(name, (count, width)), BF16))

    def low(*shape):
        return pltpu.VMEM(shape, BF16)

    def wide(*shape):
        return pltpu.VMEM(shape, F32)

    outs = pl.pallas_call(
        head_kernel,
        out_shape=(
            jax.ShapeDtypeStruct((16, width), F32),
            jax.ShapeDtypeStruct((4, patch_part, width), BF16),
            jax.ShapeDtypeStruct((4, part, width), BF16),
            *state,
        ),
        in_specs=[smem] * 2 + [vmem] * 3 + [anywhere] * 14,
        out_specs=(vmem,) + (anywhere,) * (2 + len(state)),
        scratch_shapes=[
            low(count, width),
            low(count, width),
            low(key_count, width),
            low(count, width),
            low(4, count, width),
            wide(count, width),
            low(count, width),
            low(count, width),
            low(key_count, width),
            low(key_count, width),
            low(count, width),
            low(count, width),
            low(3, count, ff_width),
            wide(count, width),
            low(count, width),
            low(count, width),
            low(own, 4, patch_part, width),
            low(count, width),
            wide(text, width),
            wide(text, width),
            wide(text, width),
            low(8, width, width),
            low(width, ff_width),
            low(width, ff_width),
            low(ff_width, width),
            wide(*norms),
            wide(*norms),
            pltpu.SemaphoreType.DMA((11,)),
            pltpu.SemaphoreType.DMA((6, 3)),
            pltpu.SemaphoreType.DMA((6, 3)),
            pltpu.SemaphoreType.DMA((6,)),
            pltpu.SemaphoreType.DMA((2, 3)),
            pltpu.SemaphoreType.DMA((2, 3)),
            pltpu.SemaphoreType.DMA((2,)),
            pltpu.SemaphoreType.DMA((len(HEAD_STATE) + 2,)),
        ],
        compiler_params=pltpu.CompilerParams(
            collective_id=1, has_side_effects=True, vmem_limit_bytes=TAIL_VMEM
        ),
    )(lengths, counts, *[g[None] for g in gains], *rows, *weights)
    return outs[0], outs[1], outs[2], dict(zip(HEAD_STATE, outs[3:]))


TAIL_INPUTS = HEAD_STATE + ["c_query", "w_out", "w_query", "w_key", "w_value"]


def tail_kernel(lengths_ref, g_self_ref, g_cross_ref, small_in, *refs):
    hbm = dict(zip(TAIL_INPUTS, refs))
    refs = refs[len(TAIL_INPUTS) :]
    narrow, wide, small_out, patch_out, x_out, layer_out = refs[:6]
    (
        after_self,
        grad_after,
        queries,
        normed,
        mlp_rows,
        grad_mlp,
        self_rows,
        self_norms,
        weights,
        wide_units,
        tall_units,
        wide_core,
        tall_core,
        wide_two,
        tall_two,
        wide_three,
        tall_three,
        square,
        square_core,
        square_two,
        square_three,
        cut_narrow,
        near_narrow,
        far_narrow,
        cut_wide,
        near_wide,
        far_wide,
        small_own,
        small_got,
        load_sem,
        send_sem,
        recv_sem,
        small_send,
        small_recv,
        cut_send,
        cut_recv,
        out_send,
        out_recv,
        out_local,
    ) = refs[6:]
    width = queries.shape[1]
    block = width // 8
    text = self_norms.shape[3]
    own = 2
    pairs = width // LANES
    part = text // 4

    dp = lax.axis_index("dp")
    seq = lax.axis_index("seq")
    core, x, y = dp % 2, (dp // 2) % 2, dp // 4
    low, high = seq % 2, seq // 2
    to_core = (dp + 1 - 2 * core, seq)
    to_x = (dp + 2 - 4 * x, seq)
    to_y = (dp + 4 - 8 * y, seq)
    near_seq = seq + 1 - 2 * low
    far_seq = seq + 2 - 4 * high
    last_seq = 3 - seq
    seq_peers = [near_seq, far_seq, last_seq]
    to_near, to_far = (dp, near_seq), (dp, far_seq)
    peers = [to_core, to_x, to_y, to_near, to_far, (dp, last_seq)]

    loads = {}

    def load(name, src, dst):
        copy = pltpu.make_async_copy(src, dst, load_sem.at[len(loads)])
        copy.start()
        loads[name] = copy

    c_units = ("dw_c_out", "dw_c_query", "dw_c_key", "dw_c_value")
    for i, name in enumerate(c_units):
        load(name, hbm[name].at[:, :, core], square.at[i])
    load("normed", hbm["normed_three"], normed)
    load("grad_gate", hbm["grad_gate"], mlp_rows.at[1])
    load("mlp_hidden", hbm["mlp_hidden"], mlp_rows.at[0])
    load("grad_mlp", hbm["grad_mlp"], grad_mlp)
    load("grad_up", hbm["grad_up"], mlp_rows.at[2])
    load("queries", hbm["grad_cross_q"], queries)
    load("after_self", hbm["after_self"], after_self)
    load("grad_after", hbm["grad_after_cross"], grad_after)
    load("c_query", hbm["c_query"], weights.at[2])
    load("w_out", hbm["w_out"], weights.at[3])
    self_q, self_k, self_v, self_mix, hidden, sbranch, grad_smix = (
        self_rows.at[i] for i in range(7)
    )
    load("self_mix", hbm["self_mix"], self_mix)
    load("self_norms", hbm["self_norms"], self_norms)
    load("self_q", hbm["self_q"], self_q)
    load("self_k", hbm["self_k"], self_k)
    load("self_v", hbm["self_v"], self_v)
    load("hidden", hbm["hidden"], hidden)
    load("w_query", hbm["w_query"], weights.at[0])
    load("w_key", hbm["w_key"], weights.at[1])

    small_own[0] = small_in[...]

    def add_row(i, value):
        small_own[0, i : i + 1] += value

    barrier = pltpu.get_barrier_semaphore()
    for peer in peers:
        pl.semaphore_signal(barrier, inc=1, device_id=peer, device_id_type=MESH)
    pl.semaphore_wait(barrier, len(peers))

    def remote(src, dst, send, recv, device):
        copy = pltpu.make_async_remote_copy(
            src_ref=src,
            dst_ref=dst,
            send_sem=send,
            recv_sem=recv,
            device_id=device,
            device_id_type=MESH,
        )
        copy.start()
        return copy

    n_square = square_core.shape[0]
    y_first = (1, 3, 5, 7, 8, 10)
    first, second, third, near, far, small = {}, {}, {}, {}, {}, {}
    got_core = [wide_core.at[0], wide_core.at[1], tall_core]
    got_core += [square_core.at[i] for i in range(n_square)]
    got_two = [wide_two.at[0], wide_two.at[1], tall_two]
    got_two += [square_two.at[i] for i in range(n_square)]
    got_three = [wide_three.at[0], wide_three.at[1], tall_three]
    got_three += [square_three.at[i] for i in range(n_square)]
    current = [wide_units.at[0], wide_units.at[1], tall_units.at[0]]
    current += [square.at[i] for i in range(n_square)]
    for i, name in enumerate(c_units):
        u = 3 + i
        first[u] = remote(
            hbm[name].at[:, :, 1 - core],
            got_core[u],
            send_sem.at[0, u],
            recv_sem.at[0, u],
            to_core,
        )

    def add(out, got):
        rows = out.shape[0]
        step = 32

        def body(i, carry):
            at = pl.ds(pl.multiple_of(i * step, step), step)
            out[at, :] = (out[at, :].astype(F32) + got[at, :].astype(F32)).astype(BF16)
            return carry

        lax.fori_loop(0, rows // step, body, 0)

    def over_core(u):
        if 3 <= u < 3 + len(c_units):
            loads[c_units[u - 3]].wait()
        first[u].wait_recv()
        for i in range(2):
            for j in range(2):
                add(current[u].at[i, j], got_core[u].at[i, j])

    def leave_two(u):
        cur = current[u]
        src, device = (cur.at[1 - y], to_y) if u in y_first else (cur.at[:, 1 - x], to_x)
        second[u] = remote(src, got_two[u], send_sem.at[1, u], recv_sem.at[1, u], device)

    def over_two(u):
        second[u].wait_recv()
        cur = current[u]
        for i in range(2):
            add(cur.at[y, i] if u in y_first else cur.at[i, x], got_two[u].at[i])
        src, device = (cur.at[y, 1 - x], to_x) if u in y_first else (cur.at[1 - y, x], to_y)
        third[u] = remote(src, got_three[u], send_sem.at[2, u], recv_sem.at[2, u], device)

    groups = [(1, 0, block, (0, 1)), (0, n_square // 2 * block, tall_three.shape[0] // 2, (2,))]
    groups += [(0, i * block, block, (3 + 2 * i, 4 + 2 * i)) for i in range(n_square // 2)]
    cut, got_near, got_far = (cut_narrow, cut_wide), (near_narrow, near_wide), (far_narrow, far_wide)
    totals = (narrow, wide)

    def over_three(g):
        buffer, row, rows, members = groups[g]
        for u in members:
            third[u].wait_recv()
        halves = [current[u][y, x].astype(F32) + got_three[u][...].astype(F32) for u in members]
        if len(members) == 1:
            halves = [halves[0][:rows], halves[0][rows:]]
        piece = halves[0].shape[1] // 4
        at = pl.ds(row, rows)
        for z in range(4):
            columns = [h[:, z * piece : (z + 1) * piece] for h in halves]
            cut[buffer][z // 2, z % 2, at] = jnp.concatenate(columns, axis=1).astype(BF16)
        near[g] = remote(
            cut[buffer].at[:, 1 - low, at],
            got_near[buffer].at[:, at],
            cut_send.at[0, g],
            cut_recv.at[0, g],
            to_near,
        )

    def over_near(g):
        buffer, row, rows, _ = groups[g]
        near[g].wait_recv()
        at = pl.ds(row, rows)
        for i in range(2):
            add(cut[buffer].at[i, low, at], got_near[buffer].at[i, at])
        far[g] = remote(
            cut[buffer].at[1 - high, low, at],
            got_far[buffer].at[at],
            cut_send.at[1, g],
            cut_recv.at[1, g],
            to_far,
        )

    def over_far(g):
        buffer, row, rows, _ = groups[g]
        far[g].wait_recv()
        at = pl.ds(row, rows)
        totals[buffer][at] = cut[buffer][high, low, at].astype(F32) + got_far[buffer][at].astype(F32)

    def give(u, src):
        first[u] = remote(src, got_core[u], send_sem.at[0, u], recv_sem.at[0, u], to_core)

    def weight_grad(i, rows, grad_rows):
        ring = n_square + i % 3
        if i - 3 >= len(c_units):
            first[i].wait_send()
            first_sent.add(i)
        half = width // 2
        for h in range(2):
            value = dot_tn(rows[:, h * half : (h + 1) * half], grad_rows[...]).astype(BF16)
            for j in range(4):
                at = i + ((j + core) % 2) * (ring - i)
                square[at, h, j // 2] = value[j * block : (j + 1) * block]
        give(3 + i, square.at[ring])

    def wide_grad(u):
        if u == 1:
            first[0].wait_send()
            first_sent.add(0)
        half, step = width // 2, wide_units.shape[4] // 4

        def body(i, carry):
            columns = pl.ds(pl.multiple_of(i * step, step), step)
            for h in range(2):
                value = dot_tn(
                    normed[:, h * half : (h + 1) * half], mlp_rows[1 + u, :, columns]
                ).astype(BF16)
                for j in range(4):
                    at = u + ((j + core) % 2) * (2 - u)
                    wide_units[at, h, j // 2, :, columns] = value[j * block : (j + 1) * block]
            return carry

        lax.fori_loop(0, 4, body, 0)
        give(u, wide_units.at[2])

    def tall_grad():
        rows = tall_units.shape[3]

        def body(j, carry):
            columns = pl.ds(pl.multiple_of(j * rows, rows), rows)
            value = dot_tn(mlp_rows[0, :, columns], grad_mlp[...]).astype(BF16)
            tall_units[(j + core) % 2, j // 4, (j // 2) % 2] = value
            return carry

        lax.fori_loop(0, 8, body, 0)
        give(2, tall_units.at[1])

    first_sent = set()

    outs, locals_ = [], []

    def send_rows(src_of, dst, number):
        for k, z in enumerate([far_seq, near_seq, last_seq]):
            outs.append(
                remote(src_of(z), dst, out_send.at[number, k], out_recv.at[number, k], (dp, z))
            )
        copy = pltpu.make_async_copy(src_of(seq), dst, out_local.at[number])
        copy.start()
        locals_.append(copy)

    send_rows(lambda z: hbm["patch_late"].at[z], patch_out.at[seq], 0)
    send_rows(
        lambda z: hbm["layer_late"].at[pl.ds(pl.multiple_of(z * part, part), part)],
        layer_out.at[seq],
        1,
    )
    chunk = own * text // 4

    for u in (3, 4, 5, 6):
        over_core(u)
        leave_two(u)
    loads["normed"].wait()
    loads["grad_gate"].wait()
    wide_grad(0)
    over_two(3)
    over_two(4)
    loads["grad_up"].wait()
    wide_grad(1)
    over_core(0)
    over_two(5)
    over_two(6)
    leave_two(0)
    over_core(1)
    leave_two(1)
    loads["mlp_hidden"].wait()
    loads["grad_mlp"].wait()
    tall_grad()
    over_three(2)

    load("normed_one", hbm["normed_one"], normed)
    for name in ("queries", "after_self", "grad_after", "c_query", "w_out"):
        loads[name].wait()

    def norm_grad(u, gain, w):
        r = lax.rsqrt(jnp.mean(u * u, axis=-1, keepdims=True) + NORM_EPS)
        gw = gain * w
        grad = r * gw - u * (r * r * r) * jnp.mean(gw * u, axis=-1, keepdims=True)
        return grad, jnp.sum(w * u * r, axis=0, keepdims=True)

    def middle(i, total):
        at = pl.ds(pl.multiple_of(i * chunk, chunk), chunk)
        w = dot_nt(queries[at, :], weights[2])
        grad, row = norm_grad(after_self[at, :], g_cross_ref[...], w)
        grad = grad_after[at, :] + grad
        grad_after[at, :] = grad
        low_grad = grad.astype(BF16)
        sbranch[at, :] = low_grad
        grad_smix[at, :] = dot_nt(low_grad, weights[3]).astype(BF16)
        return total + row

    add_row(1, lax.fori_loop(0, 4, middle, jnp.zeros((1, width), F32)))
    load("w_value", hbm["w_value"], weights.at[2])
    for name in ("self_q", "self_k", "self_v", "self_norms", "self_mix"):
        loads[name].wait()
    weight_grad(4, self_mix, sbranch)
    over_three(3)
    over_near(2)
    over_core(2)

    def self_pairs(first_step, last_step):
        def body(i, carry):
            e, p = i // pairs, i % pairs
            rows = pl.ds(pl.multiple_of(e * text, text), text)
            lanes = pl.ds(pl.multiple_of(p * LANES, LANES), LANES)
            dq, dk, dv = backward_pair(
                self_q[rows, lanes],
                self_k[rows, lanes],
                self_v[rows, lanes],
                grad_smix[rows, lanes],
                self_norms[e, p, 0:PAIR],
                lengths_ref[own * seq + e],
                True,
            )
            self_q[rows, lanes] = dq
            self_k[rows, lanes] = dk
            self_v[rows, lanes] = dv
            return carry

        lax.fori_loop(first_step, last_step, body, 0)

    self_pairs(0, pairs)
    leave_two(2)
    over_core(7)
    over_far(2)
    over_near(3)
    self_pairs(pairs, 2 * pairs)
    over_two(1)
    leave_two(7)
    over_two(0)
    for name in ("w_query", "w_key", "w_value", "hidden", "normed_one"):
        loads[name].wait()

    def last(i, carry):
        total, squares = carry
        at = pl.ds(pl.multiple_of(i * chunk, chunk), chunk)
        w = (
            dot_nt(self_q[at, :], weights[0])
            + dot_nt(self_k[at, :], weights[1])
            + dot_nt(self_v[at, :], weights[2])
        )
        grad, row = norm_grad(hidden[at, :].astype(F32), g_self_ref[...], w)
        grad = grad_after[at, :] + grad
        e, half = i // 2, i % 2
        position = lax.broadcasted_iota(jnp.int32, (chunk, 1), 0) + half * chunk
        valid = (position < lengths_ref[own * seq + e]).astype(F32)
        low_grad = grad.astype(BF16)
        for k in range(2):
            place = (2 * half + k) * own + e
            grad_mlp[pl.ds(pl.multiple_of(place * part, part), part)] = low_grad[
                k * part : (k + 1) * part
            ]
        return total + row, squares + jnp.sum(valid * grad * grad, axis=0, keepdims=True)

    zero = jnp.zeros((1, width), F32)
    total, squares = lax.fori_loop(0, 4, last, (zero, zero))
    add_row(0, total)
    add_row(8, squares)
    leaving = own * part
    send_rows(
        lambda z: grad_mlp.at[pl.ds(pl.multiple_of(z * leaving, leaving), leaving)], x_out.at[seq], 2
    )

    def send_small(i):
        small[i] = remote(
            small_own.at[i], small_got.at[i], small_send.at[i], small_recv.at[i], peers[i]
        )

    def add_small(i):
        small[i].wait_recv()
        small_own[i + 1] = small_own[i] + small_got[i]

    send_small(0)
    weight_grad(5, normed, self_q)
    weight_grad(6, normed, self_k)
    over_far(3)
    over_core(8)
    leave_two(8)
    weight_grad(7, normed, self_v)
    over_core(9)
    leave_two(9)
    over_core(10)
    leave_two(10)
    add_small(0)
    send_small(1)
    over_three(0)
    over_two(7)
    add_small(1)
    send_small(2)
    over_two(2)
    over_near(0)
    over_two(8)
    add_small(2)
    send_small(3)
    over_two(9)
    over_three(1)
    over_two(10)
    over_far(0)
    over_three(4)
    over_near(1)
    add_small(3)
    send_small(4)
    over_three(5)
    over_near(4)
    over_far(1)
    over_near(5)
    add_small(4)
    small_out[...] = small_own[5]
    over_far(4)
    over_far(5)
    for copy in outs:
        copy.wait_recv()
    for copy in locals_:
        copy.wait()
    for u, copy in first.items():
        if u not in first_sent:
            copy.wait_send()
    for copies in (second, third, near, far, small):
        for copy in copies.values():
            copy.wait_send()
    for copy in outs:
        copy.wait_send()


def split_kernel(groups, narrow_ref, wide_ref, *out_refs):
    for buffer, row, rows, members in groups:
        total = (narrow_ref, wide_ref)[buffer][row : row + rows]
        part = total.shape[1] // 2
        if len(members) == 2:
            out_refs[members[0]][...] = total[:, :part]
            out_refs[members[1]][...] = total[:, part:]
        else:
            out_refs[members[0]][0:rows] = total[:, :part]
            out_refs[members[0]][rows:] = total[:, part:]


def takes_kernel(width, n_dp, n_seq, own):
    return (
        n_dp == 8
        and n_seq == 4
        and own == 2
        and width // n_dp % 32 == 0
        and width % (2 * LANES) == 0
    )


def backward_tail(lengths, g_self, g_cross, small, arrays):
    n_square, n_late = 8, 4
    own, pairs, _, text = arrays["self_norms"].shape
    count, width = arrays["self_q"].shape
    ff_width = arrays["mlp_hidden"].shape[1]
    block, tall = width // 8, ff_width // 8
    tops = ((n_square // 2 * block + tall // 2, width // 2), (block, ff_width // 2))
    arrays = dict(arrays)
    for name in ("dw_c_out", "dw_c_query", "dw_c_key", "dw_c_value"):
        arrays[name] = arrays[name].reshape(2, 2, 2, block, width)
    vmem = pl.BlockSpec(memory_space=pltpu.VMEM)
    anywhere = pl.BlockSpec(memory_space=pl.ANY)
    smem = pl.BlockSpec(memory_space=pltpu.SMEM)

    def low(*shape):
        return pltpu.VMEM(shape, BF16)

    def wide(*shape):
        return pltpu.VMEM(shape, F32)

    units = n_square + 3
    n_groups = n_square // 2 + 2
    narrow, wide_total, total, patch_rows, x_rows, layer_rows = pl.pallas_call(
        tail_kernel,
        out_shape=tuple(jax.ShapeDtypeStruct(t, F32) for t in tops + (small.shape,))
        + (
            jax.ShapeDtypeStruct(arrays["patch_late"].shape, BF16),
            jax.ShapeDtypeStruct((4, count // 4, width), BF16),
            jax.ShapeDtypeStruct((4, text // 4, width), BF16),
        ),
        in_specs=[smem] + [vmem] * 3 + [anywhere] * len(TAIL_INPUTS),
        out_specs=(vmem,) * 3 + (anywhere,) * 3,
        scratch_shapes=[
            wide(count, width),
            wide(count, width),
            low(count, width),
            low(count, width),
            low(3, count, ff_width),
            low(count, width),
            low(7, count, width),
            wide(*arrays["self_norms"].shape),
            low(4, width, width),
            low(3, 2, 2, block, ff_width),
            low(2, 2, 2, tall, width),
            low(2, 2, 2, block, ff_width),
            low(2, 2, tall, width),
            low(2, 2, block, ff_width),
            low(2, tall, width),
            low(2, block, ff_width),
            low(tall, width),
            low(n_square + 3, 2, 2, block, width),
            low(n_square, 2, 2, block, width),
            low(n_square, 2, block, width),
            low(n_square, block, width),
            low(2, 2, *tops[0]),
            low(2, *tops[0]),
            low(*tops[0]),
            low(2, 2, *tops[1]),
            low(2, *tops[1]),
            low(*tops[1]),
            wide(6, *small.shape),
            wide(5, *small.shape),
            pltpu.SemaphoreType.DMA((24,)),
            pltpu.SemaphoreType.DMA((3, units)),
            pltpu.SemaphoreType.DMA((3, units)),
            pltpu.SemaphoreType.DMA((5,)),
            pltpu.SemaphoreType.DMA((5,)),
            pltpu.SemaphoreType.DMA((2, n_groups)),
            pltpu.SemaphoreType.DMA((2, n_groups)),
            pltpu.SemaphoreType.DMA((3, 3)),
            pltpu.SemaphoreType.DMA((3, 3)),
            pltpu.SemaphoreType.DMA((3,)),
        ],
        compiler_params=pltpu.CompilerParams(
            collective_id=0, has_side_effects=True, vmem_limit_bytes=TAIL_VMEM
        ),
    )(lengths, g_self[None], g_cross[None], small, *[arrays[n] for n in TAIL_INPUTS])
    groups = [(1, 0, block, (0, 1)), (0, n_square // 2 * block, tall // 2, (2,))]
    groups += [(0, i * block, block, (3 + 2 * i, 4 + 2 * i)) for i in range(n_square // 2)]
    shapes = [(block, ff_width // 4)] * 2 + [(tall, width // 4)] + [(block, width // 4)] * n_square
    results = pl.pallas_call(
        partial(split_kernel, groups),
        out_shape=tuple(jax.ShapeDtypeStruct(s, F32) for s in shapes),
        in_specs=[vmem] * 2,
        out_specs=(vmem,) * len(shapes),
        compiler_params=pltpu.CompilerParams(vmem_limit_bytes=VMEM_LIMIT),
    )(narrow, wide_total)
    return results, total, patch_rows, x_rows, layer_rows


def norm_forward(u, gain):
    r = lax.rsqrt(jnp.mean(u * u, axis=-1, keepdims=True) + NORM_EPS)
    return (u * r * gain).astype(BF16)


def norm_backward(u, gain, w):
    r = lax.rsqrt(jnp.mean(u * u, axis=-1, keepdims=True) + NORM_EPS)
    gw = gain * w
    grad = r * gw - u * (r * r * r) * jnp.mean(gw * u, axis=-1, keepdims=True)
    return grad, jnp.sum(w * u * r, axis=0, keepdims=True)


def to_examples(rows):
    n = lax.axis_size("seq")
    examples, part, width = rows.shape
    parts = lax.all_to_all(rows.reshape(n, examples // n, part, width), "seq", 0, 0)
    return parts.transpose(1, 0, 2, 3).reshape(examples // n, n * part, width)


def to_positions(rows):
    n = lax.axis_size("seq")
    own, positions, width = rows.shape
    parts = rows.reshape(own, n, positions // n, width).transpose(1, 0, 2, 3)
    return lax.all_to_all(parts, "seq", 0, 0).reshape(n * own, positions // n, width)


def halve_over_dp(matrix, bits):
    n = lax.axis_size("dp")
    count = n.bit_length() - 1
    rows, width = matrix.shape[0] // n, matrix.shape[1]
    place = lax.axis_index("dp")
    left = list(range(count))[::-1]
    current = matrix.reshape((2,) * count + (rows, width))
    for bit in bits:
        axis = left.index(bit)
        mine = (place >> bit) & 1
        keep = lax.dynamic_index_in_dim(current, mine, axis, keepdims=False)
        give = lax.dynamic_index_in_dim(current, 1 - mine, axis, keepdims=False)
        got = lax.ppermute(give, "dp", [(i, i ^ (1 << bit)) for i in range(n)])
        current = (keep.astype(F32) + got.astype(F32)).astype(BF16)
        left.remove(bit)
    return current


def scatter_over_seq(matrix):
    n = lax.axis_size("seq")
    rows, width = matrix.shape
    parts = matrix.reshape(rows, n, width // n).transpose(1, 0, 2)
    return jnp.sum(lax.all_to_all(parts, "seq", 0, 0).astype(F32), axis=0)


def reduce_grad(matrix, order):
    n = lax.axis_size("dp")
    bits = list(range(n.bit_length() - 1))
    if order:
        bits = bits[:1] + bits[1:][::-1]
    return scatter_over_seq(halve_over_dp(matrix, bits))


def local(
    hidden_in,
    patches,
    text_lengths,
    patch_counts,
    cotangent,
    g_self,
    g_cross,
    g_mlp,
    w_query,
    w_key,
    w_value,
    w_out,
    c_query,
    c_key,
    c_value,
    c_out,
    w_gate,
    w_up,
    w_down,
):
    n_seq = lax.axis_size("seq")
    n_dp = lax.axis_size("dp")
    seq_place = lax.axis_index("seq")
    dp_place = lax.axis_index("dp")
    width = hidden_in.shape[2]
    ff_width = w_gate.shape[1]
    own = hidden_in.shape[0] // n_seq
    if takes_kernel(width, n_dp, n_seq, own):
        small, patch_early, layer_early, state = forward_head(
            text_lengths[0],
            patch_counts,
            (g_self, g_cross, g_mlp),
            (hidden_in, patches, cotangent),
            (
                w_query,
                w_key,
                w_value,
                w_out,
                c_query,
                c_key,
                c_value,
                c_out,
                w_gate,
                w_up,
                w_down,
            ),
        )
        state.update(
            c_query=c_query, w_out=w_out, w_query=w_query, w_key=w_key, w_value=w_value
        )
        grads, total, patch_late, x_out, layer_late = backward_tail(
            text_lengths[0], g_self, g_cross, small, state
        )
        gate, up, down, c_o, c_q, c_k, c_v, w_o, w_q, w_k, w_v = grads
        summed = (w_q, w_k, w_v, w_o, c_q, c_k, c_v, c_o, gate, up, down)

        def both(early, late, like):
            return jnp.stack([early, late], axis=1).reshape(like.shape)

        layer_out = both(layer_early, layer_late, hidden_in)
        patch_out = both(patch_early, patch_late, patches)
        x_out = x_out.reshape(hidden_in.shape)
    else:
        lengths = lax.dynamic_slice_in_dim(text_lengths[0], seq_place * own, own)
        counts = lax.dynamic_slice_in_dim(patch_counts, seq_place * own, own)

        hidden = to_examples(hidden_in)
        patch = to_examples(patches)
        text = hidden.shape[1]
        slots = patch.shape[1]
        text_valid = (jnp.arange(text)[None, :] < lengths[:, None]).astype(F32).reshape(-1, 1)
        patch_valid = (jnp.arange(slots)[None, :] < counts[:, None]).astype(F32).reshape(-1, 1)
        x = hidden.reshape(-1, width).astype(F32)
        patch = patch.reshape(-1, width)
        self_flops = 4 * own * text * text * width
        cross_flops = 4 * own * text * slots * width

        normed_one = norm_forward(x, g_self)
        self_q = dot_nn(normed_one, w_query).astype(BF16)
        self_k = dot_nn(normed_one, w_key).astype(BF16)
        self_v = dot_nn(normed_one, w_value).astype(BF16)
        self_mix, self_norms = attend(
            self_forward_kernel, lengths, (self_q, self_k, self_v), None, own, self_flops
        )
        cot = to_examples(cotangent)
        self_branch = dot_nn(self_mix, w_out)
        after_self = x + self_branch
        normed_two = norm_forward(after_self, g_cross)
        cross_q = dot_nn(normed_two, c_query).astype(BF16)
        cross_k = dot_nn(patch, c_key).astype(BF16)
        cross_v = dot_nn(patch, c_value).astype(BF16)
        cross_mix, cross_norms = attend(
            cross_forward_kernel, counts, (cross_q, cross_k, cross_v), None, own, cross_flops
        )
        cross_branch = dot_nn(cross_mix, c_out)
        after_cross = after_self + cross_branch
        normed_three = norm_forward(after_cross, g_mlp)
        gate = dot_nn(normed_three, w_gate)
        up = dot_nn(normed_three, w_up)
        tanh_part = jnp.tanh(GELU_CURVE * (gate + 0.044715 * gate * gate * gate))
        gelu = 0.5 * gate * (1.0 + tanh_part)
        gelu_slope = 0.5 * (1.0 + tanh_part) + 0.5 * gate * (1.0 - tanh_part * tanh_part) * (
            GELU_CURVE * (1.0 + 3.0 * 0.044715 * gate * gate)
        )
        hidden_value = gelu * up
        hidden_low = hidden_value.astype(BF16)
        mlp_branch = dot_nn(hidden_low, w_down)
        layer_rows = after_cross + mlp_branch

        grad_y = cot.reshape(-1, width).astype(F32) * text_valid
        grad_mlp = grad_y.astype(BF16)
        grad_hidden = dot_nt(grad_mlp, w_down)
        grad_gate = (grad_hidden * up * gelu_slope).astype(BF16)
        grad_up = (grad_hidden * gelu).astype(BF16)
        grad_mlp_rows = (
            dot_tn(normed_three, grad_gate).astype(BF16),
            dot_tn(normed_three, grad_up).astype(BF16),
            dot_tn(hidden_low, grad_mlp).astype(BF16),
        )
        grad_three = dot_nt(grad_gate, w_gate) + dot_nt(grad_up, w_up)
        norm_grad, grad_g_mlp = norm_backward(after_cross, g_mlp, grad_three)
        grad_after_cross = grad_y + norm_grad
        grad_cbranch = grad_after_cross.astype(BF16)
        grad_cmix = dot_nt(grad_cbranch, c_out).astype(BF16)

        def square_row(valid, value):
            return jnp.sum(valid * value * value, axis=0, keepdims=True)

        lane = jnp.arange(LANES)
        valid_row = jnp.where(
            lane == 0, jnp.sum(lengths), jnp.where(lane == 1, jnp.sum(counts), 0)
        ).astype(F32)
        layer_low = layer_rows.astype(BF16)
        grad_cq, grad_ck, grad_cv = attend(
            cross_backward_kernel,
            counts,
            (cross_q, cross_k, cross_v, grad_cmix),
            cross_norms,
            own,
            cross_flops * 5 // 2,
        )
        grad_patch_rows = dot_nt(grad_ck, c_key) + dot_nt(grad_cv, c_value)
        grad_two = dot_nt(grad_cq, c_query)
        norm_grad, grad_g_cross = norm_backward(after_self, g_cross, grad_two)
        grad_after_self = grad_after_cross + norm_grad
        grad_sbranch = grad_after_self.astype(BF16)
        grad_smix = dot_nt(grad_sbranch, w_out).astype(BF16)
        grad_sq, grad_sk, grad_sv = attend(
            self_backward_kernel,
            lengths,
            (self_q, self_k, self_v, grad_smix),
            self_norms,
            own,
            self_flops * 5 // 2,
        )
        grad_one = dot_nt(grad_sq, w_query) + dot_nt(grad_sk, w_key) + dot_nt(grad_sv, w_value)
        norm_grad, grad_g_self = norm_backward(x, g_self, grad_one)
        grad_x_rows = grad_after_self + norm_grad
        layer_out = to_positions(layer_low.reshape(own, text, width))
        patch_out = to_positions(grad_patch_rows.astype(BF16).reshape(own, slots, width))
        x_out = to_positions(grad_x_rows.astype(BF16).reshape(own, text, width))
        grads = [
            dot_tn(rows, grad_rows).astype(BF16)
            for rows, grad_rows in (
                (normed_one, grad_sq),
                (normed_one, grad_sk),
                (normed_one, grad_sv),
                (self_mix, grad_sbranch),
                (normed_two, grad_cq),
                (patch, grad_ck),
                (patch, grad_cv),
                (cross_mix, grad_cbranch),
            )
        ]
        grads += grad_mlp_rows
        summed = tuple(reduce_grad(g, u % 2) for u, g in enumerate(grads))
        vectors = [
            grad_g_self,
            grad_g_cross,
            grad_g_mlp,
            square_row(text_valid, layer_rows),
            square_row(text_valid, self_branch),
            square_row(text_valid, cross_branch),
            square_row(text_valid, mlp_branch),
            square_row(text_valid, hidden_value),
            square_row(text_valid, grad_x_rows),
            square_row(patch_valid, grad_patch_rows),
            valid_row[None],
        ]
        folded = [
            sum(
                jnp.pad(p, ((0, 0), (0, width - p.shape[1])))
                for p in jnp.split(v, list(range(width, v.shape[1], width)), axis=1)
            )
            for v in vectors
        ]
        total = lax.psum(jnp.concatenate(folded), ("dp", "seq"))
    part = width // n_dp
    gains = [lax.dynamic_slice(total, (i, dp_place * part), (1, part))[0] for i in range(3)]
    squares = jnp.sum(total[3:10], axis=1)
    place = jnp.arange(7)
    texts, patch_count = total[10, 0], total[10, 1]
    per_value = jnp.where(
        place == 6, patch_count * width, jnp.where(place == 4, texts * ff_width, texts * width)
    )
    rms_values = jnp.sqrt(squares / per_value)
    return (
        layer_out.astype(F32),
        x_out.astype(F32),
        patch_out.astype(F32),
        gains[0],
        gains[1],
        gains[2],
        *summed,
        rms_values,
    )


def solution(mesh):
    rows = P("dp", "seq", None)
    tile = P("dp", "seq")
    in_specs = (rows, rows, P("dp", None), P("dp"), rows) + (P(),) * 14
    out_specs = (rows,) * 3 + (P("dp"),) * 3 + (tile,) * 11 + (P(),)
    return jax.shard_map(local, mesh=mesh, in_specs=in_specs, out_specs=out_specs, check_vma=False)
```

```python
from functools import partial

import jax
import jax.numpy as jnp
from jax import lax
from jax.experimental import pallas as pl
from jax.experimental.pallas import tpu as pltpu
from jax.sharding import PartitionSpec as P

HEAD_DIM = 64
LANES = 128
PAIR = LANES // HEAD_DIM
NORM_EPS = 1e-06
NEG_FILL = -1e30
GELU_CURVE = 0.7978845608028654
F32 = jnp.float32
BF16 = jnp.bfloat16
MESH = pl.DeviceIdType.MESH
VMEM_LIMIT = 48 * 1024 * 1024
TAIL_VMEM = 63 * 1024 * 1024


def dot_nn(a, b):
    return lax.dot_general(a, b, (((1,), (0,)), ((), ())), preferred_element_type=F32)


def dot_nt(a, b):
    return lax.dot_general(a, b, (((1,), (1,)), ((), ())), preferred_element_type=F32)


def dot_tn(a, b):
    return lax.dot_general(a, b, (((0,), (0,)), ((), ())), preferred_element_type=F32)


def head_mask(h, dtype):
    lane = lax.broadcasted_iota(jnp.int32, (1, LANES), 1)
    return ((lane // HEAD_DIM) == h).astype(F32).astype(dtype)


def causal_scores(raw, limit):
    key_pos = lax.broadcasted_iota(jnp.int32, raw.shape, 0)
    query_pos = lax.broadcasted_iota(jnp.int32, raw.shape, 1)
    return jnp.where((key_pos <= query_pos) & (key_pos < limit), raw, NEG_FILL)


def forward_pair(q, k, v, limit, causal):
    v_t = v.T
    mixes, norms = [], []
    for h in range(PAIR):
        q_h = q * (head_mask(h, BF16) * 0.125)
        scores = dot_nt(k, q_h)
        if causal:
            scores = causal_scores(scores, limit)
        elif limit is not None:
            key_pos = lax.broadcasted_iota(jnp.int32, scores.shape, 0)
            scores = jnp.where(key_pos < limit, scores, NEG_FILL)
        top = jnp.max(scores, axis=0, keepdims=True)
        exps = jnp.exp(scores - top)
        total = jnp.sum(exps, axis=0, keepdims=True)
        mixed = dot_nn(v_t[h * HEAD_DIM : (h + 1) * HEAD_DIM], exps.astype(BF16))
        mixes.append(mixed / total)
        norms.append(top + jnp.log(total))
    return jnp.concatenate(mixes, axis=0).T.astype(BF16), jnp.concatenate(norms, axis=0)


def backward_pair(q, k, v, grad_mix, norms, limit, causal):
    k_t = k.T * 0.125
    grad_q, grad_k, grad_v = [], 0.0, 0.0
    for h in range(PAIR):
        mask = head_mask(h, BF16)
        q_h = q * (mask * 0.125)
        scores = dot_nt(k, q_h)
        if causal:
            scores = causal_scores(scores, limit)
        elif limit is not None:
            key_pos = lax.broadcasted_iota(jnp.int32, scores.shape, 0)
            scores = jnp.where(key_pos < limit, scores, NEG_FILL)
        probs = jnp.exp(scores - norms[h : h + 1])
        grad_h = grad_mix * mask
        grad_v = grad_v + dot_nn(probs.astype(BF16), grad_h)
        grad_p = dot_nt(v, grad_h)
        inner = jnp.sum(probs * grad_p, axis=0, keepdims=True)
        grad_s = (probs * (grad_p - inner)).astype(BF16)
        grad_k = grad_k + dot_nn(grad_s, q_h)
        grad_q.append(dot_nn(k_t[h * HEAD_DIM : (h + 1) * HEAD_DIM], grad_s))
    grad_q = jnp.concatenate(grad_q, axis=0).T
    return grad_q.astype(BF16), grad_k.astype(BF16), grad_v.astype(BF16)


def self_forward_kernel(limit_ref, q_ref, k_ref, v_ref, mix_ref, norm_ref):
    limit = limit_ref[pl.program_id(0)]
    mix, norms = forward_pair(q_ref[...], k_ref[...], v_ref[...], limit, True)
    mix_ref[...] = mix
    norm_ref[0, 0, 0:PAIR] = norms


def self_backward_kernel(
    limit_ref, q_ref, k_ref, v_ref, grad_ref, norm_ref, dq_ref, dk_ref, dv_ref
):
    limit = limit_ref[pl.program_id(0)]
    dq, dk, dv = backward_pair(
        q_ref[...], k_ref[...], v_ref[...], grad_ref[...], norm_ref[0, 0, 0:PAIR], limit, True
    )
    dq_ref[...] = dq
    dk_ref[...] = dk
    dv_ref[...] = dv


def cross_forward_kernel(limit_ref, q_ref, k_ref, v_ref, mix_ref, norm_ref):
    limit = limit_ref[pl.program_id(0)]
    keys = k_ref.shape[0]
    short = keys // 4

    def run(count):
        mix, norms = forward_pair(q_ref[...], k_ref[0:count], v_ref[0:count], None, False)
        mix_ref[...] = mix
        norm_ref[0, 0, 0:PAIR] = norms

    pl.when(limit > short)(lambda: run(keys))
    pl.when(limit <= short)(lambda: run(short))


def cross_backward_kernel(
    limit_ref, q_ref, k_ref, v_ref, grad_ref, norm_ref, dq_ref, dk_ref, dv_ref
):
    limit = limit_ref[pl.program_id(0)]
    keys = k_ref.shape[0]
    short = keys // 4

    def run(count):
        dq, dk, dv = backward_pair(
            q_ref[...],
            k_ref[0:count],
            v_ref[0:count],
            grad_ref[...],
            norm_ref[0, 0, 0:PAIR],
            None,
            False,
        )
        dq_ref[...] = dq
        dk_ref[0:count] = dk
        dv_ref[0:count] = dv
        if count < keys:
            dk_ref[count:] = jnp.zeros((keys - count, LANES), BF16)
            dv_ref[count:] = jnp.zeros((keys - count, LANES), BF16)

    pl.when(limit > short)(lambda: run(keys))
    pl.when(limit <= short)(lambda: run(short))


def attend(kernel, limits, arrays, norms, examples, flops):
    width = arrays[0].shape[1]
    pairs = width // LANES
    queries = arrays[0].shape[0] // examples

    def rows_spec(array):
        return pl.BlockSpec((array.shape[0] // examples, LANES), lambda e, p: (e, p))

    norm_spec = pl.BlockSpec((1, 1, 8, queries), lambda e, p: (e, p, 0, 0))
    norm_shape = jax.ShapeDtypeStruct((examples, pairs, 8, queries), F32)
    in_specs = [pl.BlockSpec(memory_space=pltpu.SMEM)] + [rows_spec(a) for a in arrays]
    args = (limits,) + tuple(arrays)
    if norms is None:
        out_shape = (jax.ShapeDtypeStruct(arrays[0].shape, BF16), norm_shape)
        out_specs = (rows_spec(arrays[0]), norm_spec)
    else:
        in_specs.append(norm_spec)
        args = args + (norms,)
        out_shape = tuple(jax.ShapeDtypeStruct(a.shape, BF16) for a in arrays[:3])
        out_specs = tuple(rows_spec(a) for a in arrays[:3])
    return pl.pallas_call(
        kernel,
        grid=(examples, pairs),
        in_specs=in_specs,
        out_specs=out_specs,
        out_shape=out_shape,
        compiler_params=pltpu.CompilerParams(vmem_limit_bytes=VMEM_LIMIT),
        cost_estimate=pl.CostEstimate(
            flops=flops, bytes_accessed=sum(a.size * 2 for a in arrays), transcendentals=0
        ),
    )(*args)


HEAD_STATE = (
    "self_q",
    "self_k",
    "self_v",
    "self_mix",
    "normed_one",
    "hidden",
    "after_self",
    "grad_after_cross",
    "queries",
    "normed_two",
    "normed_three",
    "grad_mlp",
    "mlp_hidden",
    "grad_gate",
    "grad_up",
    "self_norms",
    "grad_mix",
    "cross_norms",
    "grad_k_early",
    "grad_v_early",
    "patch_early",
    "k_late",
    "v_late",
    "patch_rows_late",
    "layer_late",
    "dw_c_out",
)


def head_kernel(*refs):
    lengths_ref, counts_ref, g_self_ref, g_cross_ref, g_mlp_ref = refs[:5]
    hidden_in, patches_in, cot_in = refs[5:8]
    weights_in = refs[8:19]
    refs = refs[19:]
    small, patch_out, layer_out = refs[:3]
    kept = dict(zip(HEAD_STATE, refs[3 : 3 + len(HEAD_STATE)]))
    (
        hidden,
        cot,
        patch,
        normed_one,
        self_rows,
        after_self,
        normed_two,
        queries,
        keys,
        values,
        cmix,
        normed_three,
        mlp_rows,
        grad_after,
        cbranch,
        grad_mix,
        patch_send,
        layer,
        after_cross,
        mlp_sum,
        grad_three,
        squares,
        w_gate,
        w_up,
        w_down,
        self_norms,
        cross_norms,
        weight_sem,
        in_send,
        in_recv,
        in_local,
        out_send,
        out_recv,
        out_local,
        keep_sem,
    ) = refs[3 + len(HEAD_STATE) :]
    own = 2
    rows, width = hidden.shape
    text = rows // own
    slots = patch.shape[0] // own
    part, patch_part = text // 4, slots // 4
    pairs = width // LANES
    dp = lax.axis_index("dp")
    seq = lax.axis_index("seq")
    near_seq = seq + 1 - 2 * (seq % 2)
    far_seq = seq + 2 - 4 * (seq // 2)
    seq_peers = [far_seq, near_seq, 3 - seq]
    lengths = [lengths_ref[own * seq + e] for e in range(own)]
    counts = [counts_ref[own * seq + e] for e in range(own)]

    barrier = pltpu.get_barrier_semaphore()
    for z in seq_peers:
        pl.semaphore_signal(barrier, inc=1, device_id=(dp, z), device_id_type=MESH)
    pl.semaphore_wait(barrier, len(seq_peers))

    incoming = {}

    def receive(name, number, src, dst, size, e):
        first = pl.multiple_of(e * 4 * size + seq * size, size)
        copies = []
        for k, z in enumerate(seq_peers):
            copy = pltpu.make_async_remote_copy(
                src_ref=src.at[own * z + e],
                dst_ref=dst.at[pl.ds(first, size)],
                send_sem=in_send.at[number, k],
                recv_sem=in_recv.at[number, k],
                device_id=(dp, z),
                device_id_type=MESH,
            )
            copy.start()
            copies.append(copy)
        local_copy = pltpu.make_async_copy(
            src.at[own * seq + e], dst.at[pl.ds(first, size)], in_local.at[number]
        )
        local_copy.start()
        incoming[name] = (copies, local_copy)

    def arrived(name):
        copies, local_copy = incoming[name]
        local_copy.wait()
        for copy in copies:
            copy.wait_recv()

    receive("x0", 0, hidden_in, hidden, part, 0)
    receive("x1", 1, hidden_in, hidden, part, 1)

    loads = []
    targets = [squares.at[i] for i in range(8)] + [w_gate, w_up, w_down]
    for i, (src, dst) in enumerate(zip(weights_in, targets)):
        copy = pltpu.make_async_copy(src, dst, weight_sem.at[i])
        copy.start()
        loads.append(copy)
    WQ, WK, WV, WO, CQ, CK, CV, CO = range(8)

    keeping = []

    def keep(name, src):
        copy = pltpu.make_async_copy(src, kept[name], keep_sem.at[len(keeping)])
        copy.start()
        keeping.append(copy)

    small[...] = jnp.zeros(small.shape, F32)
    lane = lax.broadcasted_iota(jnp.int32, (1, width), 1)
    small[10:11] = jnp.where(
        lane == 0, lengths[0] + lengths[1], jnp.where(lane == 1, counts[0] + counts[1], 0)
    ).astype(F32)

    def add_row(i, value):
        small[i : i + 1, 0 : value.shape[1]] += value

    def valid_rows(e):
        position = lax.broadcasted_iota(jnp.int32, (text, 1), 0)
        return (position < lengths[e]).astype(F32)

    def squared(valid, value):
        return jnp.sum(valid * value * value, axis=0, keepdims=True)

    def norm(u, gain):
        r = lax.rsqrt(jnp.mean(u * u, axis=-1, keepdims=True) + NORM_EPS)
        return (u * r * gain).astype(BF16)

    for e in range(own):
        at = slice(e * text, (e + 1) * text)
        arrived("x%d" % e)
        if e == 0:
            for i in (WQ, WK, WV):
                loads[i].wait()
        else:
            receive("p0", 2, patches_in, patch, patch_part, 0)
        normed_one[at] = norm(hidden[at].astype(F32), g_self_ref[...].reshape(1, width))
        for i in (WQ, WK, WV):
            self_rows[i, at] = dot_nn(normed_one[at], squares[i]).astype(BF16)

    def self_pair(step, carry):
        e, p = step // pairs, step % pairs
        at = pl.ds(pl.multiple_of(e * text, text), text)
        lanes = pl.ds(pl.multiple_of(p * LANES, LANES), LANES)
        limit = lengths_ref[own * seq + e]
        mix, norms = forward_pair(
            self_rows[0, at, lanes], self_rows[1, at, lanes], self_rows[2, at, lanes], limit, True
        )
        self_rows[3, at, lanes] = mix
        self_norms[e, p, 0:PAIR] = norms
        return carry

    lax.fori_loop(0, own * pairs, self_pair, 0)
    receive("c0", 4, cot_in, cot, part, 0)
    receive("c1", 5, cot_in, cot, part, 1)
    loads[WO].wait()
    loads[CQ].wait()
    for e in range(own):
        at = slice(e * text, (e + 1) * text)
        branch = dot_nn(self_rows[3, at], squares[WO])
        add_row(4, squared(valid_rows(e), branch))
        after = hidden[at].astype(F32) + branch
        after_self[at] = after
        normed_two[at] = norm(after, g_cross_ref[...].reshape(1, width))
        queries[at] = dot_nn(normed_two[at], squares[CQ]).astype(BF16)
    for i, name in enumerate(("self_q", "self_k", "self_v", "self_mix")):
        keep(name, self_rows.at[i])
    keep("normed_one", normed_one)
    keep("hidden", hidden)
    keep("after_self", after_self)
    keep("self_norms", self_norms)

    def project_patches(e):
        def body(i, carry):
            at = pl.ds(pl.multiple_of(e * slots + i * patch_part, patch_part), patch_part)
            keys[at] = dot_nn(patch[at], squares[CK]).astype(BF16)
            values[at] = dot_nn(patch[at], squares[CV]).astype(BF16)
            return carry

        lax.fori_loop(0, 4, body, 0)

    def cross_forward(e):
        at, key_at = slice(e * text, (e + 1) * text), slice(e * slots, (e + 1) * slots)

        def body(p, carry):
            lanes = pl.ds(pl.multiple_of(p * LANES, LANES), LANES)
            mix, norms = forward_pair(
                queries[at, lanes], keys[key_at, lanes], values[key_at, lanes], counts[e], False
            )
            cmix[at, lanes] = mix
            cross_norms[e, p, 0:PAIR] = norms
            return carry

        lax.fori_loop(0, pairs, body, 0)

    def feed_forward(e):
        at = slice(e * text, (e + 1) * text)
        valid = valid_rows(e)
        branch = dot_nn(cmix[at], squares[CO])
        add_row(5, squared(valid, branch))
        after = after_self[at] + branch
        after_cross[...] = after
        normed_three[at] = norm(after, g_mlp_ref[...].reshape(1, width))
        arrived("c%d" % e)
        cot[at] = (cot[at].astype(F32) * valid).astype(BF16)
        mlp_sum[...] = jnp.zeros((text, width), F32)
        grad_three[...] = jnp.zeros((text, width), F32)
        step = w_gate.shape[1] // 4

        def body(i, total):
            columns = pl.ds(pl.multiple_of(i * step, step), step)
            gate = dot_nn(normed_three[at], w_gate[:, columns])
            up = dot_nn(normed_three[at], w_up[:, columns])
            tanh_part = jnp.tanh(GELU_CURVE * (gate + 0.044715 * gate * gate * gate))
            gelu = 0.5 * gate * (1.0 + tanh_part)
            slope = 0.5 * (1.0 + tanh_part) + 0.5 * gate * (1.0 - tanh_part * tanh_part) * (
                GELU_CURVE * (1.0 + 3.0 * 0.044715 * gate * gate)
            )
            value = gelu * up
            low_value = value.astype(BF16)
            mlp_rows[0, at, columns] = low_value
            mlp_sum[...] += dot_nn(low_value, w_down[columns, :])
            grad_value = dot_nt(cot[at], w_down[columns, :])
            grad_gate = (grad_value * up * slope).astype(BF16)
            grad_up = (grad_value * gelu).astype(BF16)
            mlp_rows[1, at, columns] = grad_gate
            mlp_rows[2, at, columns] = grad_up
            grad_three[...] += dot_nt(grad_gate, w_gate[:, columns]) + dot_nt(
                grad_up, w_up[:, columns]
            )
            return total + squared(valid, value)

        add_row(7, lax.fori_loop(0, 4, body, jnp.zeros((1, step), F32)))
        mlp_branch = mlp_sum[...]
        add_row(6, squared(valid, mlp_branch))
        after = after_cross[...]
        out = after + mlp_branch
        add_row(3, squared(valid, out))
        layer[at] = out.astype(BF16)
        w = grad_three[...]
        r = lax.rsqrt(jnp.mean(after * after, axis=-1, keepdims=True) + NORM_EPS)
        gw = g_mlp_ref[...].reshape(1, width) * w
        add_row(2, jnp.sum(w * after * r, axis=0, keepdims=True))
        grad = r * gw - after * (r * r * r) * jnp.mean(gw * after, axis=-1, keepdims=True)
        grad = cot[at].astype(F32) + grad
        grad_after[at] = grad
        cbranch[at] = grad.astype(BF16)
        grad_mix[at] = dot_nt(cbranch[at], squares[CO]).astype(BF16)

    def cross_backward(e):
        at, key_at = slice(e * text, (e + 1) * text), slice(e * slots, (e + 1) * slots)

        def body(p, carry):
            lanes = pl.ds(pl.multiple_of(p * LANES, LANES), LANES)
            dq, dk, dv = backward_pair(
                queries[at, lanes],
                keys[key_at, lanes],
                values[key_at, lanes],
                grad_mix[at, lanes],
                cross_norms[e, p, 0:PAIR],
                counts[e],
                False,
            )
            queries[at, lanes] = dq
            keys[key_at, lanes] = dk
            values[key_at, lanes] = dv
            return carry

        lax.fori_loop(0, pairs, body, 0)

    def patch_grads(e):
        def body(d, total):
            first = pl.multiple_of(d * patch_part, patch_part)
            at = pl.ds(e * slots + first, patch_part)
            value = dot_nt(keys[at], squares[CK]) + dot_nt(values[at], squares[CV])
            position = lax.broadcasted_iota(jnp.int32, (patch_part, 1), 0) + first
            patch_send[d] = value.astype(BF16)
            return total + squared((position < counts[e]).astype(F32), value)

        add_row(9, lax.fori_loop(0, 4, body, jnp.zeros((1, width), F32)))

    outgoing = []

    def send_rows(src_of, dst, number):
        for k, z in enumerate(seq_peers):
            copy = pltpu.make_async_remote_copy(
                src_ref=src_of(z),
                dst_ref=dst.at[seq],
                send_sem=out_send.at[number, k],
                recv_sem=out_recv.at[number, k],
                device_id=(dp, z),
                device_id_type=MESH,
            )
            copy.start()
            outgoing.append(copy)
        local_copy = pltpu.make_async_copy(src_of(seq), dst.at[seq], out_local.at[number])
        local_copy.start()
        keeping.append(local_copy)

    arrived("p0")
    receive("p1", 3, patches_in, patch, patch_part, 1)
    for copy in loads[CK:]:
        copy.wait()
    project_patches(0)
    cross_forward(0)
    feed_forward(0)
    send_rows(lambda z: layer.at[pl.ds(pl.multiple_of(z * part, part), part)], layer_out, 0)
    cross_backward(0)
    patch_grads(0)
    send_rows(lambda z: patch_send.at[z], patch_out, 1)
    keep("grad_k_early", keys.at[0:slots])
    keep("grad_v_early", values.at[0:slots])
    keep("patch_early", patch.at[0:slots])
    keep("normed_two", normed_two)
    arrived("p1")
    project_patches(1)
    keep("k_late", keys.at[slots : 2 * slots])
    keep("v_late", values.at[slots : 2 * slots])
    keep("patch_rows_late", patch.at[slots : 2 * slots])
    cross_forward(1)
    keep("queries", queries)
    keep("cross_norms", cross_norms.at[1])
    feed_forward(1)
    keep("grad_mlp", cot)
    keep("normed_three", normed_three)
    for i, name in enumerate(("mlp_hidden", "grad_gate", "grad_up")):
        keep(name, mlp_rows.at[i])
    keep("grad_after_cross", grad_after)
    keep("layer_late", layer.at[text : 2 * text])
    keep("grad_mix", grad_mix.at[text : 2 * text])

    for i in range(2):
        columns = slice(i * (width // 2), (i + 1) * (width // 2))
        squares[0, columns] = dot_tn(cmix[:, columns], cbranch[...]).astype(BF16)
    keep("dw_c_out", squares.at[0])
    for copies, local_copy in incoming.values():
        for copy in copies:
            copy.wait_send()
    for copy in outgoing:
        copy.wait()
    for copy in keeping:
        copy.wait()


def forward_head(lengths, counts, gains, rows, weights):
    examples, part, width = rows[0].shape
    patch_part = rows[1].shape[1]
    own = examples // 4
    text, slots = 4 * part, 4 * patch_part
    count, key_count = own * text, own * slots
    ff_width = weights[8].shape[1]
    pairs = width // LANES
    norms = (own, pairs, 8, text)
    vmem = pl.BlockSpec(memory_space=pltpu.VMEM)
    anywhere = pl.BlockSpec(memory_space=pl.ANY)
    smem = pl.BlockSpec(memory_space=pltpu.SMEM)
    low_shapes = dict(
        mlp_hidden=(count, ff_width),
        grad_gate=(count, ff_width),
        grad_up=(count, ff_width),
        grad_k_early=(slots, width),
        grad_v_early=(slots, width),
        patch_early=(slots, width),
        k_late=(slots, width),
        v_late=(slots, width),
        patch_rows_late=(slots, width),
        grad_mix=(text, width),
        layer_late=(text, width),
        dw_c_out=(width, width),
    )
    wide_shapes = dict(
        after_self=(count, width),
        grad_after_cross=(count, width),
        self_norms=norms,
        cross_norms=norms[1:],
    )
    state = []
    for name in HEAD_STATE:
        if name in wide_shapes:
            state.append(jax.ShapeDtypeStruct(wide_shapes[name], F32))
        else:
            state.append(jax.ShapeDtypeStruct(low_shapes.get(name, (count, width)), BF16))

    def low(*shape):
        return pltpu.VMEM(shape, BF16)

    def wide(*shape):
        return pltpu.VMEM(shape, F32)

    outs = pl.pallas_call(
        head_kernel,
        out_shape=(
            jax.ShapeDtypeStruct((16, width), F32),
            jax.ShapeDtypeStruct((4, patch_part, width), BF16),
            jax.ShapeDtypeStruct((4, part, width), BF16),
            *state,
        ),
        in_specs=[smem] * 2 + [vmem] * 3 + [anywhere] * 14,
        out_specs=(vmem,) + (anywhere,) * (2 + len(state)),
        scratch_shapes=[
            low(count, width),
            low(count, width),
            low(key_count, width),
            low(count, width),
            low(4, count, width),
            wide(count, width),
            low(count, width),
            low(count, width),
            low(key_count, width),
            low(key_count, width),
            low(count, width),
            low(count, width),
            low(3, count, ff_width),
            wide(count, width),
            low(count, width),
            low(count, width),
            low(4, patch_part, width),
            low(count, width),
            wide(text, width),
            wide(text, width),
            wide(text, width),
            low(8, width, width),
            low(width, ff_width),
            low(width, ff_width),
            low(ff_width, width),
            wide(*norms),
            wide(*norms),
            pltpu.SemaphoreType.DMA((11,)),
            pltpu.SemaphoreType.DMA((6, 3)),
            pltpu.SemaphoreType.DMA((6, 3)),
            pltpu.SemaphoreType.DMA((6,)),
            pltpu.SemaphoreType.DMA((2, 3)),
            pltpu.SemaphoreType.DMA((2, 3)),
            pltpu.SemaphoreType.DMA((2,)),
            pltpu.SemaphoreType.DMA((len(HEAD_STATE) + 2,)),
        ],
        compiler_params=pltpu.CompilerParams(
            collective_id=1, has_side_effects=True, vmem_limit_bytes=TAIL_VMEM
        ),
    )(lengths, counts, *gains, *rows, *weights)
    return outs[0], outs[1], outs[2], dict(zip(HEAD_STATE, outs[3:]))


TAIL_INPUTS = HEAD_STATE + ("c_key", "c_value", "c_query", "w_out", "w_query", "w_key", "w_value")


TAIL_ORDER = (
    "gate", "up", "down", ("core", 0), ("go", 0), ("core", 3), ("go", 3), "loads", "cross0",
    ("core", 1), ("go", 1), "cross1", ("core", 2), "c_query", ("go", 2), "middle", "patches",
    ("core", 4), ("go", 4), "keys", "self0", ("two", 0), "w_out", ("two", 1), "self1", "c_key",
    ("two", 2), "c_value", ("two", 4), "w_query", ("two", 3), "w_key", "w_value", ("core", 5),
    ("go", 5), ("core", 6), ("core", 7), ("go", 6), ("go", 7), ("three", 0), ("core", 8),
    ("core", 10), ("go", 8), ("core", 9), ("three", 2), ("go", 9), ("go", 10), "last", ("two", 6),
    ("three", 1), ("near", 0), ("two", 5), ("small", 0), ("two", 8), ("two", 7), ("near", 1),
    ("two", 10), ("small", 1), ("two", 9), ("near", 2), ("three", 3), ("three", 4), ("small", 2),
    ("three", 5), ("near", 3), ("near", 4), ("far", 0), ("small", 3), ("far", 1), ("near", 5),
    ("far", 3), ("far", 4), ("far", 2), ("far", 5), ("small", 4),
)


def tail_kernel(lengths_ref, counts_ref, g_self_ref, g_cross_ref, small_in, *refs):
    hbm = dict(zip(TAIL_INPUTS, refs))
    refs = refs[len(TAIL_INPUTS) :]
    narrow, wide, small_out, patch_out, x_out, layer_out = refs[:6]
    (
        after_self,
        grad_after,
        queries,
        normed,
        normed_two,
        mlp_rows,
        grad_mlp,
        big,
        grad_mix,
        cross_norms,
        self_norms,
        weights,
        wide_units,
        tall_units,
        wide_core,
        tall_core,
        wide_two,
        tall_two,
        wide_three,
        tall_three,
        square,
        square_core,
        square_two,
        square_three,
        cut_narrow,
        near_narrow,
        far_narrow,
        cut_wide,
        near_wide,
        far_wide,
        small_own,
        small_got,
        load_sem,
        send_sem,
        recv_sem,
        small_send,
        small_recv,
        cut_send,
        cut_recv,
        out_send,
        out_recv,
        out_local,
    ) = refs[6:]
    width = queries.shape[1]
    block = width // 8
    text = self_norms.shape[3]
    own = 2
    pairs = width // LANES
    part = text // 4

    dp = lax.axis_index("dp")
    seq = lax.axis_index("seq")
    core, x, y = dp % 2, (dp // 2) % 2, dp // 4
    low, high = seq % 2, seq // 2
    to_core = (dp + 1 - 2 * core, seq)
    to_x = (dp + 2 - 4 * x, seq)
    to_y = (dp + 4 - 8 * y, seq)
    near_seq = seq + 1 - 2 * low
    far_seq = seq + 2 - 4 * high
    last_seq = 3 - seq
    seq_peers = [near_seq, far_seq, last_seq]
    to_near, to_far = (dp, near_seq), (dp, far_seq)
    peers = [to_core, to_x, to_y, to_near, to_far, (dp, last_seq)]

    loads = {}

    ready = set()

    def need(*names):
        for name in names:
            if name not in ready:
                loads[name].wait()
                ready.add(name)

    def load(name, src, dst):
        copy = pltpu.make_async_copy(src, dst, load_sem.at[len(loads)])
        copy.start()
        loads[name] = copy

    slots = big.shape[0] // 4
    patch_part = slots // 4
    keys, values, patch, patch_send = (big.at[i * slots : (i + 1) * slots] for i in range(4))
    self_q, self_k, self_v, self_mix, hidden, sbranch = (
        mlp_rows.at[i // 2, :, i % 2 * width : (i % 2 + 1) * width] for i in range(6)
    )
    grad_smix = normed_two
    load("dw_c_out", hbm["dw_c_out"].at[:, :, core], square.at[0])
    load("normed", hbm["normed_three"], normed)
    load("grad_gate", hbm["grad_gate"], mlp_rows.at[1])
    load("grad_up", hbm["grad_up"], mlp_rows.at[2])
    load("queries", hbm["queries"], queries)
    load("keys", hbm["k_late"], keys)
    load("values", hbm["v_late"], values)
    load("grad_mix", hbm["grad_mix"], grad_mix)
    load("cross_norms", hbm["cross_norms"], cross_norms)
    load("c_key", hbm["c_key"], weights.at[0])
    load("c_value", hbm["c_value"], weights.at[1])
    load("patch", hbm["patch_rows_late"], patch)
    load("normed_two", hbm["normed_two"], normed_two)
    load("mlp_hidden", hbm["mlp_hidden"], mlp_rows.at[0])
    load("grad_mlp", hbm["grad_mlp"], grad_mlp)
    load("after_self", hbm["after_self"], after_self)
    load("grad_after", hbm["grad_after_cross"], grad_after)
    load("c_query", hbm["c_query"], weights.at[2])
    load("w_out", hbm["w_out"], weights.at[3])
    load("self_norms", hbm["self_norms"], self_norms)

    small_own[0] = small_in[...]

    def add_row(i, value):
        small_own[0, i : i + 1] += value

    barrier = pltpu.get_barrier_semaphore()
    for peer in peers:
        pl.semaphore_signal(barrier, inc=1, device_id=peer, device_id_type=MESH)
    pl.semaphore_wait(barrier, len(peers))

    def remote(src, dst, send, recv, device):
        copy = pltpu.make_async_remote_copy(
            src_ref=src,
            dst_ref=dst,
            send_sem=send,
            recv_sem=recv,
            device_id=device,
            device_id_type=MESH,
        )
        copy.start()
        return copy

    n_square = square_core.shape[0]
    y_first = (0, 2, 6, 8, 10)
    first, second, third, near, far, small = {}, {}, {}, {}, {}, {}
    got_core = [wide_core.at[0], wide_core.at[1], tall_core]
    got_core += [square_core.at[i] for i in range(n_square)]
    got_two = [wide_two.at[0], wide_two.at[1], tall_two]
    got_two += [square_two.at[i] for i in range(n_square)]
    got_three = [wide_three.at[0], wide_three.at[1], tall_three]
    got_three += [square_three.at[i] for i in range(n_square)]
    current = [wide_units.at[0], wide_units.at[1], tall_units.at[0]]
    current += [square.at[i] for i in range(n_square)]
    first[3] = remote(
        hbm["dw_c_out"].at[:, :, 1 - core],
        got_core[3],
        send_sem.at[0, 3],
        recv_sem.at[0, 3],
        to_core,
    )

    def add(out, got):
        rows = out.shape[0]
        step = 32

        def body(i, carry):
            at = pl.ds(pl.multiple_of(i * step, step), step)
            out[at, :] = (out[at, :].astype(F32) + got[at, :].astype(F32)).astype(BF16)
            return carry

        lax.fori_loop(0, rows // step, body, 0)

    def over_core(u):
        if u == 3:
            need("dw_c_out")
        first[u].wait_recv()
        for i in range(2):
            for j in range(2):
                add(current[u].at[i, j], got_core[u].at[i, j])

    def leave_two(u):
        cur = current[u]
        src, device = (cur.at[1 - y], to_y) if u in y_first else (cur.at[:, 1 - x], to_x)
        second[u] = remote(src, got_two[u], send_sem.at[1, u], recv_sem.at[1, u], device)

    def over_two(u):
        second[u].wait_recv()
        cur = current[u]
        for i in range(2):
            add(cur.at[y, i] if u in y_first else cur.at[i, x], got_two[u].at[i])
        src, device = (cur.at[y, 1 - x], to_x) if u in y_first else (cur.at[1 - y, x], to_y)
        third[u] = remote(src, got_three[u], send_sem.at[2, u], recv_sem.at[2, u], device)

    groups = [(1, 0, block, (0, 1)), (0, n_square // 2 * block, tall_three.shape[0] // 2, (2,))]
    groups += [(0, i * block, block, (3 + 2 * i, 4 + 2 * i)) for i in range(n_square // 2)]
    cut, got_near, got_far = (cut_narrow, cut_wide), (near_narrow, near_wide), (far_narrow, far_wide)
    totals = (narrow, wide)

    def over_three(g):
        buffer, row, rows, members = groups[g]
        for u in members:
            third[u].wait_recv()
        halves = [current[u][y, x].astype(F32) + got_three[u][...].astype(F32) for u in members]
        if len(members) == 1:
            halves = [halves[0][:rows], halves[0][rows:]]
        piece = halves[0].shape[1] // 4
        at = pl.ds(row, rows)
        for z in range(4):
            columns = [h[:, z * piece : (z + 1) * piece] for h in halves]
            cut[buffer][z // 2, z % 2, at] = jnp.concatenate(columns, axis=1).astype(BF16)
        near[g] = remote(
            cut[buffer].at[:, 1 - low, at],
            got_near[buffer].at[:, at],
            cut_send.at[0, g],
            cut_recv.at[0, g],
            to_near,
        )

    def over_near(g):
        buffer, row, rows, _ = groups[g]
        near[g].wait_recv()
        at = pl.ds(row, rows)
        for i in range(2):
            add(cut[buffer].at[i, low, at], got_near[buffer].at[i, at])
        far[g] = remote(
            cut[buffer].at[1 - high, low, at],
            got_far[buffer].at[at],
            cut_send.at[1, g],
            cut_recv.at[1, g],
            to_far,
        )

    def over_far(g):
        buffer, row, rows, _ = groups[g]
        far[g].wait_recv()
        at = pl.ds(row, rows)
        totals[buffer][at] = cut[buffer][high, low, at].astype(F32) + got_far[buffer][at].astype(F32)

    def give(u, src):
        first[u] = remote(src, got_core[u], send_sem.at[0, u], recv_sem.at[0, u], to_core)

    def weight_grad(i, rows, grad_rows, more=None):
        ring = n_square + len(ring_units) % 2
        if len(ring_units) >= 2:
            first[ring_units[-2]].wait_send()
            first_sent.add(ring_units[-2])
        ring_units.append(3 + i)
        half = width // 2
        for h in range(2):
            value = dot_tn(rows[:, h * half : (h + 1) * half], grad_rows[...])
            if more is not None:
                value = value + more[h * half : (h + 1) * half].astype(F32)
            value = value.astype(BF16)
            for j in range(4):
                at = i + ((j + core) % 2) * (ring - i)
                square[at, h, j // 2] = value[j * block : (j + 1) * block]
        give(3 + i, square.at[ring])

    def wide_grad(u):
        if u == 1:
            first[0].wait_send()
            first_sent.add(0)
        half, step = width // 2, wide_units.shape[4] // 4

        def body(i, carry):
            columns = pl.ds(pl.multiple_of(i * step, step), step)
            for h in range(2):
                value = dot_tn(
                    normed[:, h * half : (h + 1) * half], mlp_rows[1 + u, :, columns]
                ).astype(BF16)
                for j in range(4):
                    at = u + ((j + core) % 2) * (2 - u)
                    wide_units[at, h, j // 2, :, columns] = value[j * block : (j + 1) * block]
            return carry

        lax.fori_loop(0, 4, body, 0)
        give(u, wide_units.at[2])

    def tall_grad():
        rows = tall_units.shape[3]

        def body(j, carry):
            columns = pl.ds(pl.multiple_of(j * rows, rows), rows)
            value = dot_tn(mlp_rows[0, :, columns], grad_mlp[...]).astype(BF16)
            tall_units[(j + core) % 2, j // 4, (j // 2) % 2] = value
            return carry

        lax.fori_loop(0, 8, body, 0)
        give(2, tall_units.at[1])

    first_sent, ring_units = set(), []

    outs, locals_ = [], []

    def send_rows(src_of, dst, number):
        for k, z in enumerate([far_seq, near_seq, last_seq]):
            outs.append(
                remote(src_of(z), dst, out_send.at[number, k], out_recv.at[number, k], (dp, z))
            )
        copy = pltpu.make_async_copy(src_of(seq), dst, out_local.at[number])
        copy.start()
        locals_.append(copy)

    send_rows(
        lambda z: hbm["layer_late"].at[pl.ds(pl.multiple_of(z * part, part), part)],
        layer_out.at[seq],
        1,
    )
    chunk = own * text // 4
    late = slice(text, 2 * text)
    limit = counts_ref[own * seq + 1]

    def cross_pairs(first_pair, last_pair):
        def body(p, carry):
            lanes = pl.ds(pl.multiple_of(p * LANES, LANES), LANES)
            dq, dk, dv = backward_pair(
                queries[late, lanes],
                keys[:, lanes],
                values[:, lanes],
                grad_mix[:, lanes],
                cross_norms[p, 0:PAIR],
                limit,
                False,
            )
            queries[late, lanes] = dq
            keys[:, lanes] = dk
            values[:, lanes] = dv
            return carry

        lax.fori_loop(first_pair, last_pair, body, 0)

    def patch_grads():
        def body(d, total):
            at = pl.ds(pl.multiple_of(d * patch_part, patch_part), patch_part)
            value = dot_nt(keys[at, :], weights[0]) + dot_nt(values[at, :], weights[1])
            position = lax.broadcasted_iota(jnp.int32, (patch_part, 1), 0) + d * patch_part
            patch_send[at, :] = value.astype(BF16)
            valid = (position < limit).astype(F32)
            return total + jnp.sum(valid * value * value, axis=0, keepdims=True)

        add_row(9, lax.fori_loop(0, 4, body, jnp.zeros((1, width), F32)))
        send_rows(
            lambda z: patch_send.at[pl.ds(pl.multiple_of(z * patch_part, patch_part), patch_part)],
            patch_out.at[seq],
            0,
        )

    def gate_weight():
        need("normed", "grad_gate")
        wide_grad(0)

    def up_weight():
        need("normed", "grad_up")
        wide_grad(1)
        load("normed_one", hbm["normed_one"], normed)

    def down_weight():
        need("mlp_hidden", "grad_mlp")
        tall_grad()

    def cross_some(first_pair, last_pair):
        need("queries", "keys", "values", "grad_mix", "cross_norms")
        cross_pairs(first_pair, last_pair)

    def late_patches():
        need("c_key", "c_value")
        patch_grads()

    def late_keys():
        need("patch")
        half = width // 2
        for slot, right in ((0, keys), (1, values)):
            for h in range(2):
                columns = slice(h * half, (h + 1) * half)
                weights[slot, columns] = dot_tn(patch[:, columns], right[...]).astype(BF16)
        load("grad_k", hbm["grad_k_early"], keys)
        load("grad_v", hbm["grad_v_early"], values)
        load("patch_early", hbm["patch_early"], patch)

    def query_weight():
        need("normed_two")
        weight_grad(1, normed_two, queries)

    def key_weight():
        need("grad_k", "patch_early")
        weight_grad(2, patch, keys, weights.at[0])

    def value_weight():
        need("grad_v", "patch_early")
        weight_grad(3, patch, values, weights.at[1])
        load("w_query", hbm["w_query"], weights.at[0])
        load("w_key", hbm["w_key"], weights.at[1])

    def self_loads():
        for name, dst in (
            ("self_q", self_q),
            ("self_k", self_k),
            ("self_v", self_v),
            ("self_mix", self_mix),
            ("hidden", hidden),
        ):
            load(name, hbm[name], dst)

    def out_weight():
        need("self_mix")
        weight_grad(4, self_mix, sbranch)

    def self_weight(i, rows):
        need("normed_one")
        weight_grad(i, normed, rows)

    def norm_grad(u, gain, w):
        r = lax.rsqrt(jnp.mean(u * u, axis=-1, keepdims=True) + NORM_EPS)
        gw = gain * w
        grad = r * gw - u * (r * r * r) * jnp.mean(gw * u, axis=-1, keepdims=True)
        return grad, jnp.sum(w * u * r, axis=0, keepdims=True)

    def middle(i, total):
        at = pl.ds(pl.multiple_of(i * chunk, chunk), chunk)
        w = dot_nt(queries[at, :], weights[2])
        grad, row = norm_grad(after_self[at, :], g_cross_ref[...].reshape(1, width), w)
        grad = grad_after[at, :] + grad
        grad_after[at, :] = grad
        low_grad = grad.astype(BF16)
        sbranch[at, :] = low_grad
        grad_smix[at, :] = dot_nt(low_grad, weights[3]).astype(BF16)
        return total + row

    def self_inputs():
        need("after_self", "grad_after", "c_query", "w_out")
        add_row(1, lax.fori_loop(0, 4, middle, jnp.zeros((1, width), F32)))
        load("w_value", hbm["w_value"], weights.at[2])

    def self_pairs(first_step, last_step):
        def body(i, carry):
            e, p = i // pairs, i % pairs
            rows = pl.ds(pl.multiple_of(e * text, text), text)
            lanes = pl.ds(pl.multiple_of(p * LANES, LANES), LANES)
            dq, dk, dv = backward_pair(
                self_q[rows, lanes],
                self_k[rows, lanes],
                self_v[rows, lanes],
                grad_smix[rows, lanes],
                self_norms[e, p, 0:PAIR],
                lengths_ref[own * seq + e],
                True,
            )
            self_q[rows, lanes] = dq
            self_k[rows, lanes] = dk
            self_v[rows, lanes] = dv
            return carry

        lax.fori_loop(first_step, last_step, body, 0)

    def self_some(first_step, last_step):
        need("self_q", "self_k", "self_v", "self_norms")
        self_pairs(first_step, last_step)

    def last(i, carry):
        total, squares = carry
        at = pl.ds(pl.multiple_of(i * chunk, chunk), chunk)
        w = (
            dot_nt(self_q[at, :], weights[0])
            + dot_nt(self_k[at, :], weights[1])
            + dot_nt(self_v[at, :], weights[2])
        )
        grad, row = norm_grad(hidden[at, :].astype(F32), g_self_ref[...].reshape(1, width), w)
        grad = grad_after[at, :] + grad
        e, half = i // 2, i % 2
        position = lax.broadcasted_iota(jnp.int32, (chunk, 1), 0) + half * chunk
        valid = (position < lengths_ref[own * seq + e]).astype(F32)
        low_grad = grad.astype(BF16)
        for k in range(2):
            place = (2 * half + k) * own + e
            grad_mlp[pl.ds(pl.multiple_of(place * part, part), part)] = low_grad[
                k * part : (k + 1) * part
            ]
        return total + row, squares + jnp.sum(valid * grad * grad, axis=0, keepdims=True)

    def inputs_grad():
        need("w_query", "w_key", "w_value", "hidden")
        zero = jnp.zeros((1, width), F32)
        total, squares = lax.fori_loop(0, 4, last, (zero, zero))
        add_row(0, total)
        add_row(8, squares)
        leaving = own * part
        send_rows(
            lambda z: grad_mlp.at[pl.ds(pl.multiple_of(z * leaving, leaving), leaving)],
            x_out.at[seq],
            2,
        )
        send_small(0)

    def send_small(i):
        small[i] = remote(
            small_own.at[i], small_got.at[i], small_send.at[i], small_recv.at[i], peers[i]
        )

    def add_small(i):
        small[i].wait_recv()
        small_own[i + 1] = small_own[i] + small_got[i]

    def pass_small(i):
        add_small(i)
        if i < 4:
            send_small(i + 1)

    work = {
        "gate": gate_weight,
        "up": up_weight,
        "down": down_weight,
        "cross0": lambda: cross_some(0, pairs // 2),
        "cross1": lambda: cross_some(pairs // 2, pairs),
        "patches": late_patches,
        "keys": late_keys,
        "c_query": query_weight,
        "c_key": key_weight,
        "c_value": value_weight,
        "loads": self_loads,
        "middle": self_inputs,
        "w_out": out_weight,
        "self0": lambda: self_some(0, pairs),
        "self1": lambda: self_some(pairs, 2 * pairs),
        "last": inputs_grad,
        "w_query": lambda: self_weight(5, self_q),
        "w_key": lambda: self_weight(6, self_k),
        "w_value": lambda: self_weight(7, self_v),
    }
    exchange = {
        "core": over_core,
        "go": leave_two,
        "two": over_two,
        "three": over_three,
        "near": over_near,
        "far": over_far,
        "small": pass_small,
    }
    for step in TAIL_ORDER:
        if step in work:
            work[step]()
        else:
            exchange[step[0]](step[1])
    small_out[...] = small_own[5]
    for copy in outs:
        copy.wait_recv()
    for copy in locals_:
        copy.wait()
    for u, copy in first.items():
        if u not in first_sent:
            copy.wait_send()
    for copies in (second, third, near, far, small):
        for copy in copies.values():
            copy.wait_send()
    for copy in outs:
        copy.wait_send()


def finish_kernel(groups, ff_width, *refs):
    narrow_ref, wide_ref, small_ref, patch_early, patch_late, layer_early, layer_late, x_in = refs[:8]
    layer_out, x_out, patch_out, gain_self, gain_cross, gain_mlp, rms_out = refs[8:15]
    out_refs = refs[15:]
    step = pl.program_id(0)
    x_out[...] = x_in[...].astype(F32)

    @pl.when(step % 2 == 0)
    def even():
        patch_out[...] = patch_early[...].astype(F32)
        layer_out[...] = layer_early[...].astype(F32)

    @pl.when(step % 2 == 1)
    def odd():
        patch_out[...] = patch_late[...].astype(F32)
        layer_out[...] = layer_late[...].astype(F32)

    @pl.when(step == 0)
    def sums():
        for buffer, row, rows, members in groups:
            total = (narrow_ref, wide_ref)[buffer][row : row + rows]
            part = total.shape[1] // 2
            if len(members) == 2:
                out_refs[members[0]][...] = total[:, :part]
                out_refs[members[1]][...] = total[:, part:]
            else:
                out_refs[members[0]][0:rows] = total[:, :part]
                out_refs[members[0]][rows:] = total[:, part:]
        small = small_ref[...]
        width = small.shape[1]
        piece = width // 8
        for i, gain in enumerate((gain_self, gain_cross, gain_mlp)):
            for d in range(8):
                value = small[i : i + 1, d * piece : (d + 1) * piece]
                pl.when(lax.axis_index("dp") == d)(partial(store, gain, value))
        squares = jnp.sum(small, axis=1, keepdims=True)
        row = lax.broadcasted_iota(jnp.int32, squares.shape, 0)
        texts, patch_count = small[10:11, 0:1], small[10:11, 1:2]
        count = jnp.where(
            row == 9, patch_count * width, jnp.where(row == 7, texts * ff_width, texts * width)
        )
        rms_out[...] = jnp.sqrt(squares / count)


def store(ref, value):
    ref[...] = value


def takes_kernel(width, n_dp, n_seq, own):
    return (
        n_dp == 8
        and n_seq == 4
        and own == 2
        and width // n_dp % 32 == 0
        and width % (2 * LANES) == 0
    )


def backward_tail(lengths, counts, g_self, g_cross, small, arrays):
    n_square, n_late = 8, 4
    own, pairs, _, text = arrays["self_norms"].shape
    count, width = arrays["self_q"].shape
    ff_width = arrays["mlp_hidden"].shape[1]
    block, tall = width // 8, ff_width // 8
    tops = ((n_square // 2 * block + tall // 2, width // 2), (block, ff_width // 2))
    arrays = dict(arrays)
    arrays["dw_c_out"] = arrays["dw_c_out"].reshape(2, 2, 2, block, width)
    slots = arrays["k_late"].shape[0]
    vmem = pl.BlockSpec(memory_space=pltpu.VMEM)
    anywhere = pl.BlockSpec(memory_space=pl.ANY)
    smem = pl.BlockSpec(memory_space=pltpu.SMEM)

    def low(*shape):
        return pltpu.VMEM(shape, BF16)

    def wide(*shape):
        return pltpu.VMEM(shape, F32)

    units = n_square + 3
    n_groups = n_square // 2 + 2
    narrow, wide_total, total, patch_rows, x_rows, layer_rows = pl.pallas_call(
        tail_kernel,
        out_shape=tuple(jax.ShapeDtypeStruct(t, F32) for t in tops + (small.shape,))
        + (
            jax.ShapeDtypeStruct((4, slots // 4, width), BF16),
            jax.ShapeDtypeStruct((4, count // 4, width), BF16),
            jax.ShapeDtypeStruct((4, text // 4, width), BF16),
        ),
        in_specs=[smem] * 2 + [vmem] * 3 + [anywhere] * len(TAIL_INPUTS),
        out_specs=(vmem,) * 3 + (anywhere,) * 3,
        scratch_shapes=[
            wide(count, width),
            wide(count, width),
            low(count, width),
            low(count, width),
            low(count, width),
            low(3, count, ff_width),
            low(count, width),
            low(4 * slots, width),
            low(text, width),
            wide(*arrays["cross_norms"].shape),
            wide(*arrays["self_norms"].shape),
            low(4, width, width),
            low(3, 2, 2, block, ff_width),
            low(2, 2, 2, tall, width),
            low(2, 2, 2, block, ff_width),
            low(2, 2, tall, width),
            low(2, 2, block, ff_width),
            low(2, tall, width),
            low(2, block, ff_width),
            low(tall, width),
            low(n_square + 2, 2, 2, block, width),
            low(n_square, 2, 2, block, width),
            low(n_square, 2, block, width),
            low(n_square, block, width),
            low(2, 2, *tops[0]),
            low(2, *tops[0]),
            low(*tops[0]),
            low(2, 2, *tops[1]),
            low(2, *tops[1]),
            low(*tops[1]),
            wide(6, *small.shape),
            wide(5, *small.shape),
            pltpu.SemaphoreType.DMA((32,)),
            pltpu.SemaphoreType.DMA((3, units)),
            pltpu.SemaphoreType.DMA((3, units)),
            pltpu.SemaphoreType.DMA((5,)),
            pltpu.SemaphoreType.DMA((5,)),
            pltpu.SemaphoreType.DMA((2, n_groups)),
            pltpu.SemaphoreType.DMA((2, n_groups)),
            pltpu.SemaphoreType.DMA((3, 3)),
            pltpu.SemaphoreType.DMA((3, 3)),
            pltpu.SemaphoreType.DMA((3,)),
        ],
        compiler_params=pltpu.CompilerParams(
            collective_id=0, has_side_effects=True, vmem_limit_bytes=TAIL_VMEM
        ),
    )(lengths, counts, g_self, g_cross, small, *[arrays[n] for n in TAIL_INPUTS])
    return narrow, wide_total, total, patch_rows, x_rows, layer_rows


def finish(narrow, wide_total, total, patches, layers, x_rows):
    n_square = 8
    parts, patch_part, width = patches[0].shape
    part = layers[0].shape[1]
    examples = 2 * parts
    block, ff_width = width // 8, 2 * wide_total.shape[1]
    tall = 2 * (narrow.shape[0] - n_square // 2 * block)
    groups = [(1, 0, block, (0, 1)), (0, n_square // 2 * block, tall // 2, (2,))]
    groups += [(0, i * block, block, (3 + 2 * i, 4 + 2 * i)) for i in range(n_square // 2)]
    shapes = [(block, ff_width // 4)] * 2 + [(tall, width // 4)] + [(block, width // 4)] * n_square

    def whole(shape):
        return pl.BlockSpec(shape, lambda e: (0,) * len(shape))

    def example(rows):
        return pl.BlockSpec((1, rows, width), lambda e: (e, 0, 0))

    def pair(rows):
        return pl.BlockSpec((1, rows, width), lambda e: (e // 2, 0, 0))

    outs = [
        ((examples, part, width), example(part)),
        ((examples, part, width), example(part)),
        ((examples, patch_part, width), example(patch_part)),
        ((1, block), whole((1, block))),
        ((1, block), whole((1, block))),
        ((1, block), whole((1, block))),
        ((total.shape[0], 1), whole((total.shape[0], 1))),
    ] + [(s, whole(s)) for s in shapes]
    results = pl.pallas_call(
        partial(finish_kernel, groups, ff_width),
        grid=(examples,),
        out_shape=tuple(jax.ShapeDtypeStruct(s, F32) for s, _ in outs),
        in_specs=[whole(narrow.shape), whole(wide_total.shape), whole(total.shape)]
        + [pair(patch_part)] * 2
        + [pair(part)] * 2
        + [example(part)],
        out_specs=tuple(spec for _, spec in outs),
        compiler_params=pltpu.CompilerParams(vmem_limit_bytes=TAIL_VMEM),
    )(narrow, wide_total, total, *patches, *layers, x_rows)
    gains = [g[0] for g in results[3:6]]
    return results[:3], gains, results[6][3:10, 0], results[7:]


def norm_forward(u, gain):
    r = lax.rsqrt(jnp.mean(u * u, axis=-1, keepdims=True) + NORM_EPS)
    return (u * r * gain).astype(BF16)


def norm_backward(u, gain, w):
    r = lax.rsqrt(jnp.mean(u * u, axis=-1, keepdims=True) + NORM_EPS)
    gw = gain * w
    grad = r * gw - u * (r * r * r) * jnp.mean(gw * u, axis=-1, keepdims=True)
    return grad, jnp.sum(w * u * r, axis=0, keepdims=True)


def to_examples(rows):
    n = lax.axis_size("seq")
    examples, part, width = rows.shape
    parts = lax.all_to_all(rows.reshape(n, examples // n, part, width), "seq", 0, 0)
    return parts.transpose(1, 0, 2, 3).reshape(examples // n, n * part, width)


def to_positions(rows):
    n = lax.axis_size("seq")
    own, positions, width = rows.shape
    parts = rows.reshape(own, n, positions // n, width).transpose(1, 0, 2, 3)
    return lax.all_to_all(parts, "seq", 0, 0).reshape(n * own, positions // n, width)


def halve_over_dp(matrix, bits):
    n = lax.axis_size("dp")
    count = n.bit_length() - 1
    rows, width = matrix.shape[0] // n, matrix.shape[1]
    place = lax.axis_index("dp")
    left = list(range(count))[::-1]
    current = matrix.reshape((2,) * count + (rows, width))
    for bit in bits:
        axis = left.index(bit)
        mine = (place >> bit) & 1
        keep = lax.dynamic_index_in_dim(current, mine, axis, keepdims=False)
        give = lax.dynamic_index_in_dim(current, 1 - mine, axis, keepdims=False)
        got = lax.ppermute(give, "dp", [(i, i ^ (1 << bit)) for i in range(n)])
        current = (keep.astype(F32) + got.astype(F32)).astype(BF16)
        left.remove(bit)
    return current


def scatter_over_seq(matrix):
    n = lax.axis_size("seq")
    rows, width = matrix.shape
    parts = matrix.reshape(rows, n, width // n).transpose(1, 0, 2)
    return jnp.sum(lax.all_to_all(parts, "seq", 0, 0).astype(F32), axis=0)


def reduce_grad(matrix, order):
    n = lax.axis_size("dp")
    bits = list(range(n.bit_length() - 1))
    if order:
        bits = bits[:1] + bits[1:][::-1]
    return scatter_over_seq(halve_over_dp(matrix, bits))


def local(
    hidden_in,
    patches,
    text_lengths,
    patch_counts,
    cotangent,
    g_self,
    g_cross,
    g_mlp,
    w_query,
    w_key,
    w_value,
    w_out,
    c_query,
    c_key,
    c_value,
    c_out,
    w_gate,
    w_up,
    w_down,
):
    n_seq = lax.axis_size("seq")
    n_dp = lax.axis_size("dp")
    seq_place = lax.axis_index("seq")
    dp_place = lax.axis_index("dp")
    width = hidden_in.shape[2]
    ff_width = w_gate.shape[1]
    own = hidden_in.shape[0] // n_seq
    if takes_kernel(width, n_dp, n_seq, own):
        small, patch_early, layer_early, state = forward_head(
            text_lengths[0],
            patch_counts,
            (g_self, g_cross, g_mlp),
            (hidden_in, patches, cotangent),
            (
                w_query,
                w_key,
                w_value,
                w_out,
                c_query,
                c_key,
                c_value,
                c_out,
                w_gate,
                w_up,
                w_down,
            ),
        )
        state.update(
            c_key=c_key,
            c_value=c_value,
            c_query=c_query,
            w_out=w_out,
            w_query=w_query,
            w_key=w_key,
            w_value=w_value,
        )
        narrow, wide, total, patch_late, x_out, layer_late = backward_tail(
            text_lengths[0], patch_counts, g_self, g_cross, small, state
        )
        rows, gains, rms_values, grads = finish(
            narrow,
            wide,
            total,
            (patch_early, patch_late),
            (layer_early, layer_late),
            x_out.reshape(hidden_in.shape),
        )
        gate, up, down, c_o, c_q, c_k, c_v, w_o, w_q, w_k, w_v = grads
        return (
            *rows,
            *gains,
            w_q,
            w_k,
            w_v,
            w_o,
            c_q,
            c_k,
            c_v,
            c_o,
            gate,
            up,
            down,
            rms_values,
        )
    else:
        lengths = lax.dynamic_slice_in_dim(text_lengths[0], seq_place * own, own)
        counts = lax.dynamic_slice_in_dim(patch_counts, seq_place * own, own)

        hidden = to_examples(hidden_in)
        patch = to_examples(patches)
        text = hidden.shape[1]
        slots = patch.shape[1]
        text_valid = (jnp.arange(text)[None, :] < lengths[:, None]).astype(F32).reshape(-1, 1)
        patch_valid = (jnp.arange(slots)[None, :] < counts[:, None]).astype(F32).reshape(-1, 1)
        x = hidden.reshape(-1, width).astype(F32)
        patch = patch.reshape(-1, width)
        self_flops = 4 * own * text * text * width
        cross_flops = 4 * own * text * slots * width

        normed_one = norm_forward(x, g_self)
        self_q = dot_nn(normed_one, w_query).astype(BF16)
        self_k = dot_nn(normed_one, w_key).astype(BF16)
        self_v = dot_nn(normed_one, w_value).astype(BF16)
        self_mix, self_norms = attend(
            self_forward_kernel, lengths, (self_q, self_k, self_v), None, own, self_flops
        )
        cot = to_examples(cotangent)
        self_branch = dot_nn(self_mix, w_out)
        after_self = x + self_branch
        normed_two = norm_forward(after_self, g_cross)
        cross_q = dot_nn(normed_two, c_query).astype(BF16)
        cross_k = dot_nn(patch, c_key).astype(BF16)
        cross_v = dot_nn(patch, c_value).astype(BF16)
        cross_mix, cross_norms = attend(
            cross_forward_kernel, counts, (cross_q, cross_k, cross_v), None, own, cross_flops
        )
        cross_branch = dot_nn(cross_mix, c_out)
        after_cross = after_self + cross_branch
        normed_three = norm_forward(after_cross, g_mlp)
        gate = dot_nn(normed_three, w_gate)
        up = dot_nn(normed_three, w_up)
        tanh_part = jnp.tanh(GELU_CURVE * (gate + 0.044715 * gate * gate * gate))
        gelu = 0.5 * gate * (1.0 + tanh_part)
        gelu_slope = 0.5 * (1.0 + tanh_part) + 0.5 * gate * (1.0 - tanh_part * tanh_part) * (
            GELU_CURVE * (1.0 + 3.0 * 0.044715 * gate * gate)
        )
        hidden_value = gelu * up
        hidden_low = hidden_value.astype(BF16)
        mlp_branch = dot_nn(hidden_low, w_down)
        layer_rows = after_cross + mlp_branch

        grad_y = cot.reshape(-1, width).astype(F32) * text_valid
        grad_mlp = grad_y.astype(BF16)
        grad_hidden = dot_nt(grad_mlp, w_down)
        grad_gate = (grad_hidden * up * gelu_slope).astype(BF16)
        grad_up = (grad_hidden * gelu).astype(BF16)
        grad_mlp_rows = (
            dot_tn(normed_three, grad_gate).astype(BF16),
            dot_tn(normed_three, grad_up).astype(BF16),
            dot_tn(hidden_low, grad_mlp).astype(BF16),
        )
        grad_three = dot_nt(grad_gate, w_gate) + dot_nt(grad_up, w_up)
        norm_grad, grad_g_mlp = norm_backward(after_cross, g_mlp, grad_three)
        grad_after_cross = grad_y + norm_grad
        grad_cbranch = grad_after_cross.astype(BF16)
        grad_cmix = dot_nt(grad_cbranch, c_out).astype(BF16)

        def square_row(valid, value):
            return jnp.sum(valid * value * value, axis=0, keepdims=True)

        lane = jnp.arange(LANES)
        valid_row = jnp.where(
            lane == 0, jnp.sum(lengths), jnp.where(lane == 1, jnp.sum(counts), 0)
        ).astype(F32)
        layer_low = layer_rows.astype(BF16)
        grad_cq, grad_ck, grad_cv = attend(
            cross_backward_kernel,
            counts,
            (cross_q, cross_k, cross_v, grad_cmix),
            cross_norms,
            own,
            cross_flops * 5 // 2,
        )
        grad_patch_rows = dot_nt(grad_ck, c_key) + dot_nt(grad_cv, c_value)
        grad_two = dot_nt(grad_cq, c_query)
        norm_grad, grad_g_cross = norm_backward(after_self, g_cross, grad_two)
        grad_after_self = grad_after_cross + norm_grad
        grad_sbranch = grad_after_self.astype(BF16)
        grad_smix = dot_nt(grad_sbranch, w_out).astype(BF16)
        grad_sq, grad_sk, grad_sv = attend(
            self_backward_kernel,
            lengths,
            (self_q, self_k, self_v, grad_smix),
            self_norms,
            own,
            self_flops * 5 // 2,
        )
        grad_one = dot_nt(grad_sq, w_query) + dot_nt(grad_sk, w_key) + dot_nt(grad_sv, w_value)
        norm_grad, grad_g_self = norm_backward(x, g_self, grad_one)
        grad_x_rows = grad_after_self + norm_grad
        layer_out = to_positions(layer_low.reshape(own, text, width))
        patch_out = to_positions(grad_patch_rows.astype(BF16).reshape(own, slots, width))
        x_out = to_positions(grad_x_rows.astype(BF16).reshape(own, text, width))
        grads = [
            dot_tn(rows, grad_rows).astype(BF16)
            for rows, grad_rows in (
                (normed_one, grad_sq),
                (normed_one, grad_sk),
                (normed_one, grad_sv),
                (self_mix, grad_sbranch),
                (normed_two, grad_cq),
                (patch, grad_ck),
                (patch, grad_cv),
                (cross_mix, grad_cbranch),
            )
        ]
        grads += grad_mlp_rows
        summed = tuple(reduce_grad(g, u % 2) for u, g in enumerate(grads))
        vectors = [
            grad_g_self,
            grad_g_cross,
            grad_g_mlp,
            square_row(text_valid, layer_rows),
            square_row(text_valid, self_branch),
            square_row(text_valid, cross_branch),
            square_row(text_valid, mlp_branch),
            square_row(text_valid, hidden_value),
            square_row(text_valid, grad_x_rows),
            square_row(patch_valid, grad_patch_rows),
            valid_row[None],
        ]
        folded = [
            sum(
                jnp.pad(p, ((0, 0), (0, width - p.shape[1])))
                for p in jnp.split(v, list(range(width, v.shape[1], width)), axis=1)
            )
            for v in vectors
        ]
        total = lax.psum(jnp.concatenate(folded), ("dp", "seq"))
    part = width // n_dp
    gains = [lax.dynamic_slice(total, (i, dp_place * part), (1, part))[0] for i in range(3)]
    squares = jnp.sum(total[3:10], axis=1)
    place = jnp.arange(7)
    texts, patch_count = total[10, 0], total[10, 1]
    per_value = jnp.where(
        place == 6, patch_count * width, jnp.where(place == 4, texts * ff_width, texts * width)
    )
    rms_values = jnp.sqrt(squares / per_value)
    return (
        layer_out.astype(F32),
        x_out.astype(F32),
        patch_out.astype(F32),
        gains[0],
        gains[1],
        gains[2],
        *summed,
        rms_values,
    )


def solution(mesh):
    rows = P("dp", "seq", None)
    tile = P("dp", "seq")
    in_specs = (rows, rows, P("dp", None), P("dp"), rows) + (P(),) * 14
    out_specs = (rows,) * 3 + (P("dp"),) * 3 + (tile,) * 11 + (P(),)
    return jax.shard_map(local, mesh=mesh, in_specs=in_specs, out_specs=out_specs, check_vma=False)
```

```python
from functools import partial
from types import SimpleNamespace
from typing import Any, NamedTuple

import jax
import jax.numpy as jnp
from jax import lax
from jax.experimental import pallas as pl
from jax.experimental.pallas import tpu as pltpu
from jax.sharding import PartitionSpec as P

HEAD_DIM = 64
LANES = 128
PAIR = LANES // HEAD_DIM
NORM_EPS = 1e-06
NEG_FILL = -1e30
GELU_CURVE = 0.7978845608028654
F32 = jnp.float32
BF16 = jnp.bfloat16
MESH = pl.DeviceIdType.MESH
VMEM_LIMIT = 48 * 1024 * 1024
TAIL_VMEM = 63 * 1024 * 1024
HELD_BACK = 2


def dot_nn(a, b):
    return lax.dot_general(a, b, (((1,), (0,)), ((), ())), preferred_element_type=F32)


def dot_nt(a, b):
    return lax.dot_general(a, b, (((1,), (1,)), ((), ())), preferred_element_type=F32)


def dot_tn(a, b):
    return lax.dot_general(a, b, (((0,), (0,)), ((), ())), preferred_element_type=F32)


def head_mask(h, dtype):
    lane = lax.broadcasted_iota(jnp.int32, (1, LANES), 1)
    return ((lane // HEAD_DIM) == h).astype(F32).astype(dtype)


def causal_scores(raw, limit):
    key_pos = lax.broadcasted_iota(jnp.int32, raw.shape, 0)
    query_pos = lax.broadcasted_iota(jnp.int32, raw.shape, 1)
    return jnp.where((key_pos <= query_pos) & (key_pos < limit), raw, NEG_FILL)


def forward_pair(q, k, v, limit, causal):
    v_t = v.T
    mixes, norms = [], []
    for h in range(PAIR):
        q_h = q * (head_mask(h, BF16) * 0.125)
        scores = dot_nt(k, q_h)
        if causal:
            scores = causal_scores(scores, limit)
        elif limit is not None:
            key_pos = lax.broadcasted_iota(jnp.int32, scores.shape, 0)
            scores = jnp.where(key_pos < limit, scores, NEG_FILL)
        top = jnp.max(scores, axis=0, keepdims=True)
        exps = jnp.exp(scores - top)
        total = jnp.sum(exps, axis=0, keepdims=True)
        mixed = dot_nn(v_t[h * HEAD_DIM : (h + 1) * HEAD_DIM], exps.astype(BF16))
        mixes.append(mixed / total)
        norms.append(top + jnp.log(total))
    return jnp.concatenate(mixes, axis=0).T.astype(BF16), jnp.concatenate(norms, axis=0)


def backward_pair(q, k, v, grad_mix, norms, limit, causal):
    k_t = k.T * 0.125
    grad_q, grad_k, grad_v = [], 0.0, 0.0
    for h in range(PAIR):
        mask = head_mask(h, BF16)
        q_h = q * (mask * 0.125)
        scores = dot_nt(k, q_h)
        if causal:
            scores = causal_scores(scores, limit)
        elif limit is not None:
            key_pos = lax.broadcasted_iota(jnp.int32, scores.shape, 0)
            scores = jnp.where(key_pos < limit, scores, NEG_FILL)
        probs = jnp.exp(scores - norms[h : h + 1])
        grad_h = grad_mix * mask
        grad_v = grad_v + dot_nn(probs.astype(BF16), grad_h)
        grad_p = dot_nt(v, grad_h)
        inner = jnp.sum(probs * grad_p, axis=0, keepdims=True)
        grad_s = (probs * (grad_p - inner)).astype(BF16)
        grad_k = grad_k + dot_nn(grad_s, q_h)
        grad_q.append(dot_nn(k_t[h * HEAD_DIM : (h + 1) * HEAD_DIM], grad_s))
    grad_q = jnp.concatenate(grad_q, axis=0).T
    return grad_q.astype(BF16), grad_k.astype(BF16), grad_v.astype(BF16)


def self_forward_kernel(limit_ref, q_ref, k_ref, v_ref, mix_ref, norm_ref):
    limit = limit_ref[pl.program_id(0)]
    mix, norms = forward_pair(q_ref[...], k_ref[...], v_ref[...], limit, True)
    mix_ref[...] = mix
    norm_ref[0, 0, 0:PAIR] = norms


def self_backward_kernel(
    limit_ref, q_ref, k_ref, v_ref, grad_ref, norm_ref, dq_ref, dk_ref, dv_ref
):
    limit = limit_ref[pl.program_id(0)]
    dq, dk, dv = backward_pair(
        q_ref[...], k_ref[...], v_ref[...], grad_ref[...], norm_ref[0, 0, 0:PAIR], limit, True
    )
    dq_ref[...] = dq
    dk_ref[...] = dk
    dv_ref[...] = dv


def cross_forward_kernel(limit_ref, q_ref, k_ref, v_ref, mix_ref, norm_ref):
    limit = limit_ref[pl.program_id(0)]
    keys = k_ref.shape[0]
    short = keys // 4

    def run(count):
        mix, norms = forward_pair(q_ref[...], k_ref[0:count], v_ref[0:count], None, False)
        mix_ref[...] = mix
        norm_ref[0, 0, 0:PAIR] = norms

    pl.when(limit > short)(lambda: run(keys))
    pl.when(limit <= short)(lambda: run(short))


def cross_backward_kernel(
    limit_ref, q_ref, k_ref, v_ref, grad_ref, norm_ref, dq_ref, dk_ref, dv_ref
):
    limit = limit_ref[pl.program_id(0)]
    keys = k_ref.shape[0]
    short = keys // 4

    def run(count):
        dq, dk, dv = backward_pair(
            q_ref[...],
            k_ref[0:count],
            v_ref[0:count],
            grad_ref[...],
            norm_ref[0, 0, 0:PAIR],
            None,
            False,
        )
        dq_ref[...] = dq
        dk_ref[0:count] = dk
        dv_ref[0:count] = dv
        if count < keys:
            dk_ref[count:] = jnp.zeros((keys - count, LANES), BF16)
            dv_ref[count:] = jnp.zeros((keys - count, LANES), BF16)

    pl.when(limit > short)(lambda: run(keys))
    pl.when(limit <= short)(lambda: run(short))


def attend(kernel, limits, arrays, norms, examples, flops):
    width = arrays[0].shape[1]
    pairs = width // LANES
    queries = arrays[0].shape[0] // examples

    def rows_spec(array):
        return pl.BlockSpec((array.shape[0] // examples, LANES), lambda e, p: (e, p))

    norm_spec = pl.BlockSpec((1, 1, 8, queries), lambda e, p: (e, p, 0, 0))
    norm_shape = jax.ShapeDtypeStruct((examples, pairs, 8, queries), F32)
    in_specs = [pl.BlockSpec(memory_space=pltpu.SMEM)] + [rows_spec(a) for a in arrays]
    args = (limits,) + tuple(arrays)
    if norms is None:
        out_shape = (jax.ShapeDtypeStruct(arrays[0].shape, BF16), norm_shape)
        out_specs = (rows_spec(arrays[0]), norm_spec)
    else:
        in_specs.append(norm_spec)
        args = args + (norms,)
        out_shape = tuple(jax.ShapeDtypeStruct(a.shape, BF16) for a in arrays[:3])
        out_specs = tuple(rows_spec(a) for a in arrays[:3])
    return pl.pallas_call(
        kernel,
        grid=(examples, pairs),
        in_specs=in_specs,
        out_specs=out_specs,
        out_shape=out_shape,
        compiler_params=pltpu.CompilerParams(vmem_limit_bytes=VMEM_LIMIT),
        cost_estimate=pl.CostEstimate(
            flops=flops, bytes_accessed=sum(a.size * 2 for a in arrays), transcendentals=0
        ),
    )(*args)


class HeadState(NamedTuple):
    self_q: Any
    self_k: Any
    self_v: Any
    self_mix: Any
    normed_one: Any
    hidden: Any
    after_self: Any
    grad_after_cross: Any
    queries: Any
    normed_two: Any
    normed_three: Any
    grad_mlp: Any
    mlp_hidden: Any
    grad_gate: Any
    grad_up: Any
    self_norms: Any
    grad_mix: Any
    cross_norms: Any
    grad_k_early: Any
    grad_v_early: Any
    patch_early: Any
    k_late: Any
    v_late: Any
    patch_rows_late: Any
    layer_late: Any
    patch_grad_early: Any
    dw_c_out: Any


def head_kernel(*refs):
    lengths_ref, counts_ref, g_self_ref, g_cross_ref, g_mlp_ref = refs[:5]
    hidden_in, patches_in, cot_in = refs[5:8]
    weights_in = refs[8:19]
    refs = refs[19:]
    small, patch_out, layer_out = refs[:3]
    n_state = len(HeadState._fields)
    kept = HeadState(*refs[3 : 3 + n_state])
    (
        hidden,
        cot,
        patch,
        normed_one,
        self_rows,
        after_self,
        normed_two,
        queries,
        keys,
        values,
        cmix,
        normed_three,
        mlp_rows,
        grad_after,
        cbranch,
        grad_mix,
        patch_send,
        layer,
        after_cross,
        mlp_sum,
        grad_three,
        squares,
        w_gate,
        w_up,
        w_down,
        self_norms,
        cross_norms,
        weight_sem,
        in_send,
        in_recv,
        in_local,
        out_send,
        out_recv,
        out_local,
        keep_sem,
    ) = refs[3 + n_state :]
    own = 2
    rows, width = hidden.shape
    text = rows // own
    slots = patch.shape[0] // own
    part, patch_part = text // 4, slots // 4
    pairs = width // LANES
    dp = lax.axis_index("dp")
    seq = lax.axis_index("seq")
    near_seq = seq + 1 - 2 * (seq % 2)
    far_seq = seq + 2 - 4 * (seq // 2)
    seq_peers = [far_seq, near_seq, 3 - seq]
    lengths = [lengths_ref[own * seq + e] for e in range(own)]
    counts = [counts_ref[own * seq + e] for e in range(own)]

    barrier = pltpu.get_barrier_semaphore()
    for z in seq_peers:
        pl.semaphore_signal(barrier, inc=1, device_id=(dp, z), device_id_type=MESH)
    pl.semaphore_wait(barrier, len(seq_peers))

    incoming = {}

    def receive(number, src, dst, size, e):
        first = pl.multiple_of(e * 4 * size + seq * size, size)
        copies = []
        for k, z in enumerate(seq_peers):
            copy = pltpu.make_async_remote_copy(
                src_ref=src.at[own * z + e],
                dst_ref=dst.at[pl.ds(first, size)],
                send_sem=in_send.at[number, k],
                recv_sem=in_recv.at[number, k],
                device_id=(dp, z),
                device_id_type=MESH,
            )
            copy.start()
            copies.append(copy)
        local_copy = pltpu.make_async_copy(
            src.at[own * seq + e], dst.at[pl.ds(first, size)], in_local.at[number]
        )
        local_copy.start()
        incoming[number] = (copies, local_copy)

    def arrived(number):
        copies, local_copy = incoming[number]
        local_copy.wait()
        for copy in copies:
            copy.wait_recv()

    receive(0, hidden_in, hidden, part, 0)
    receive(1, hidden_in, hidden, part, 1)

    loads = []
    targets = [squares.at[i] for i in range(8)] + [w_gate, w_up, w_down]
    for i, (src, dst) in enumerate(zip(weights_in, targets)):
        copy = pltpu.make_async_copy(src, dst, weight_sem.at[i])
        copy.start()
        loads.append(copy)
    WQ, WK, WV, WO, CQ, CK, CV, CO = range(8)

    keeping = []

    def keep(dst, src):
        copy = pltpu.make_async_copy(src, dst, keep_sem.at[len(keeping)])
        copy.start()
        keeping.append(copy)

    small[...] = jnp.zeros(small.shape, F32)
    lane = lax.broadcasted_iota(jnp.int32, (1, width), 1)
    small[10:11] = jnp.where(
        lane == 0, lengths[0] + lengths[1], jnp.where(lane == 1, counts[0] + counts[1], 0)
    ).astype(F32)

    def add_row(i, value):
        small[i : i + 1, 0 : value.shape[1]] += value

    def valid_rows(e):
        position = lax.broadcasted_iota(jnp.int32, (text, 1), 0)
        return (position < lengths[e]).astype(F32)

    def squared(valid, value):
        return jnp.sum(valid * value * value, axis=0, keepdims=True)

    def norm(u, gain):
        r = lax.rsqrt(jnp.mean(u * u, axis=-1, keepdims=True) + NORM_EPS)
        return (u * r * gain).astype(BF16)

    arrived(0)
    arrived(1)
    receive(2, patches_in, patch, patch_part, 0)
    for i in (WQ, WK, WV):
        loads[i].wait()
    for e in range(own):
        at = slice(e * text, (e + 1) * text)
        normed_one[at] = norm(hidden[at].astype(F32), g_self_ref[...].reshape(1, width))
        for i in (WQ, WK, WV):
            self_rows[i, at] = dot_nn(normed_one[at], squares[i]).astype(BF16)

    def self_pair(step, carry):
        e, p = step // pairs, step % pairs
        at = pl.ds(pl.multiple_of(e * text, text), text)
        lanes = pl.ds(pl.multiple_of(p * LANES, LANES), LANES)
        limit = lengths_ref[own * seq + e]
        mix, norms = forward_pair(
            self_rows[0, at, lanes], self_rows[1, at, lanes], self_rows[2, at, lanes], limit, True
        )
        self_rows[3, at, lanes] = mix
        self_norms[e, p, 0:PAIR] = norms
        return carry

    lax.fori_loop(0, own * pairs, self_pair, 0)
    loads[WO].wait()
    loads[CQ].wait()
    for e in range(own):
        at = slice(e * text, (e + 1) * text)
        branch = dot_nn(self_rows[3, at], squares[WO])
        add_row(4, squared(valid_rows(e), branch))
        after = hidden[at].astype(F32) + branch
        after_self[at] = after
        normed_two[at] = norm(after, g_cross_ref[...].reshape(1, width))
        queries[at] = dot_nn(normed_two[at], squares[CQ]).astype(BF16)
    for i, dst in enumerate((kept.self_q, kept.self_k, kept.self_v, kept.self_mix)):
        keep(dst, self_rows.at[i])
    keep(kept.normed_one, normed_one)
    keep(kept.hidden, hidden)
    keep(kept.after_self, after_self)
    keep(kept.self_norms, self_norms)

    def project_patches(e):
        def body(i, carry):
            at = pl.ds(pl.multiple_of(e * slots + i * patch_part, patch_part), patch_part)
            keys[at] = dot_nn(patch[at], squares[CK]).astype(BF16)
            values[at] = dot_nn(patch[at], squares[CV]).astype(BF16)
            return carry

        lax.fori_loop(0, 4, body, 0)

    def cross_forward(e):
        at, key_at = slice(e * text, (e + 1) * text), slice(e * slots, (e + 1) * slots)

        def body(p, carry):
            lanes = pl.ds(pl.multiple_of(p * LANES, LANES), LANES)
            mix, norms = forward_pair(
                queries[at, lanes], keys[key_at, lanes], values[key_at, lanes], counts[e], False
            )
            cmix[at, lanes] = mix
            cross_norms[e, p, 0:PAIR] = norms
            return carry

        lax.fori_loop(0, pairs, body, 0)

    def feed_forward(e):
        at = slice(e * text, (e + 1) * text)
        valid = valid_rows(e)
        branch = dot_nn(cmix[at], squares[CO])
        add_row(5, squared(valid, branch))
        after = after_self[at] + branch
        after_cross[...] = after
        normed_three[at] = norm(after, g_mlp_ref[...].reshape(1, width))
        arrived(4 + e)
        cot[at] = (cot[at].astype(F32) * valid).astype(BF16)
        mlp_sum[...] = jnp.zeros((text, width), F32)
        grad_three[...] = jnp.zeros((text, width), F32)
        step = w_gate.shape[1] // 4

        def body(i, total):
            columns = pl.ds(pl.multiple_of(i * step, step), step)
            gate = dot_nn(normed_three[at], w_gate[:, columns])
            up = dot_nn(normed_three[at], w_up[:, columns])
            tanh_part = jnp.tanh(GELU_CURVE * (gate + 0.044715 * gate * gate * gate))
            gelu = 0.5 * gate * (1.0 + tanh_part)
            slope = 0.5 * (1.0 + tanh_part) + 0.5 * gate * (1.0 - tanh_part * tanh_part) * (
                GELU_CURVE * (1.0 + 3.0 * 0.044715 * gate * gate)
            )
            value = gelu * up
            low_value = value.astype(BF16)
            mlp_rows[0, at, columns] = low_value
            mlp_sum[...] += dot_nn(low_value, w_down[columns, :])
            grad_value = dot_nt(cot[at], w_down[columns, :])
            grad_gate = (grad_value * up * slope).astype(BF16)
            grad_up = (grad_value * gelu).astype(BF16)
            mlp_rows[1, at, columns] = grad_gate
            mlp_rows[2, at, columns] = grad_up
            grad_three[...] += dot_nt(grad_gate, w_gate[:, columns]) + dot_nt(
                grad_up, w_up[:, columns]
            )
            return total + squared(valid, value)

        add_row(7, lax.fori_loop(0, 4, body, jnp.zeros((1, step), F32)))
        mlp_branch = mlp_sum[...]
        add_row(6, squared(valid, mlp_branch))
        after = after_cross[...]
        out = after + mlp_branch
        add_row(3, squared(valid, out))
        layer[at] = out.astype(BF16)
        w = grad_three[...]
        r = lax.rsqrt(jnp.mean(after * after, axis=-1, keepdims=True) + NORM_EPS)
        gw = g_mlp_ref[...].reshape(1, width) * w
        add_row(2, jnp.sum(w * after * r, axis=0, keepdims=True))
        grad = r * gw - after * (r * r * r) * jnp.mean(gw * after, axis=-1, keepdims=True)
        grad = cot[at].astype(F32) + grad
        grad_after[at] = grad
        cbranch[at] = grad.astype(BF16)
        grad_mix[at] = dot_nt(cbranch[at], squares[CO]).astype(BF16)

    def cross_backward(e):
        at, key_at = slice(e * text, (e + 1) * text), slice(e * slots, (e + 1) * slots)

        def body(p, carry):
            lanes = pl.ds(pl.multiple_of(p * LANES, LANES), LANES)
            dq, dk, dv = backward_pair(
                queries[at, lanes],
                keys[key_at, lanes],
                values[key_at, lanes],
                grad_mix[at, lanes],
                cross_norms[e, p, 0:PAIR],
                counts[e],
                False,
            )
            queries[at, lanes] = dq
            keys[key_at, lanes] = dk
            values[key_at, lanes] = dv
            return carry

        lax.fori_loop(0, pairs, body, 0)

    def patch_grads(e):
        def body(d, total):
            first = pl.multiple_of(d * patch_part, patch_part)
            at = pl.ds(e * slots + first, patch_part)
            value = dot_nt(keys[at], squares[CK]) + dot_nt(values[at], squares[CV])
            position = lax.broadcasted_iota(jnp.int32, (patch_part, 1), 0) + first
            patch_send[d] = value.astype(BF16)
            return total + squared((position < counts[e]).astype(F32), value)

        add_row(9, lax.fori_loop(0, 4, body, jnp.zeros((1, width), F32)))

    outgoing = []

    def send_rows(src_of, dst, number):
        for k, z in enumerate(seq_peers):
            copy = pltpu.make_async_remote_copy(
                src_ref=src_of(z),
                dst_ref=dst.at[seq],
                send_sem=out_send.at[number, k],
                recv_sem=out_recv.at[number, k],
                device_id=(dp, z),
                device_id_type=MESH,
            )
            copy.start()
            outgoing.append(copy)
        local_copy = pltpu.make_async_copy(src_of(seq), dst.at[seq], out_local.at[number])
        local_copy.start()
        keeping.append(local_copy)

    arrived(2)
    receive(4, cot_in, cot, part, 0)
    receive(3, patches_in, patch, patch_part, 1)
    for copy in loads[CK:]:
        copy.wait()
    project_patches(0)
    cross_forward(0)
    feed_forward(0)
    send_rows(lambda z: layer.at[pl.ds(pl.multiple_of(z * part, part), part)], layer_out, 0)
    cross_backward(0)
    receive(5, cot_in, cot, part, 1)
    patch_grads(0)
    split = patch_part - patch_part // HELD_BACK
    send_rows(lambda z: patch_send.at[z, 0:split], patch_out, 1)
    keep(kept.patch_grad_early, patch_send.at[:, split:patch_part])
    keep(kept.grad_k_early, keys.at[0:slots])
    keep(kept.grad_v_early, values.at[0:slots])
    keep(kept.patch_early, patch.at[0:slots])
    keep(kept.normed_two, normed_two)
    arrived(3)
    project_patches(1)
    keep(kept.k_late, keys.at[slots : 2 * slots])
    keep(kept.v_late, values.at[slots : 2 * slots])
    keep(kept.patch_rows_late, patch.at[slots : 2 * slots])
    cross_forward(1)
    keep(kept.queries, queries)
    keep(kept.cross_norms, cross_norms.at[1])
    feed_forward(1)
    keep(kept.grad_mlp, cot)
    keep(kept.normed_three, normed_three)
    for i, dst in enumerate((kept.mlp_hidden, kept.grad_gate, kept.grad_up)):
        keep(dst, mlp_rows.at[i])
    keep(kept.grad_after_cross, grad_after)
    keep(kept.layer_late, layer.at[text : 2 * text])
    keep(kept.grad_mix, grad_mix.at[text : 2 * text])

    for i in range(2):
        columns = slice(i * (width // 2), (i + 1) * (width // 2))
        squares[0, columns] = dot_tn(cmix[:, columns], cbranch[...]).astype(BF16)
    keep(kept.dw_c_out, squares.at[0])
    for copies, local_copy in incoming.values():
        for copy in copies:
            copy.wait_send()
    for copy in outgoing:
        copy.wait()
    for copy in keeping:
        copy.wait()


def forward_head(lengths, counts, gains, rows, weights):
    examples, part, width = rows[0].shape
    patch_part = rows[1].shape[1]
    own = examples // 4
    text, slots = 4 * part, 4 * patch_part
    count, key_count = own * text, own * slots
    ff_width = weights[8].shape[1]
    pairs = width // LANES
    norms = (own, pairs, 8, text)
    vmem = pl.BlockSpec(memory_space=pltpu.VMEM)
    anywhere = pl.BlockSpec(memory_space=pl.ANY)
    smem = pl.BlockSpec(memory_space=pltpu.SMEM)
    rows_low = jax.ShapeDtypeStruct((count, width), BF16)
    rows_wide = jax.ShapeDtypeStruct((count, width), F32)
    rows_ff = jax.ShapeDtypeStruct((count, ff_width), BF16)
    keys_low = jax.ShapeDtypeStruct((slots, width), BF16)
    late_low = jax.ShapeDtypeStruct((text, width), BF16)
    state = HeadState(*[rows_low] * len(HeadState._fields))._replace(
        after_self=rows_wide,
        grad_after_cross=rows_wide,
        mlp_hidden=rows_ff,
        grad_gate=rows_ff,
        grad_up=rows_ff,
        self_norms=jax.ShapeDtypeStruct(norms, F32),
        cross_norms=jax.ShapeDtypeStruct(norms[1:], F32),
        grad_k_early=keys_low,
        grad_v_early=keys_low,
        patch_early=keys_low,
        k_late=keys_low,
        v_late=keys_low,
        patch_rows_late=keys_low,
        grad_mix=late_low,
        layer_late=late_low,
        dw_c_out=jax.ShapeDtypeStruct((width, width), BF16),
        patch_grad_early=jax.ShapeDtypeStruct((4, patch_part // HELD_BACK, width), BF16),
    )

    def low(*shape):
        return pltpu.VMEM(shape, BF16)

    def wide(*shape):
        return pltpu.VMEM(shape, F32)

    outs = pl.pallas_call(
        head_kernel,
        out_shape=(
            jax.ShapeDtypeStruct((16, width), F32),
            jax.ShapeDtypeStruct((4, patch_part - patch_part // HELD_BACK, width), BF16),
            jax.ShapeDtypeStruct((4, part, width), BF16),
            *state,
        ),
        in_specs=[smem] * 2 + [vmem] * 3 + [anywhere] * 14,
        out_specs=(vmem,) + (anywhere,) * (2 + len(state)),
        scratch_shapes=[
            low(count, width),
            low(count, width),
            low(key_count, width),
            low(count, width),
            low(4, count, width),
            wide(count, width),
            low(count, width),
            low(count, width),
            low(key_count, width),
            low(key_count, width),
            low(count, width),
            low(count, width),
            low(3, count, ff_width),
            wide(count, width),
            low(count, width),
            low(count, width),
            low(4, patch_part, width),
            low(count, width),
            wide(text, width),
            wide(text, width),
            wide(text, width),
            low(8, width, width),
            low(width, ff_width),
            low(width, ff_width),
            low(ff_width, width),
            wide(*norms),
            wide(*norms),
            pltpu.SemaphoreType.DMA((11,)),
            pltpu.SemaphoreType.DMA((6, 3)),
            pltpu.SemaphoreType.DMA((6, 3)),
            pltpu.SemaphoreType.DMA((6,)),
            pltpu.SemaphoreType.DMA((2, 3)),
            pltpu.SemaphoreType.DMA((2, 3)),
            pltpu.SemaphoreType.DMA((2,)),
            pltpu.SemaphoreType.DMA((len(state) + 2,)),
        ],
        compiler_params=pltpu.CompilerParams(
            collective_id=1, has_side_effects=True, vmem_limit_bytes=TAIL_VMEM
        ),
    )(lengths, counts, *gains, *rows, *weights)
    return outs[0], outs[1], outs[2], HeadState(*outs[3:])


(
    GATE,
    UP,
    DOWN,
    CROSS_A,
    CROSS_B,
    PATCHES,
    KEYS,
    C_QUERY,
    C_KEY,
    C_VALUE,
    LOADS,
    MIDDLE,
    W_OUT,
    SELF_A,
    SELF_B,
    LAST,
    W_QUERY,
    W_KEY,
    W_VALUE,
) = range(19)
CORE, GO, TWO, THREE, NEAR, FAR, SMALL = range(7)
TAIL_ORDER = (
    DOWN, GATE, (CORE, 3), UP, (GO, 3), (CORE, 2), (GO, 2), CROSS_A, (CORE, 0), (GO, 0), CROSS_B,
    C_QUERY, LOADS, (CORE, 1), (GO, 1), MIDDLE, (CORE, 4), (GO, 4), PATCHES, SELF_A, (TWO, 2), SELF_B,
    (TWO, 3), (TWO, 4), (TWO, 0), W_QUERY, W_KEY, W_VALUE, (TWO, 1), KEYS, W_OUT, (CORE, 8), (THREE, 1),
    (CORE, 10), (CORE, 7), (GO, 7), (GO, 8), C_KEY, (GO, 10), (THREE, 2), C_VALUE, (CORE, 9), (NEAR, 1),
    (CORE, 5), (GO, 9), (GO, 5), (THREE, 0), (NEAR, 2), (CORE, 6), (GO, 6), LAST, (TWO, 8), (TWO, 7),
    (TWO, 9), (SMALL, 0), (NEAR, 0), (TWO, 10), (TWO, 6), (SMALL, 1), (TWO, 5), (THREE, 4), (THREE, 5),
    (SMALL, 2), (THREE, 3), (NEAR, 4), (NEAR, 5), (SMALL, 3), (FAR, 0), (NEAR, 3), (FAR, 1), (FAR, 4),
    (FAR, 5), (FAR, 2), (FAR, 3), (SMALL, 4),
)
Y_FIRST = (1, 2, 6, 8, 9)


def tail_kernel(lengths_ref, counts_ref, g_self_ref, g_cross_ref, small_in, *refs):
    n_state = len(HeadState._fields)
    hbm = HeadState(*refs[:n_state])
    c_key, c_value, c_query, w_out, w_query, w_key, w_value = refs[n_state : n_state + 7]
    refs = refs[n_state + 7 :]
    narrow, wide, small_out, early_out, patch_out, x_out, layer_out = refs[:7]
    (
        after_self,
        grad_after,
        queries,
        normed,
        normed_two,
        mlp_rows,
        grad_mlp,
        big,
        grad_mix,
        cross_norms,
        self_norms,
        weights,
        wide_units,
        tall_units,
        wide_core,
        tall_core,
        wide_two,
        tall_two,
        wide_three,
        tall_three,
        square,
        square_core,
        square_two,
        square_three,
        cut_narrow,
        near_narrow,
        far_narrow,
        cut_wide,
        near_wide,
        far_wide,
        small_own,
        small_got,
        load_sem,
        send_sem,
        recv_sem,
        small_send,
        small_recv,
        cut_send,
        cut_recv,
        out_send,
        out_recv,
        out_local,
    ) = refs[7:]
    width = queries.shape[1]
    block = width // 8
    text = self_norms.shape[3]
    own = 2
    pairs = width // LANES
    part = text // 4

    dp = lax.axis_index("dp")
    seq = lax.axis_index("seq")
    core, x, y = dp % 2, (dp // 2) % 2, dp // 4
    low, high = seq % 2, seq // 2
    to_core = (dp + 1 - 2 * core, seq)
    to_x = (dp + 2 - 4 * x, seq)
    to_y = (dp + 4 - 8 * y, seq)
    near_seq = seq + 1 - 2 * low
    far_seq = seq + 2 - 4 * high
    last_seq = 3 - seq
    seq_peers = [near_seq, far_seq, last_seq]
    to_near, to_far = (dp, near_seq), (dp, far_seq)
    peers = [to_core, to_x, to_y, to_near, to_far, (dp, last_seq)]

    got, waited = SimpleNamespace(count=0), set()

    def need(*copies):
        for copy in copies:
            if id(copy) not in waited:
                copy.wait()
                waited.add(id(copy))

    def load(src, dst):
        copy = pltpu.make_async_copy(src, dst, load_sem.at[got.count])
        copy.start()
        got.count += 1
        return copy

    slots = big.shape[0] // 4
    patch_part = slots // 4
    keys, values, patch, patch_send = (big.at[i * slots : (i + 1) * slots] for i in range(4))
    self_q, self_k, self_v, self_mix, hidden, sbranch = (
        mlp_rows.at[i // 2, :, i % 2 * width : (i % 2 + 1) * width] for i in range(6)
    )
    grad_smix = normed_two
    got.dw_c_out = load(hbm.dw_c_out.at[:, :, core], square.at[0])
    got.normed = load(hbm.normed_three, normed)
    got.grad_gate = load(hbm.grad_gate, mlp_rows.at[1])
    got.grad_up = load(hbm.grad_up, mlp_rows.at[2])
    got.queries = load(hbm.queries, queries)
    got.keys = load(hbm.k_late, keys)
    got.values = load(hbm.v_late, values)
    got.grad_mix = load(hbm.grad_mix, grad_mix)
    got.cross_norms = load(hbm.cross_norms, cross_norms)
    got.c_key = load(c_key, weights.at[0])
    got.c_value = load(c_value, weights.at[1])
    got.patch = load(hbm.patch_rows_late, patch)
    got.normed_two = load(hbm.normed_two, normed_two)
    got.mlp_hidden = load(hbm.mlp_hidden, mlp_rows.at[0])
    got.grad_mlp = load(hbm.grad_mlp, grad_mlp)
    got.after_self = load(hbm.after_self, after_self)
    got.grad_after = load(hbm.grad_after_cross, grad_after)
    got.c_query = load(c_query, weights.at[2])
    got.w_out = load(w_out, weights.at[3])
    got.self_norms = load(hbm.self_norms, self_norms)

    small_own[0] = small_in[...]

    def add_row(i, value):
        small_own[0, i : i + 1] += value

    barrier = pltpu.get_barrier_semaphore()
    for peer in peers:
        pl.semaphore_signal(barrier, inc=1, device_id=peer, device_id_type=MESH)
    pl.semaphore_wait(barrier, len(peers))

    def remote(src, dst, send, recv, device):
        copy = pltpu.make_async_remote_copy(
            src_ref=src,
            dst_ref=dst,
            send_sem=send,
            recv_sem=recv,
            device_id=device,
            device_id_type=MESH,
        )
        copy.start()
        return copy

    n_square = square_core.shape[0]
    y_first = Y_FIRST
    first, second, third, near, far, small = {}, {}, {}, {}, {}, {}
    got_core = [wide_core.at[0], wide_core.at[1], tall_core]
    got_core += [square_core.at[i] for i in range(n_square)]
    got_two = [wide_two.at[0], wide_two.at[1], tall_two]
    got_two += [square_two.at[i] for i in range(n_square)]
    got_three = [wide_three.at[0], wide_three.at[1], tall_three]
    got_three += [square_three.at[i] for i in range(n_square)]
    current = [wide_units.at[0], wide_units.at[1], tall_units.at[0]]
    current += [square.at[i] for i in range(n_square)]
    first[3] = remote(
        hbm.dw_c_out.at[:, :, 1 - core],
        got_core[3],
        send_sem.at[0, 3],
        recv_sem.at[0, 3],
        to_core,
    )

    def add(out, got):
        rows = out.shape[0]
        step = 32

        def body(i, carry):
            at = pl.ds(pl.multiple_of(i * step, step), step)
            out[at, :] = (out[at, :].astype(F32) + got[at, :].astype(F32)).astype(BF16)
            return carry

        lax.fori_loop(0, rows // step, body, 0)

    def over_core(u):
        if u == 3:
            need(got.dw_c_out)
        first[u].wait_recv()
        for i in range(2):
            for j in range(2):
                add(current[u].at[i, j], got_core[u].at[i, j])

    def leave_two(u):
        cur = current[u]
        src, device = (cur.at[1 - y], to_y) if u in y_first else (cur.at[:, 1 - x], to_x)
        second[u] = remote(src, got_two[u], send_sem.at[1, u], recv_sem.at[1, u], device)

    def over_two(u):
        second[u].wait_recv()
        cur = current[u]
        for i in range(2):
            add(cur.at[y, i] if u in y_first else cur.at[i, x], got_two[u].at[i])
        src, device = (cur.at[y, 1 - x], to_x) if u in y_first else (cur.at[1 - y, x], to_y)
        third[u] = remote(src, got_three[u], send_sem.at[2, u], recv_sem.at[2, u], device)

    groups = [(1, 0, block, (0, 1)), (0, n_square // 2 * block, tall_three.shape[0] // 2, (2,))]
    groups += [(0, i * block, block, (3 + 2 * i, 4 + 2 * i)) for i in range(n_square // 2)]
    cut, got_near, got_far = (cut_narrow, cut_wide), (near_narrow, near_wide), (far_narrow, far_wide)
    totals = (narrow, wide)

    def over_three(g):
        buffer, row, rows, members = groups[g]
        for u in members:
            third[u].wait_recv()
        halves = [current[u][y, x].astype(F32) + got_three[u][...].astype(F32) for u in members]
        if len(members) == 1:
            halves = [halves[0][:rows], halves[0][rows:]]
        piece = halves[0].shape[1] // 4
        at = pl.ds(row, rows)
        for z in range(4):
            columns = [h[:, z * piece : (z + 1) * piece] for h in halves]
            cut[buffer][z // 2, z % 2, at] = jnp.concatenate(columns, axis=1).astype(BF16)
        near[g] = remote(
            cut[buffer].at[:, 1 - low, at],
            got_near[buffer].at[:, at],
            cut_send.at[0, g],
            cut_recv.at[0, g],
            to_near,
        )

    def over_near(g):
        buffer, row, rows, _ = groups[g]
        near[g].wait_recv()
        at = pl.ds(row, rows)
        for i in range(2):
            add(cut[buffer].at[i, low, at], got_near[buffer].at[i, at])
        far[g] = remote(
            cut[buffer].at[1 - high, low, at],
            got_far[buffer].at[at],
            cut_send.at[1, g],
            cut_recv.at[1, g],
            to_far,
        )

    def over_far(g):
        buffer, row, rows, _ = groups[g]
        far[g].wait_recv()
        at = pl.ds(row, rows)
        totals[buffer][at] = cut[buffer][high, low, at].astype(F32) + got_far[buffer][at].astype(F32)

    def give(u, src):
        first[u] = remote(src, got_core[u], send_sem.at[0, u], recv_sem.at[0, u], to_core)

    def weight_grad(i, rows, grad_rows, more=None):
        ring = n_square + len(ring_units) % 2
        if len(ring_units) >= 2:
            first[ring_units[-2]].wait_send()
            first_sent.add(ring_units[-2])
        ring_units.append(3 + i)
        half = width // 2
        for h in range(2):
            value = dot_tn(rows[:, h * half : (h + 1) * half], grad_rows[...])
            if more is not None:
                value = value + more[h * half : (h + 1) * half].astype(F32)
            value = value.astype(BF16)
            for j in range(4):
                at = i + ((j + core) % 2) * (ring - i)
                square[at, h, j // 2] = value[j * block : (j + 1) * block]
        give(3 + i, square.at[ring])

    def wide_grad(u):
        if u == 1:
            first[0].wait_send()
            first_sent.add(0)
        half, step = width // 2, wide_units.shape[4] // 4

        def body(i, carry):
            columns = pl.ds(pl.multiple_of(i * step, step), step)
            for h in range(2):
                value = dot_tn(
                    normed[:, h * half : (h + 1) * half], mlp_rows[1 + u, :, columns]
                ).astype(BF16)
                for j in range(4):
                    at = u + ((j + core) % 2) * (2 - u)
                    wide_units[at, h, j // 2, :, columns] = value[j * block : (j + 1) * block]
            return carry

        lax.fori_loop(0, 4, body, 0)
        give(u, wide_units.at[2])

    def tall_grad():
        rows = tall_units.shape[3]

        def body(j, carry):
            columns = pl.ds(pl.multiple_of(j * rows, rows), rows)
            value = dot_tn(mlp_rows[0, :, columns], grad_mlp[...]).astype(BF16)
            tall_units[(j + core) % 2, j // 4, (j // 2) % 2] = value
            return carry

        lax.fori_loop(0, 8, body, 0)
        give(2, tall_units.at[1])

    first_sent, ring_units = set(), []

    outs, locals_ = [], []

    def send_rows(src_of, dst, number):
        for k, z in enumerate([far_seq, near_seq, last_seq]):
            outs.append(
                remote(src_of(z), dst, out_send.at[number, k], out_recv.at[number, k], (dp, z))
            )
        copy = pltpu.make_async_copy(src_of(seq), dst, out_local.at[number])
        copy.start()
        locals_.append(copy)

    send_rows(
        lambda z: hbm.layer_late.at[pl.ds(pl.multiple_of(z * part, part), part)],
        layer_out.at[seq],
        1,
    )
    send_rows(lambda z: hbm.patch_grad_early.at[z], early_out.at[seq], 3)
    chunk = own * text // 4
    late = slice(text, 2 * text)
    limit = counts_ref[own * seq + 1]

    def cross_pairs(first_pair, last_pair):
        def body(p, carry):
            lanes = pl.ds(pl.multiple_of(p * LANES, LANES), LANES)
            dq, dk, dv = backward_pair(
                queries[late, lanes],
                keys[:, lanes],
                values[:, lanes],
                grad_mix[:, lanes],
                cross_norms[p, 0:PAIR],
                limit,
                False,
            )
            queries[late, lanes] = dq
            keys[:, lanes] = dk
            values[:, lanes] = dv
            return carry

        lax.fori_loop(first_pair, last_pair, body, 0)

    def patch_grads():
        def body(d, total):
            at = pl.ds(pl.multiple_of(d * patch_part, patch_part), patch_part)
            value = dot_nt(keys[at, :], weights[0]) + dot_nt(values[at, :], weights[1])
            position = lax.broadcasted_iota(jnp.int32, (patch_part, 1), 0) + d * patch_part
            patch_send[at, :] = value.astype(BF16)
            valid = (position < limit).astype(F32)
            return total + jnp.sum(valid * value * value, axis=0, keepdims=True)

        add_row(9, lax.fori_loop(0, 4, body, jnp.zeros((1, width), F32)))
        send_rows(
            lambda z: patch_send.at[pl.ds(pl.multiple_of(z * patch_part, patch_part), patch_part)],
            patch_out.at[seq],
            0,
        )

    def gate_weight():
        need(got.normed, got.grad_gate)
        wide_grad(0)

    def up_weight():
        need(got.normed, got.grad_up)
        wide_grad(1)
        got.normed_one = load(hbm.normed_one, normed)

    def down_weight():
        need(got.mlp_hidden, got.grad_mlp)
        tall_grad()

    def cross_some(first_pair, last_pair):
        need(got.queries, got.keys, got.values, got.grad_mix, got.cross_norms)
        cross_pairs(first_pair, last_pair)

    def late_patches():
        need(got.c_key, got.c_value)
        patch_grads()

    def late_keys():
        need(got.patch)
        half = width // 2
        for slot, right in ((0, keys), (1, values)):
            for h in range(2):
                columns = slice(h * half, (h + 1) * half)
                weights[slot, columns] = dot_tn(patch[:, columns], right[...]).astype(BF16)
        got.grad_k = load(hbm.grad_k_early, keys)
        got.grad_v = load(hbm.grad_v_early, values)
        got.patch_early = load(hbm.patch_early, patch)

    def query_weight():
        need(got.normed_two)
        weight_grad(1, normed_two, queries)

    def key_weight():
        need(got.grad_k, got.patch_early)
        weight_grad(2, patch, keys, weights.at[0])

    def value_weight():
        need(got.grad_v, got.patch_early)
        weight_grad(3, patch, values, weights.at[1])
        got.w_query = load(w_query, weights.at[0])
        got.w_key = load(w_key, weights.at[1])

    def self_loads():
        got.self_q = load(hbm.self_q, self_q)
        got.self_k = load(hbm.self_k, self_k)
        got.self_v = load(hbm.self_v, self_v)
        got.self_mix = load(hbm.self_mix, self_mix)
        got.hidden = load(hbm.hidden, hidden)

    def out_weight():
        need(got.self_mix)
        weight_grad(4, self_mix, sbranch)

    def self_weight(i, rows):
        need(got.normed_one)
        weight_grad(i, normed, rows)

    def norm_grad(u, gain, w):
        r = lax.rsqrt(jnp.mean(u * u, axis=-1, keepdims=True) + NORM_EPS)
        gw = gain * w
        grad = r * gw - u * (r * r * r) * jnp.mean(gw * u, axis=-1, keepdims=True)
        return grad, jnp.sum(w * u * r, axis=0, keepdims=True)

    def middle(i, total):
        at = pl.ds(pl.multiple_of(i * chunk, chunk), chunk)
        w = dot_nt(queries[at, :], weights[2])
        grad, row = norm_grad(after_self[at, :], g_cross_ref[...].reshape(1, width), w)
        grad = grad_after[at, :] + grad
        grad_after[at, :] = grad
        low_grad = grad.astype(BF16)
        sbranch[at, :] = low_grad
        grad_smix[at, :] = dot_nt(low_grad, weights[3]).astype(BF16)
        return total + row

    def self_inputs():
        need(got.after_self, got.grad_after, got.c_query, got.w_out)
        add_row(1, lax.fori_loop(0, 4, middle, jnp.zeros((1, width), F32)))
        got.w_value = load(w_value, weights.at[2])

    def self_pairs(first_step, last_step):
        def body(i, carry):
            e, p = i // pairs, i % pairs
            rows = pl.ds(pl.multiple_of(e * text, text), text)
            lanes = pl.ds(pl.multiple_of(p * LANES, LANES), LANES)
            dq, dk, dv = backward_pair(
                self_q[rows, lanes],
                self_k[rows, lanes],
                self_v[rows, lanes],
                grad_smix[rows, lanes],
                self_norms[e, p, 0:PAIR],
                lengths_ref[own * seq + e],
                True,
            )
            self_q[rows, lanes] = dq
            self_k[rows, lanes] = dk
            self_v[rows, lanes] = dv
            return carry

        lax.fori_loop(first_step, last_step, body, 0)

    def self_some(first_step, last_step):
        need(got.self_q, got.self_k, got.self_v, got.self_norms)
        self_pairs(first_step, last_step)

    def last(i, carry):
        total, squares = carry
        at = pl.ds(pl.multiple_of(i * chunk, chunk), chunk)
        w = (
            dot_nt(self_q[at, :], weights[0])
            + dot_nt(self_k[at, :], weights[1])
            + dot_nt(self_v[at, :], weights[2])
        )
        grad, row = norm_grad(hidden[at, :].astype(F32), g_self_ref[...].reshape(1, width), w)
        grad = grad_after[at, :] + grad
        e, half = i // 2, i % 2
        position = lax.broadcasted_iota(jnp.int32, (chunk, 1), 0) + half * chunk
        valid = (position < lengths_ref[own * seq + e]).astype(F32)
        low_grad = grad.astype(BF16)
        for k in range(2):
            place = (2 * half + k) * own + e
            grad_mlp[pl.ds(pl.multiple_of(place * part, part), part)] = low_grad[
                k * part : (k + 1) * part
            ]
        return total + row, squares + jnp.sum(valid * grad * grad, axis=0, keepdims=True)

    def inputs_grad():
        need(got.w_query, got.w_key, got.w_value, got.hidden)
        zero = jnp.zeros((1, width), F32)
        total, squares = lax.fori_loop(0, 4, last, (zero, zero))
        add_row(0, total)
        add_row(8, squares)
        leaving = own * part
        send_rows(
            lambda z: grad_mlp.at[pl.ds(pl.multiple_of(z * leaving, leaving), leaving)],
            x_out.at[seq],
            2,
        )
        send_small(0)

    def send_small(i):
        small[i] = remote(
            small_own.at[i], small_got.at[i], small_send.at[i], small_recv.at[i], peers[i]
        )

    def add_small(i):
        small[i].wait_recv()
        small_own[i + 1] = small_own[i] + small_got[i]

    def pass_small(i):
        add_small(i)
        if i < 4:
            send_small(i + 1)

    work = {
        GATE: gate_weight,
        UP: up_weight,
        DOWN: down_weight,
        CROSS_A: lambda: cross_some(0, pairs // 2),
        CROSS_B: lambda: cross_some(pairs // 2, pairs),
        PATCHES: late_patches,
        KEYS: late_keys,
        C_QUERY: query_weight,
        C_KEY: key_weight,
        C_VALUE: value_weight,
        LOADS: self_loads,
        MIDDLE: self_inputs,
        W_OUT: out_weight,
        SELF_A: lambda: self_some(0, pairs),
        SELF_B: lambda: self_some(pairs, 2 * pairs),
        LAST: inputs_grad,
        W_QUERY: lambda: self_weight(5, self_q),
        W_KEY: lambda: self_weight(6, self_k),
        W_VALUE: lambda: self_weight(7, self_v),
    }
    exchange = {
        CORE: over_core,
        GO: leave_two,
        TWO: over_two,
        THREE: over_three,
        NEAR: over_near,
        FAR: over_far,
        SMALL: pass_small,
    }
    for step in TAIL_ORDER:
        if isinstance(step, tuple):
            exchange[step[0]](step[1])
        else:
            work[step]()
    small_out[...] = small_own[5]
    for copy in outs:
        copy.wait_recv()
    for copy in locals_:
        copy.wait()
    for u, copy in first.items():
        if u not in first_sent:
            copy.wait_send()
    for copies in (second, third, near, far, small):
        for copy in copies.values():
            copy.wait_send()
    for copy in outs:
        copy.wait_send()


def finish_kernel(groups, ff_width, *refs):
    narrow_ref, wide_ref, small_ref, patch_first, patch_rest, patch_late = refs[:6]
    layer_early, layer_late, x_in = refs[6:9]
    layer_out, x_out, patch_out, gain_self, gain_cross, gain_mlp, rms_out = refs[9:16]
    out_refs = refs[16:]
    step = pl.program_id(0)
    split = patch_first.shape[1]
    x_out[...] = x_in[...].astype(F32)
    patch_out[0, :split] = patch_first[0].astype(F32)
    patch_out[0, split:] = patch_rest[0].astype(F32)
    patch_out[1] = patch_late[0].astype(F32)
    layer_out[0] = layer_early[0].astype(F32)
    layer_out[1] = layer_late[0].astype(F32)

    @pl.when(step == 0)
    def sums():
        for buffer, row, rows, members in groups:
            total = (narrow_ref, wide_ref)[buffer][row : row + rows]
            part = total.shape[1] // 2
            if len(members) == 2:
                out_refs[members[0]][...] = total[:, :part]
                out_refs[members[1]][...] = total[:, part:]
            else:
                out_refs[members[0]][0:rows] = total[:, :part]
                out_refs[members[0]][rows:] = total[:, part:]
        small = small_ref[...]
        width = small.shape[1]
        piece = width // 8
        for i, gain in enumerate((gain_self, gain_cross, gain_mlp)):
            for d in range(8):
                value = small[i : i + 1, d * piece : (d + 1) * piece]
                pl.when(lax.axis_index("dp") == d)(partial(store, gain, value))
        squares = jnp.sum(small, axis=1, keepdims=True)
        row = lax.broadcasted_iota(jnp.int32, squares.shape, 0)
        texts, patch_count = small[10:11, 0:1], small[10:11, 1:2]
        count = jnp.where(
            row == 9, patch_count * width, jnp.where(row == 7, texts * ff_width, texts * width)
        )
        rms_out[...] = jnp.sqrt(squares / count)


def store(ref, value):
    ref[...] = value


def takes_kernel(width, n_dp, n_seq, own):
    return (
        n_dp == 8
        and n_seq == 4
        and own == 2
        and width // n_dp % 32 == 0
        and width % (2 * LANES) == 0
    )


def backward_tail(lengths, counts, g_self, g_cross, small, state, weights):
    n_square, n_late = 8, 4
    own, pairs, _, text = state.self_norms.shape
    count, width = state.self_q.shape
    ff_width = state.mlp_hidden.shape[1]
    block, tall = width // 8, ff_width // 8
    tops = ((n_square // 2 * block + tall // 2, width // 2), (block, ff_width // 2))
    state = state._replace(dw_c_out=state.dw_c_out.reshape(2, 2, 2, block, width))
    slots = state.k_late.shape[0]
    vmem = pl.BlockSpec(memory_space=pltpu.VMEM)
    anywhere = pl.BlockSpec(memory_space=pl.ANY)
    smem = pl.BlockSpec(memory_space=pltpu.SMEM)

    def low(*shape):
        return pltpu.VMEM(shape, BF16)

    def wide(*shape):
        return pltpu.VMEM(shape, F32)

    units = n_square + 3
    n_groups = n_square // 2 + 2
    return pl.pallas_call(
        tail_kernel,
        out_shape=tuple(jax.ShapeDtypeStruct(t, F32) for t in tops + (small.shape,))
        + (
            jax.ShapeDtypeStruct(state.patch_grad_early.shape, BF16),
            jax.ShapeDtypeStruct((4, slots // 4, width), BF16),
            jax.ShapeDtypeStruct((4, count // 4, width), BF16),
            jax.ShapeDtypeStruct((4, text // 4, width), BF16),
        ),
        in_specs=[smem] * 2 + [vmem] * 3 + [anywhere] * (len(state) + len(weights)),
        out_specs=(vmem,) * 3 + (anywhere,) * 4,
        scratch_shapes=[
            wide(count, width),
            wide(count, width),
            low(count, width),
            low(count, width),
            low(count, width),
            low(3, count, ff_width),
            low(count, width),
            low(4 * slots, width),
            low(text, width),
            wide(*state.cross_norms.shape),
            wide(*state.self_norms.shape),
            low(4, width, width),
            low(3, 2, 2, block, ff_width),
            low(2, 2, 2, tall, width),
            low(2, 2, 2, block, ff_width),
            low(2, 2, tall, width),
            low(2, 2, block, ff_width),
            low(2, tall, width),
            low(2, block, ff_width),
            low(tall, width),
            low(n_square + 2, 2, 2, block, width),
            low(n_square, 2, 2, block, width),
            low(n_square, 2, block, width),
            low(n_square, block, width),
            low(2, 2, *tops[0]),
            low(2, *tops[0]),
            low(*tops[0]),
            low(2, 2, *tops[1]),
            low(2, *tops[1]),
            low(*tops[1]),
            wide(6, *small.shape),
            wide(5, *small.shape),
            pltpu.SemaphoreType.DMA((32,)),
            pltpu.SemaphoreType.DMA((3, units)),
            pltpu.SemaphoreType.DMA((3, units)),
            pltpu.SemaphoreType.DMA((5,)),
            pltpu.SemaphoreType.DMA((5,)),
            pltpu.SemaphoreType.DMA((2, n_groups)),
            pltpu.SemaphoreType.DMA((2, n_groups)),
            pltpu.SemaphoreType.DMA((4, 3)),
            pltpu.SemaphoreType.DMA((4, 3)),
            pltpu.SemaphoreType.DMA((4,)),
        ],
        compiler_params=pltpu.CompilerParams(
            collective_id=0, has_side_effects=True, vmem_limit_bytes=TAIL_VMEM
        ),
    )(lengths, counts, g_self, g_cross, small, *state, *weights)


def finish(narrow, wide_total, total, patches, layers, x_rows):
    n_square = 8
    parts, patch_part, width = patches[2].shape
    part = layers[0].shape[1]
    examples = 2 * parts
    block, ff_width = width // 8, 2 * wide_total.shape[1]
    tall = 2 * (narrow.shape[0] - n_square // 2 * block)
    groups = [(1, 0, block, (0, 1)), (0, n_square // 2 * block, tall // 2, (2,))]
    groups += [(0, i * block, block, (3 + 2 * i, 4 + 2 * i)) for i in range(n_square // 2)]
    shapes = [(block, ff_width // 4)] * 2 + [(tall, width // 4)] + [(block, width // 4)] * n_square

    def whole(shape):
        return pl.BlockSpec(shape, lambda e: (0,) * len(shape))

    def one(rows):
        return pl.BlockSpec((1, rows, width), lambda e: (e, 0, 0))

    def both(rows):
        return pl.BlockSpec((2, rows, width), lambda e: (e, 0, 0))

    outs = [
        ((examples, part, width), both(part)),
        ((examples, part, width), both(part)),
        ((examples, patch_part, width), both(patch_part)),
        ((1, block), whole((1, block))),
        ((1, block), whole((1, block))),
        ((1, block), whole((1, block))),
        ((total.shape[0], 1), whole((total.shape[0], 1))),
    ] + [(s, whole(s)) for s in shapes]
    results = pl.pallas_call(
        partial(finish_kernel, groups, ff_width),
        grid=(parts,),
        out_shape=tuple(jax.ShapeDtypeStruct(s, F32) for s, _ in outs),
        in_specs=[whole(narrow.shape), whole(wide_total.shape), whole(total.shape)]
        + [one(p.shape[1]) for p in patches]
        + [one(part)] * 2
        + [both(part)],
        out_specs=tuple(spec for _, spec in outs),
        compiler_params=pltpu.CompilerParams(vmem_limit_bytes=TAIL_VMEM),
    )(narrow, wide_total, total, *patches, *layers, x_rows)
    gains = [g[0] for g in results[3:6]]
    return results[:3], gains, results[6][3:10, 0], results[7:]


def norm_forward(u, gain):
    r = lax.rsqrt(jnp.mean(u * u, axis=-1, keepdims=True) + NORM_EPS)
    return (u * r * gain).astype(BF16)


def norm_backward(u, gain, w):
    r = lax.rsqrt(jnp.mean(u * u, axis=-1, keepdims=True) + NORM_EPS)
    gw = gain * w
    grad = r * gw - u * (r * r * r) * jnp.mean(gw * u, axis=-1, keepdims=True)
    return grad, jnp.sum(w * u * r, axis=0, keepdims=True)


def to_examples(rows):
    n = lax.axis_size("seq")
    examples, part, width = rows.shape
    parts = lax.all_to_all(rows.reshape(n, examples // n, part, width), "seq", 0, 0)
    return parts.transpose(1, 0, 2, 3).reshape(examples // n, n * part, width)


def to_positions(rows):
    n = lax.axis_size("seq")
    own, positions, width = rows.shape
    parts = rows.reshape(own, n, positions // n, width).transpose(1, 0, 2, 3)
    return lax.all_to_all(parts, "seq", 0, 0).reshape(n * own, positions // n, width)


def halve_over_dp(matrix, bits):
    n = lax.axis_size("dp")
    count = n.bit_length() - 1
    rows, width = matrix.shape[0] // n, matrix.shape[1]
    place = lax.axis_index("dp")
    left = list(range(count))[::-1]
    current = matrix.reshape((2,) * count + (rows, width))
    for bit in bits:
        axis = left.index(bit)
        mine = (place >> bit) & 1
        keep = lax.dynamic_index_in_dim(current, mine, axis, keepdims=False)
        give = lax.dynamic_index_in_dim(current, 1 - mine, axis, keepdims=False)
        got = lax.ppermute(give, "dp", [(i, i ^ (1 << bit)) for i in range(n)])
        current = (keep.astype(F32) + got.astype(F32)).astype(BF16)
        left.remove(bit)
    return current


def scatter_over_seq(matrix):
    n = lax.axis_size("seq")
    rows, width = matrix.shape
    parts = matrix.reshape(rows, n, width // n).transpose(1, 0, 2)
    return jnp.sum(lax.all_to_all(parts, "seq", 0, 0).astype(F32), axis=0)


def reduce_grad(matrix, order):
    n = lax.axis_size("dp")
    bits = list(range(n.bit_length() - 1))
    if order:
        bits = bits[:1] + bits[1:][::-1]
    return scatter_over_seq(halve_over_dp(matrix, bits))


def local(
    hidden_in,
    patches,
    text_lengths,
    patch_counts,
    cotangent,
    g_self,
    g_cross,
    g_mlp,
    w_query,
    w_key,
    w_value,
    w_out,
    c_query,
    c_key,
    c_value,
    c_out,
    w_gate,
    w_up,
    w_down,
):
    n_seq = lax.axis_size("seq")
    n_dp = lax.axis_size("dp")
    seq_place = lax.axis_index("seq")
    dp_place = lax.axis_index("dp")
    width = hidden_in.shape[2]
    ff_width = w_gate.shape[1]
    own = hidden_in.shape[0] // n_seq
    if takes_kernel(width, n_dp, n_seq, own):
        small, patch_early, layer_early, state = forward_head(
            text_lengths[0],
            patch_counts,
            (g_self, g_cross, g_mlp),
            (hidden_in, patches, cotangent),
            (
                w_query,
                w_key,
                w_value,
                w_out,
                c_query,
                c_key,
                c_value,
                c_out,
                w_gate,
                w_up,
                w_down,
            ),
        )
        narrow, wide, total, patch_rest, patch_late, x_out, layer_late = backward_tail(
            text_lengths[0],
            patch_counts,
            g_self,
            g_cross,
            small,
            state,
            (c_key, c_value, c_query, w_out, w_query, w_key, w_value),
        )
        rows, gains, rms_values, grads = finish(
            narrow,
            wide,
            total,
            (patch_early, patch_rest, patch_late),
            (layer_early, layer_late),
            x_out.reshape(hidden_in.shape),
        )
        gate, up, down, c_o, c_q, c_k, c_v, w_o, w_q, w_k, w_v = grads
        return (
            *rows,
            *gains,
            w_q,
            w_k,
            w_v,
            w_o,
            c_q,
            c_k,
            c_v,
            c_o,
            gate,
            up,
            down,
            rms_values,
        )
    else:
        lengths = lax.dynamic_slice_in_dim(text_lengths[0], seq_place * own, own)
        counts = lax.dynamic_slice_in_dim(patch_counts, seq_place * own, own)

        hidden = to_examples(hidden_in)
        patch = to_examples(patches)
        text = hidden.shape[1]
        slots = patch.shape[1]
        text_valid = (jnp.arange(text)[None, :] < lengths[:, None]).astype(F32).reshape(-1, 1)
        patch_valid = (jnp.arange(slots)[None, :] < counts[:, None]).astype(F32).reshape(-1, 1)
        x = hidden.reshape(-1, width).astype(F32)
        patch = patch.reshape(-1, width)
        self_flops = 4 * own * text * text * width
        cross_flops = 4 * own * text * slots * width

        normed_one = norm_forward(x, g_self)
        self_q = dot_nn(normed_one, w_query).astype(BF16)
        self_k = dot_nn(normed_one, w_key).astype(BF16)
        self_v = dot_nn(normed_one, w_value).astype(BF16)
        self_mix, self_norms = attend(
            self_forward_kernel, lengths, (self_q, self_k, self_v), None, own, self_flops
        )
        cot = to_examples(cotangent)
        self_branch = dot_nn(self_mix, w_out)
        after_self = x + self_branch
        normed_two = norm_forward(after_self, g_cross)
        cross_q = dot_nn(normed_two, c_query).astype(BF16)
        cross_k = dot_nn(patch, c_key).astype(BF16)
        cross_v = dot_nn(patch, c_value).astype(BF16)
        cross_mix, cross_norms = attend(
            cross_forward_kernel, counts, (cross_q, cross_k, cross_v), None, own, cross_flops
        )
        cross_branch = dot_nn(cross_mix, c_out)
        after_cross = after_self + cross_branch
        normed_three = norm_forward(after_cross, g_mlp)
        gate = dot_nn(normed_three, w_gate)
        up = dot_nn(normed_three, w_up)
        tanh_part = jnp.tanh(GELU_CURVE * (gate + 0.044715 * gate * gate * gate))
        gelu = 0.5 * gate * (1.0 + tanh_part)
        gelu_slope = 0.5 * (1.0 + tanh_part) + 0.5 * gate * (1.0 - tanh_part * tanh_part) * (
            GELU_CURVE * (1.0 + 3.0 * 0.044715 * gate * gate)
        )
        hidden_value = gelu * up
        hidden_low = hidden_value.astype(BF16)
        mlp_branch = dot_nn(hidden_low, w_down)
        layer_rows = after_cross + mlp_branch

        grad_y = cot.reshape(-1, width).astype(F32) * text_valid
        grad_mlp = grad_y.astype(BF16)
        grad_hidden = dot_nt(grad_mlp, w_down)
        grad_gate = (grad_hidden * up * gelu_slope).astype(BF16)
        grad_up = (grad_hidden * gelu).astype(BF16)
        grad_mlp_rows = (
            dot_tn(normed_three, grad_gate).astype(BF16),
            dot_tn(normed_three, grad_up).astype(BF16),
            dot_tn(hidden_low, grad_mlp).astype(BF16),
        )
        grad_three = dot_nt(grad_gate, w_gate) + dot_nt(grad_up, w_up)
        norm_grad, grad_g_mlp = norm_backward(after_cross, g_mlp, grad_three)
        grad_after_cross = grad_y + norm_grad
        grad_cbranch = grad_after_cross.astype(BF16)
        grad_cmix = dot_nt(grad_cbranch, c_out).astype(BF16)

        def square_row(valid, value):
            return jnp.sum(valid * value * value, axis=0, keepdims=True)

        lane = jnp.arange(LANES)
        valid_row = jnp.where(
            lane == 0, jnp.sum(lengths), jnp.where(lane == 1, jnp.sum(counts), 0)
        ).astype(F32)
        layer_low = layer_rows.astype(BF16)
        grad_cq, grad_ck, grad_cv = attend(
            cross_backward_kernel,
            counts,
            (cross_q, cross_k, cross_v, grad_cmix),
            cross_norms,
            own,
            cross_flops * 5 // 2,
        )
        grad_patch_rows = dot_nt(grad_ck, c_key) + dot_nt(grad_cv, c_value)
        grad_two = dot_nt(grad_cq, c_query)
        norm_grad, grad_g_cross = norm_backward(after_self, g_cross, grad_two)
        grad_after_self = grad_after_cross + norm_grad
        grad_sbranch = grad_after_self.astype(BF16)
        grad_smix = dot_nt(grad_sbranch, w_out).astype(BF16)
        grad_sq, grad_sk, grad_sv = attend(
            self_backward_kernel,
            lengths,
            (self_q, self_k, self_v, grad_smix),
            self_norms,
            own,
            self_flops * 5 // 2,
        )
        grad_one = dot_nt(grad_sq, w_query) + dot_nt(grad_sk, w_key) + dot_nt(grad_sv, w_value)
        norm_grad, grad_g_self = norm_backward(x, g_self, grad_one)
        grad_x_rows = grad_after_self + norm_grad
        layer_out = to_positions(layer_low.reshape(own, text, width))
        patch_out = to_positions(grad_patch_rows.astype(BF16).reshape(own, slots, width))
        x_out = to_positions(grad_x_rows.astype(BF16).reshape(own, text, width))
        grads = [
            dot_tn(rows, grad_rows).astype(BF16)
            for rows, grad_rows in (
                (normed_one, grad_sq),
                (normed_one, grad_sk),
                (normed_one, grad_sv),
                (self_mix, grad_sbranch),
                (normed_two, grad_cq),
                (patch, grad_ck),
                (patch, grad_cv),
                (cross_mix, grad_cbranch),
            )
        ]
        grads += grad_mlp_rows
        summed = tuple(reduce_grad(g, u % 2) for u, g in enumerate(grads))
        vectors = [
            grad_g_self,
            grad_g_cross,
            grad_g_mlp,
            square_row(text_valid, layer_rows),
            square_row(text_valid, self_branch),
            square_row(text_valid, cross_branch),
            square_row(text_valid, mlp_branch),
            square_row(text_valid, hidden_value),
            square_row(text_valid, grad_x_rows),
            square_row(patch_valid, grad_patch_rows),
            valid_row[None],
        ]
        folded = [
            sum(
                jnp.pad(p, ((0, 0), (0, width - p.shape[1])))
                for p in jnp.split(v, list(range(width, v.shape[1], width)), axis=1)
            )
            for v in vectors
        ]
        total = lax.psum(jnp.concatenate(folded), ("dp", "seq"))
    part = width // n_dp
    gains = [lax.dynamic_slice(total, (i, dp_place * part), (1, part))[0] for i in range(3)]
    squares = jnp.sum(total[3:10], axis=1)
    place = jnp.arange(7)
    texts, patch_count = total[10, 0], total[10, 1]
    per_value = jnp.where(
        place == 6, patch_count * width, jnp.where(place == 4, texts * ff_width, texts * width)
    )
    rms_values = jnp.sqrt(squares / per_value)
    return (
        layer_out.astype(F32),
        x_out.astype(F32),
        patch_out.astype(F32),
        gains[0],
        gains[1],
        gains[2],
        *summed,
        rms_values,
    )


def solution(mesh):
    rows = P("dp", "seq", None)
    tile = P("dp", "seq")
    in_specs = (rows, rows, P("dp", None), P("dp"), rows) + (P(),) * 14
    out_specs = (rows,) * 3 + (P("dp"),) * 3 + (tile,) * 11 + (P(),)
    return jax.shard_map(local, mesh=mesh, in_specs=in_specs, out_specs=out_specs, check_vma=False)
```

```python
from functools import partial
from types import SimpleNamespace
from typing import Any, NamedTuple

import jax
import jax.numpy as jnp
from jax import lax
from jax.experimental import pallas as pl
from jax.experimental.pallas import tpu as pltpu
from jax.sharding import PartitionSpec as P

HEAD_DIM = 64
LANES = 128
PAIR = LANES // HEAD_DIM
NORM_EPS = 1e-06
NEG_FILL = -1e30
GELU_CURVE = 0.7978845608028654
F32 = jnp.float32
BF16 = jnp.bfloat16
MESH = pl.DeviceIdType.MESH
VMEM_LIMIT = 48 * 1024 * 1024
TAIL_VMEM = 63 * 1024 * 1024
HELD_BACK = 2


def dot_nn(a, b):
    return lax.dot_general(a, b, (((1,), (0,)), ((), ())), preferred_element_type=F32)


def dot_nt(a, b):
    return lax.dot_general(a, b, (((1,), (1,)), ((), ())), preferred_element_type=F32)


def dot_tn(a, b):
    return lax.dot_general(a, b, (((0,), (0,)), ((), ())), preferred_element_type=F32)


def head_mask(h, dtype):
    lane = lax.broadcasted_iota(jnp.int32, (1, LANES), 1)
    return ((lane // HEAD_DIM) == h).astype(F32).astype(dtype)


def masked(scores, limit, causal):
    if limit is None:
        return scores
    key_pos = lax.broadcasted_iota(jnp.int32, scores.shape, 0)
    allowed = key_pos < limit
    if causal:
        queries = scores.shape[1] // PAIR
        query_pos = lax.broadcasted_iota(jnp.int32, scores.shape, 1)
        query_pos = jnp.where(query_pos < queries, query_pos, query_pos - queries)
        allowed = allowed & (key_pos <= query_pos)
    return jnp.where(allowed, scores, NEG_FILL)


def stacked(rows, factor):
    return jnp.concatenate([rows * (head_mask(h, BF16) * factor) for h in range(PAIR)], axis=0)


def own_rows(value, queries):
    parts = [
        value[h * HEAD_DIM : (h + 1) * HEAD_DIM, h * queries : (h + 1) * queries]
        for h in range(PAIR)
    ]
    return jnp.concatenate(parts, axis=0).T.astype(BF16)


def forward_pair(q, k, v, limit, causal):
    queries = q.shape[0]
    scores = masked(dot_nt(k, stacked(q, 0.125)), limit, causal)
    top = jnp.max(scores, axis=0, keepdims=True)
    exps = jnp.exp(scores - top)
    total = jnp.sum(exps, axis=0, keepdims=True)
    mixed = dot_nn(v.T, exps.astype(BF16)) / total
    norms = top + jnp.log(total)
    norms = jnp.concatenate([norms[:, :queries], norms[:, queries:]], axis=0)
    return own_rows(mixed, queries), norms


def backward_pair(q, k, v, grad_mix, norms, limit, causal):
    queries = q.shape[0]
    q_both, grad_both = stacked(q, 0.125), stacked(grad_mix, 1.0)
    norm_row = jnp.concatenate([norms[h : h + 1] for h in range(PAIR)], axis=1)
    probs = jnp.exp(masked(dot_nt(k, q_both), limit, causal) - norm_row)
    grad_v = dot_nn(probs.astype(BF16), grad_both)
    grad_p = dot_nt(v, grad_both)
    inner = jnp.sum(probs * grad_p, axis=0, keepdims=True)
    grad_s = (probs * (grad_p - inner)).astype(BF16)
    grad_k = dot_nn(grad_s, q_both)
    grad_q = dot_nn(k.T * 0.125, grad_s)
    return own_rows(grad_q, queries), grad_k.astype(BF16), grad_v.astype(BF16)


def self_forward_kernel(limit_ref, q_ref, k_ref, v_ref, mix_ref, norm_ref):
    limit = limit_ref[pl.program_id(0)]
    mix, norms = forward_pair(q_ref[...], k_ref[...], v_ref[...], limit, True)
    mix_ref[...] = mix
    norm_ref[0, 0, 0:PAIR] = norms


def self_backward_kernel(
    limit_ref, q_ref, k_ref, v_ref, grad_ref, norm_ref, dq_ref, dk_ref, dv_ref
):
    limit = limit_ref[pl.program_id(0)]
    dq, dk, dv = backward_pair(
        q_ref[...], k_ref[...], v_ref[...], grad_ref[...], norm_ref[0, 0, 0:PAIR], limit, True
    )
    dq_ref[...] = dq
    dk_ref[...] = dk
    dv_ref[...] = dv


def cross_forward_kernel(limit_ref, q_ref, k_ref, v_ref, mix_ref, norm_ref):
    limit = limit_ref[pl.program_id(0)]
    keys = k_ref.shape[0]
    short = keys // 4

    def run(count):
        mix, norms = forward_pair(q_ref[...], k_ref[0:count], v_ref[0:count], None, False)
        mix_ref[...] = mix
        norm_ref[0, 0, 0:PAIR] = norms

    pl.when(limit > short)(lambda: run(keys))
    pl.when(limit <= short)(lambda: run(short))


def cross_backward_kernel(
    limit_ref, q_ref, k_ref, v_ref, grad_ref, norm_ref, dq_ref, dk_ref, dv_ref
):
    limit = limit_ref[pl.program_id(0)]
    keys = k_ref.shape[0]
    short = keys // 4

    def run(count):
        dq, dk, dv = backward_pair(
            q_ref[...],
            k_ref[0:count],
            v_ref[0:count],
            grad_ref[...],
            norm_ref[0, 0, 0:PAIR],
            None,
            False,
        )
        dq_ref[...] = dq
        dk_ref[0:count] = dk
        dv_ref[0:count] = dv
        if count < keys:
            dk_ref[count:] = jnp.zeros((keys - count, LANES), BF16)
            dv_ref[count:] = jnp.zeros((keys - count, LANES), BF16)

    pl.when(limit > short)(lambda: run(keys))
    pl.when(limit <= short)(lambda: run(short))


def attend(kernel, limits, arrays, norms, examples, flops):
    width = arrays[0].shape[1]
    pairs = width // LANES
    queries = arrays[0].shape[0] // examples

    def rows_spec(array):
        return pl.BlockSpec((array.shape[0] // examples, LANES), lambda e, p: (e, p))

    norm_spec = pl.BlockSpec((1, 1, 8, queries), lambda e, p: (e, p, 0, 0))
    norm_shape = jax.ShapeDtypeStruct((examples, pairs, 8, queries), F32)
    in_specs = [pl.BlockSpec(memory_space=pltpu.SMEM)] + [rows_spec(a) for a in arrays]
    args = (limits,) + tuple(arrays)
    if norms is None:
        out_shape = (jax.ShapeDtypeStruct(arrays[0].shape, BF16), norm_shape)
        out_specs = (rows_spec(arrays[0]), norm_spec)
    else:
        in_specs.append(norm_spec)
        args = args + (norms,)
        out_shape = tuple(jax.ShapeDtypeStruct(a.shape, BF16) for a in arrays[:3])
        out_specs = tuple(rows_spec(a) for a in arrays[:3])
    return pl.pallas_call(
        kernel,
        grid=(examples, pairs),
        in_specs=in_specs,
        out_specs=out_specs,
        out_shape=out_shape,
        compiler_params=pltpu.CompilerParams(vmem_limit_bytes=VMEM_LIMIT),
        cost_estimate=pl.CostEstimate(
            flops=flops, bytes_accessed=sum(a.size * 2 for a in arrays), transcendentals=0
        ),
    )(*args)


class HeadState(NamedTuple):
    self_q: Any
    self_k: Any
    self_v: Any
    self_mix: Any
    normed_one: Any
    hidden: Any
    after_self: Any
    grad_after_cross: Any
    queries: Any
    normed_two: Any
    normed_three: Any
    grad_mlp: Any
    mlp_hidden: Any
    grad_gate: Any
    grad_up: Any
    self_norms: Any
    grad_mix: Any
    cross_norms: Any
    grad_k_early: Any
    grad_v_early: Any
    patch_early: Any
    k_late: Any
    v_late: Any
    patch_rows_late: Any
    layer: Any
    patch_grad_early: Any
    dw_c_out: Any


def head_kernel(*refs):
    lengths_ref, counts_ref, g_self_ref, g_cross_ref, g_mlp_ref = refs[:5]
    hidden_in, patches_in, cot_in = refs[5:8]
    weights_in = refs[8:19]
    refs = refs[19:]
    small, patch_out = refs[:2]
    n_state = len(HeadState._fields)
    kept = HeadState(*refs[2 : 2 + n_state])
    (
        hidden,
        cot,
        patch,
        normed_one,
        self_rows,
        after_self,
        normed_two,
        queries,
        keys,
        values,
        cmix,
        normed_three,
        mlp_rows,
        grad_after,
        cbranch,
        grad_mix,
        patch_send,
        layer,
        after_cross,
        mlp_sum,
        grad_three,
        squares,
        w_gate,
        w_up,
        w_down,
        self_norms,
        cross_norms,
        weight_sem,
        in_send,
        in_recv,
        in_local,
        out_send,
        out_recv,
        out_local,
        keep_sem,
    ) = refs[2 + n_state :]
    own = 2
    rows, width = hidden.shape
    text = rows // own
    slots = patch.shape[0] // own
    part, patch_part = text // 4, slots // 4
    pairs = width // LANES
    dp = lax.axis_index("dp")
    seq = lax.axis_index("seq")
    near_seq = seq + 1 - 2 * (seq % 2)
    far_seq = seq + 2 - 4 * (seq // 2)
    seq_peers = [far_seq, near_seq, 3 - seq]
    lengths = [lengths_ref[own * seq + e] for e in range(own)]
    counts = [counts_ref[own * seq + e] for e in range(own)]

    barrier = pltpu.get_barrier_semaphore()
    for z in seq_peers:
        pl.semaphore_signal(barrier, inc=1, device_id=(dp, z), device_id_type=MESH)
    pl.semaphore_wait(barrier, len(seq_peers))

    incoming = {}

    def receive(number, src, dst, size, e):
        first = pl.multiple_of(e * 4 * size + seq * size, size)
        copies = []
        for k, z in enumerate(seq_peers):
            copy = pltpu.make_async_remote_copy(
                src_ref=src.at[own * z + e],
                dst_ref=dst.at[pl.ds(first, size)],
                send_sem=in_send.at[number, k],
                recv_sem=in_recv.at[number, k],
                device_id=(dp, z),
                device_id_type=MESH,
            )
            copy.start()
            copies.append(copy)
        local_copy = pltpu.make_async_copy(
            src.at[own * seq + e], dst.at[pl.ds(first, size)], in_local.at[number]
        )
        local_copy.start()
        incoming[number] = (copies, local_copy)

    def arrived(number):
        copies, local_copy = incoming[number]
        local_copy.wait()
        for copy in copies:
            copy.wait_recv()

    receive(0, hidden_in, hidden, part, 0)
    receive(1, hidden_in, hidden, part, 1)
    receive(2, patches_in, patch, patch_part, 0)

    loads = []
    targets = [squares.at[i] for i in range(8)] + [w_gate, w_up, w_down]
    for i, (src, dst) in enumerate(zip(weights_in, targets)):
        copy = pltpu.make_async_copy(src, dst, weight_sem.at[i])
        copy.start()
        loads.append(copy)
    WQ, WK, WV, WO, CQ, CK, CV, CO = range(8)

    keeping = []

    def keep(dst, src):
        copy = pltpu.make_async_copy(src, dst, keep_sem.at[len(keeping)])
        copy.start()
        keeping.append(copy)

    small[...] = jnp.zeros(small.shape, F32)
    lane = lax.broadcasted_iota(jnp.int32, (1, width), 1)
    small[10:11] = jnp.where(
        lane == 0, lengths[0] + lengths[1], jnp.where(lane == 1, counts[0] + counts[1], 0)
    ).astype(F32)

    def add_row(i, value):
        small[i : i + 1, 0 : value.shape[1]] += value

    def valid_rows(e):
        position = lax.broadcasted_iota(jnp.int32, (text, 1), 0)
        return (position < lengths[e]).astype(F32)

    def squared(valid, value):
        return jnp.sum(valid * value * value, axis=0, keepdims=True)

    def norm(u, gain):
        r = lax.rsqrt(jnp.mean(u * u, axis=-1, keepdims=True) + NORM_EPS)
        return (u * r * gain).astype(BF16)

    arrived(0)
    arrived(1)
    for i in (WQ, WK, WV):
        loads[i].wait()
    for e in range(own):
        at = slice(e * text, (e + 1) * text)
        normed_one[at] = norm(hidden[at].astype(F32), g_self_ref[...].reshape(1, width))
        for i in (WQ, WK, WV):
            self_rows[i, at] = dot_nn(normed_one[at], squares[i]).astype(BF16)

    def self_pair(step, carry):
        e, p = step // pairs, step % pairs
        at = pl.ds(pl.multiple_of(e * text, text), text)
        lanes = pl.ds(pl.multiple_of(p * LANES, LANES), LANES)
        limit = lengths_ref[own * seq + e]
        mix, norms = forward_pair(
            self_rows[0, at, lanes], self_rows[1, at, lanes], self_rows[2, at, lanes], limit, True
        )
        self_rows[3, at, lanes] = mix
        self_norms[e, p, 0:PAIR] = norms
        return carry

    lax.fori_loop(0, own * pairs, self_pair, 0)
    receive(4, cot_in, cot, part, 0)
    receive(3, patches_in, patch, patch_part, 1)
    loads[WO].wait()
    loads[CQ].wait()
    for e in range(own):
        at = slice(e * text, (e + 1) * text)
        branch = dot_nn(self_rows[3, at], squares[WO])
        add_row(4, squared(valid_rows(e), branch))
        after = hidden[at].astype(F32) + branch
        after_self[at] = after
        normed_two[at] = norm(after, g_cross_ref[...].reshape(1, width))
        queries[at] = dot_nn(normed_two[at], squares[CQ]).astype(BF16)
    for i, dst in enumerate((kept.self_q, kept.self_k, kept.self_v, kept.self_mix)):
        keep(dst, self_rows.at[i])
    keep(kept.normed_one, normed_one)
    keep(kept.hidden, hidden)
    keep(kept.after_self, after_self)
    keep(kept.self_norms, self_norms)

    def project_patches(e):
        def body(i, carry):
            at = pl.ds(pl.multiple_of(e * slots + i * patch_part, patch_part), patch_part)
            keys[at] = dot_nn(patch[at], squares[CK]).astype(BF16)
            values[at] = dot_nn(patch[at], squares[CV]).astype(BF16)
            return carry

        lax.fori_loop(0, 4, body, 0)

    def cross_forward(e):
        at, key_at = slice(e * text, (e + 1) * text), slice(e * slots, (e + 1) * slots)

        def body(p, carry):
            lanes = pl.ds(pl.multiple_of(p * LANES, LANES), LANES)
            mix, norms = forward_pair(
                queries[at, lanes], keys[key_at, lanes], values[key_at, lanes], counts[e], False
            )
            cmix[at, lanes] = mix
            cross_norms[e, p, 0:PAIR] = norms
            return carry

        lax.fori_loop(0, pairs, body, 0)

    def feed_forward(e):
        at = slice(e * text, (e + 1) * text)
        valid = valid_rows(e)
        branch = dot_nn(cmix[at], squares[CO])
        add_row(5, squared(valid, branch))
        after = after_self[at] + branch
        after_cross[...] = after
        normed_three[at] = norm(after, g_mlp_ref[...].reshape(1, width))
        arrived(4 + e)
        cot[at] = (cot[at].astype(F32) * valid).astype(BF16)
        mlp_sum[...] = jnp.zeros((text, width), F32)
        grad_three[...] = jnp.zeros((text, width), F32)
        step = w_gate.shape[1] // 4

        def body(i, total):
            columns = pl.ds(pl.multiple_of(i * step, step), step)
            gate = dot_nn(normed_three[at], w_gate[:, columns])
            up = dot_nn(normed_three[at], w_up[:, columns])
            tanh_part = jnp.tanh(GELU_CURVE * (gate + 0.044715 * gate * gate * gate))
            gelu = 0.5 * gate * (1.0 + tanh_part)
            slope = 0.5 * (1.0 + tanh_part) + 0.5 * gate * (1.0 - tanh_part * tanh_part) * (
                GELU_CURVE * (1.0 + 3.0 * 0.044715 * gate * gate)
            )
            value = gelu * up
            low_value = value.astype(BF16)
            mlp_rows[0, at, columns] = low_value
            mlp_sum[...] += dot_nn(low_value, w_down[columns, :])
            grad_value = dot_nt(cot[at], w_down[columns, :])
            grad_gate = (grad_value * up * slope).astype(BF16)
            grad_up = (grad_value * gelu).astype(BF16)
            mlp_rows[1, at, columns] = grad_gate
            mlp_rows[2, at, columns] = grad_up
            grad_three[...] += dot_nt(grad_gate, w_gate[:, columns]) + dot_nt(
                grad_up, w_up[:, columns]
            )
            return total + squared(valid, value)

        add_row(7, lax.fori_loop(0, 4, body, jnp.zeros((1, step), F32)))
        mlp_branch = mlp_sum[...]
        add_row(6, squared(valid, mlp_branch))
        after = after_cross[...]
        out = after + mlp_branch
        add_row(3, squared(valid, out))
        layer[at] = out.astype(BF16)
        w = grad_three[...]
        r = lax.rsqrt(jnp.mean(after * after, axis=-1, keepdims=True) + NORM_EPS)
        gw = g_mlp_ref[...].reshape(1, width) * w
        add_row(2, jnp.sum(w * after * r, axis=0, keepdims=True))
        grad = r * gw - after * (r * r * r) * jnp.mean(gw * after, axis=-1, keepdims=True)
        grad = cot[at].astype(F32) + grad
        grad_after[at] = grad
        cbranch[at] = grad.astype(BF16)
        grad_mix[at] = dot_nt(cbranch[at], squares[CO]).astype(BF16)

    def cross_backward(e):
        at, key_at = slice(e * text, (e + 1) * text), slice(e * slots, (e + 1) * slots)

        def body(p, carry):
            lanes = pl.ds(pl.multiple_of(p * LANES, LANES), LANES)
            dq, dk, dv = backward_pair(
                queries[at, lanes],
                keys[key_at, lanes],
                values[key_at, lanes],
                grad_mix[at, lanes],
                cross_norms[e, p, 0:PAIR],
                counts[e],
                False,
            )
            queries[at, lanes] = dq
            keys[key_at, lanes] = dk
            values[key_at, lanes] = dv
            return carry

        lax.fori_loop(0, pairs, body, 0)

    def patch_grads(e):
        def body(d, total):
            first = pl.multiple_of(d * patch_part, patch_part)
            at = pl.ds(e * slots + first, patch_part)
            value = dot_nt(keys[at], squares[CK]) + dot_nt(values[at], squares[CV])
            position = lax.broadcasted_iota(jnp.int32, (patch_part, 1), 0) + first
            patch_send[d] = value.astype(BF16)
            return total + squared((position < counts[e]).astype(F32), value)

        add_row(9, lax.fori_loop(0, 4, body, jnp.zeros((1, width), F32)))

    outgoing = []

    def send_rows(src_of, dst, number):
        for k, z in enumerate(seq_peers):
            copy = pltpu.make_async_remote_copy(
                src_ref=src_of(z),
                dst_ref=dst.at[seq],
                send_sem=out_send.at[number, k],
                recv_sem=out_recv.at[number, k],
                device_id=(dp, z),
                device_id_type=MESH,
            )
            copy.start()
            outgoing.append(copy)
        local_copy = pltpu.make_async_copy(src_of(seq), dst.at[seq], out_local.at[number])
        local_copy.start()
        keeping.append(local_copy)

    arrived(2)
    for copy in loads[CK:]:
        copy.wait()
    project_patches(0)
    cross_forward(0)
    feed_forward(0)
    cross_backward(0)
    receive(5, cot_in, cot, part, 1)
    patch_grads(0)
    split = patch_part - patch_part // HELD_BACK
    keep(kept.patch_grad_early, patch_send.at[:, split:patch_part])
    keep(kept.grad_k_early, keys.at[0:slots])
    keep(kept.grad_v_early, values.at[0:slots])
    keep(kept.patch_early, patch.at[0:slots])
    keep(kept.normed_two, normed_two)
    arrived(3)
    send_rows(lambda z: patch_send.at[z, 0:split], patch_out, 0)
    project_patches(1)
    keep(kept.k_late, keys.at[slots : 2 * slots])
    keep(kept.v_late, values.at[slots : 2 * slots])
    keep(kept.patch_rows_late, patch.at[slots : 2 * slots])
    cross_forward(1)
    keep(kept.queries, queries)
    keep(kept.cross_norms, cross_norms.at[1])
    feed_forward(1)
    keep(kept.grad_mlp, cot)
    keep(kept.normed_three, normed_three)
    for i, dst in enumerate((kept.mlp_hidden, kept.grad_gate, kept.grad_up)):
        keep(dst, mlp_rows.at[i])
    keep(kept.grad_after_cross, grad_after)
    keep(kept.layer, layer)
    keep(kept.grad_mix, grad_mix.at[text : 2 * text])

    for i in range(2):
        columns = slice(i * (width // 2), (i + 1) * (width // 2))
        squares[0, columns] = dot_tn(cmix[:, columns], cbranch[...]).astype(BF16)
    keep(kept.dw_c_out, squares.at[0])
    for copies, local_copy in incoming.values():
        for copy in copies:
            copy.wait_send()
    for copy in outgoing:
        copy.wait()
    for copy in keeping:
        copy.wait()


def forward_head(lengths, counts, gains, rows, weights):
    examples, part, width = rows[0].shape
    patch_part = rows[1].shape[1]
    own = examples // 4
    text, slots = 4 * part, 4 * patch_part
    count, key_count = own * text, own * slots
    ff_width = weights[8].shape[1]
    pairs = width // LANES
    norms = (own, pairs, 8, text)
    vmem = pl.BlockSpec(memory_space=pltpu.VMEM)
    anywhere = pl.BlockSpec(memory_space=pl.ANY)
    smem = pl.BlockSpec(memory_space=pltpu.SMEM)
    rows_low = jax.ShapeDtypeStruct((count, width), BF16)
    rows_wide = jax.ShapeDtypeStruct((count, width), F32)
    rows_ff = jax.ShapeDtypeStruct((count, ff_width), BF16)
    keys_low = jax.ShapeDtypeStruct((slots, width), BF16)
    late_low = jax.ShapeDtypeStruct((text, width), BF16)
    state = HeadState(*[rows_low] * len(HeadState._fields))._replace(
        after_self=rows_wide,
        grad_after_cross=rows_wide,
        mlp_hidden=rows_ff,
        grad_gate=rows_ff,
        grad_up=rows_ff,
        self_norms=jax.ShapeDtypeStruct(norms, F32),
        cross_norms=jax.ShapeDtypeStruct(norms[1:], F32),
        grad_k_early=keys_low,
        grad_v_early=keys_low,
        patch_early=keys_low,
        k_late=keys_low,
        v_late=keys_low,
        patch_rows_late=keys_low,
        grad_mix=late_low,
        dw_c_out=jax.ShapeDtypeStruct((width, width), BF16),
        patch_grad_early=jax.ShapeDtypeStruct((4, patch_part // HELD_BACK, width), BF16),
    )

    def low(*shape):
        return pltpu.VMEM(shape, BF16)

    def wide(*shape):
        return pltpu.VMEM(shape, F32)

    outs = pl.pallas_call(
        head_kernel,
        out_shape=(
            jax.ShapeDtypeStruct((16, width), F32),
            jax.ShapeDtypeStruct((4, patch_part - patch_part // HELD_BACK, width), BF16),
            *state,
        ),
        in_specs=[smem] * 2 + [vmem] * 3 + [anywhere] * 14,
        out_specs=(vmem,) + (anywhere,) * (1 + len(state)),
        scratch_shapes=[
            low(count, width),
            low(count, width),
            low(key_count, width),
            low(count, width),
            low(4, count, width),
            wide(count, width),
            low(count, width),
            low(count, width),
            low(key_count, width),
            low(key_count, width),
            low(count, width),
            low(count, width),
            low(3, count, ff_width),
            wide(count, width),
            low(count, width),
            low(count, width),
            low(4, patch_part, width),
            low(count, width),
            wide(text, width),
            wide(text, width),
            wide(text, width),
            low(8, width, width),
            low(width, ff_width),
            low(width, ff_width),
            low(ff_width, width),
            wide(*norms),
            wide(*norms),
            pltpu.SemaphoreType.DMA((11,)),
            pltpu.SemaphoreType.DMA((6, 3)),
            pltpu.SemaphoreType.DMA((6, 3)),
            pltpu.SemaphoreType.DMA((6,)),
            pltpu.SemaphoreType.DMA((1, 3)),
            pltpu.SemaphoreType.DMA((1, 3)),
            pltpu.SemaphoreType.DMA((1,)),
            pltpu.SemaphoreType.DMA((len(state) + 2,)),
        ],
        compiler_params=pltpu.CompilerParams(
            collective_id=1, has_side_effects=True, vmem_limit_bytes=TAIL_VMEM
        ),
    )(lengths, counts, *gains, *rows, *weights)
    return outs[0], outs[1], HeadState(*outs[2:])


(
    GATE,
    UP,
    CROSS_A,
    CROSS_B,
    PATCHES,
    KEYS,
    C_QUERY,
    C_KEY,
    C_VALUE,
    LOADS,
    MIDDLE,
    W_OUT,
    SELF_A,
    SELF_B,
    LAST,
    W_QUERY,
    W_KEY,
    W_VALUE,
) = range(18)
CORE, GO, TWO, THREE, NEAR, FAR, SMALL = range(7)
TAIL_ORDER = (
    GATE, (CORE, 3), UP, (GO, 3), (CORE, 2), (GO, 2), CROSS_A, (CORE, 0), (GO, 0), CROSS_B, C_QUERY,
    LOADS, (CORE, 1), (GO, 1), MIDDLE, (CORE, 4), (GO, 4), PATCHES, SELF_A, (TWO, 2), SELF_B, (TWO, 3),
    (TWO, 4), (TWO, 0), W_QUERY, W_KEY, W_VALUE, (TWO, 1), KEYS, W_OUT, (CORE, 8), (THREE, 1),
    (CORE, 10), (CORE, 7), (GO, 7), (GO, 8), C_KEY, (GO, 10), (THREE, 2), C_VALUE, (CORE, 9), (NEAR, 1),
    (CORE, 5), (GO, 9), (GO, 5), (THREE, 0), (NEAR, 2), (CORE, 6), (GO, 6), LAST, (TWO, 8), (TWO, 7),
    (TWO, 9), (SMALL, 0), (NEAR, 0), (TWO, 10), (TWO, 6), (SMALL, 1), (TWO, 5), (THREE, 4), (THREE, 5),
    (SMALL, 2), (THREE, 3), (NEAR, 4), (NEAR, 5), (SMALL, 3), (FAR, 0), (NEAR, 3), (FAR, 1), (FAR, 4),
    (FAR, 5), (FAR, 2), (FAR, 3), (SMALL, 4),
)
Y_FIRST = (1, 2, 6, 8, 9)


def tail_kernel(lengths_ref, counts_ref, g_self_ref, g_cross_ref, small_in, *refs):
    n_state = len(HeadState._fields)
    hbm = HeadState(*refs[:n_state])
    c_key, c_value, c_query, w_out, w_query, w_key, w_value = refs[n_state : n_state + 7]
    refs = refs[n_state + 7 :]
    narrow, wide, small_out, early_out, patch_out, x_out, layer_out, layer_late_out = refs[:8]
    (
        after_self,
        grad_after,
        queries,
        normed,
        normed_two,
        mlp_rows,
        grad_mlp,
        big,
        grad_mix,
        cross_norms,
        self_norms,
        weights,
        wide_units,
        tall_units,
        wide_core,
        tall_core,
        wide_two,
        tall_two,
        wide_three,
        tall_three,
        square,
        square_core,
        square_two,
        square_three,
        cut_narrow,
        near_narrow,
        far_narrow,
        cut_wide,
        near_wide,
        far_wide,
        small_own,
        small_got,
        load_sem,
        send_sem,
        recv_sem,
        small_send,
        small_recv,
        cut_send,
        cut_recv,
        out_send,
        out_recv,
        out_local,
    ) = refs[8:]
    width = queries.shape[1]
    block = width // 8
    text = self_norms.shape[3]
    own = 2
    pairs = width // LANES
    part = text // 4

    dp = lax.axis_index("dp")
    seq = lax.axis_index("seq")
    core, x, y = dp % 2, (dp // 2) % 2, dp // 4
    low, high = seq % 2, seq // 2
    to_core = (dp + 1 - 2 * core, seq)
    to_x = (dp + 2 - 4 * x, seq)
    to_y = (dp + 4 - 8 * y, seq)
    near_seq = seq + 1 - 2 * low
    far_seq = seq + 2 - 4 * high
    last_seq = 3 - seq
    seq_peers = [near_seq, far_seq, last_seq]
    to_near, to_far = (dp, near_seq), (dp, far_seq)
    peers = [to_core, to_x, to_y, to_near, to_far, (dp, last_seq)]

    barrier = pltpu.get_barrier_semaphore()
    for peer in peers:
        pl.semaphore_signal(barrier, inc=1, device_id=peer, device_id_type=MESH)

    got, waited = SimpleNamespace(count=0), set()

    def need(*copies):
        for copy in copies:
            if id(copy) not in waited:
                copy.wait()
                waited.add(id(copy))

    def load(src, dst):
        copy = pltpu.make_async_copy(src, dst, load_sem.at[got.count])
        copy.start()
        got.count += 1
        return copy

    slots = big.shape[0] // 4
    patch_part = slots // 4
    keys, values, patch, patch_send = (big.at[i * slots : (i + 1) * slots] for i in range(4))
    self_q, self_k, self_v, self_mix, hidden, sbranch = (
        mlp_rows.at[i // 2, :, i % 2 * width : (i % 2 + 1) * width] for i in range(6)
    )
    grad_smix = normed_two
    got.mlp_hidden = load(hbm.mlp_hidden, mlp_rows.at[0])
    got.grad_mlp = load(hbm.grad_mlp, grad_mlp)
    got.normed = load(hbm.normed_three, normed)
    got.grad_gate = load(hbm.grad_gate, mlp_rows.at[1])
    got.grad_up = load(hbm.grad_up, mlp_rows.at[2])
    got.dw_c_out = load(hbm.dw_c_out.at[:, :, core], square.at[0])
    got.queries = load(hbm.queries, queries)
    got.keys = load(hbm.k_late, keys)
    got.values = load(hbm.v_late, values)
    got.grad_mix = load(hbm.grad_mix, grad_mix)
    got.cross_norms = load(hbm.cross_norms, cross_norms)
    got.c_key = load(c_key, weights.at[0])
    got.c_value = load(c_value, weights.at[1])
    got.patch = load(hbm.patch_rows_late, patch)
    got.normed_two = load(hbm.normed_two, normed_two)
    got.after_self = load(hbm.after_self, after_self)
    got.grad_after = load(hbm.grad_after_cross, grad_after)
    got.c_query = load(c_query, weights.at[2])
    got.w_out = load(w_out, weights.at[3])
    got.self_norms = load(hbm.self_norms, self_norms)

    small_own[0] = small_in[...]

    def add_row(i, value):
        small_own[0, i : i + 1] += value

    def remote(src, dst, send, recv, device):
        copy = pltpu.make_async_remote_copy(
            src_ref=src,
            dst_ref=dst,
            send_sem=send,
            recv_sem=recv,
            device_id=device,
            device_id_type=MESH,
        )
        copy.start()
        return copy

    n_square = square_core.shape[0]
    y_first = Y_FIRST
    first, second, third, near, far, small = {}, {}, {}, {}, {}, {}
    got_core = [wide_core.at[0], wide_core.at[1], tall_core]
    got_core += [square_core.at[i] for i in range(n_square)]
    got_two = [wide_two.at[0], wide_two.at[1], tall_two]
    got_two += [square_two.at[i] for i in range(n_square)]
    got_three = [wide_three.at[0], wide_three.at[1], tall_three]
    got_three += [square_three.at[i] for i in range(n_square)]
    current = [wide_units.at[0], wide_units.at[1], tall_units.at[0]]
    current += [square.at[i] for i in range(n_square)]
    def add(out, got):
        rows = out.shape[0]
        step = 32

        def body(i, carry):
            at = pl.ds(pl.multiple_of(i * step, step), step)
            out[at, :] = (out[at, :].astype(F32) + got[at, :].astype(F32)).astype(BF16)
            return carry

        lax.fori_loop(0, rows // step, body, 0)

    def over_core(u):
        if u == 3:
            need(got.dw_c_out)
        first[u].wait_recv()
        for i in range(2):
            for j in range(2):
                add(current[u].at[i, j], got_core[u].at[i, j])

    def leave_two(u):
        cur = current[u]
        src, device = (cur.at[1 - y], to_y) if u in y_first else (cur.at[:, 1 - x], to_x)
        second[u] = remote(src, got_two[u], send_sem.at[1, u], recv_sem.at[1, u], device)

    def over_two(u):
        second[u].wait_recv()
        cur = current[u]
        for i in range(2):
            add(cur.at[y, i] if u in y_first else cur.at[i, x], got_two[u].at[i])
        src, device = (cur.at[y, 1 - x], to_x) if u in y_first else (cur.at[1 - y, x], to_y)
        third[u] = remote(src, got_three[u], send_sem.at[2, u], recv_sem.at[2, u], device)

    groups = [(1, 0, block, (0, 1)), (0, n_square // 2 * block, tall_three.shape[0] // 2, (2,))]
    groups += [(0, i * block, block, (3 + 2 * i, 4 + 2 * i)) for i in range(n_square // 2)]
    cut, got_near, got_far = (cut_narrow, cut_wide), (near_narrow, near_wide), (far_narrow, far_wide)
    totals = (narrow, wide)

    def over_three(g):
        buffer, row, rows, members = groups[g]
        for u in members:
            third[u].wait_recv()
        halves = [current[u][y, x].astype(F32) + got_three[u][...].astype(F32) for u in members]
        if len(members) == 1:
            halves = [halves[0][:rows], halves[0][rows:]]
        piece = halves[0].shape[1] // 4
        at = pl.ds(row, rows)
        for z in range(4):
            columns = [h[:, z * piece : (z + 1) * piece] for h in halves]
            cut[buffer][z // 2, z % 2, at] = jnp.concatenate(columns, axis=1).astype(BF16)
        near[g] = remote(
            cut[buffer].at[:, 1 - low, at],
            got_near[buffer].at[:, at],
            cut_send.at[0, g],
            cut_recv.at[0, g],
            to_near,
        )

    def over_near(g):
        buffer, row, rows, _ = groups[g]
        near[g].wait_recv()
        at = pl.ds(row, rows)
        for i in range(2):
            add(cut[buffer].at[i, low, at], got_near[buffer].at[i, at])
        far[g] = remote(
            cut[buffer].at[1 - high, low, at],
            got_far[buffer].at[at],
            cut_send.at[1, g],
            cut_recv.at[1, g],
            to_far,
        )

    def over_far(g):
        buffer, row, rows, _ = groups[g]
        far[g].wait_recv()
        at = pl.ds(row, rows)
        totals[buffer][at] = cut[buffer][high, low, at].astype(F32) + got_far[buffer][at].astype(F32)

    def give(u, src):
        first[u] = remote(src, got_core[u], send_sem.at[0, u], recv_sem.at[0, u], to_core)

    def weight_grad(i, rows, grad_rows, more=None):
        ring = n_square + len(ring_units) % 2
        if len(ring_units) >= 2:
            first[ring_units[-2]].wait_send()
            first_sent.add(ring_units[-2])
        ring_units.append(3 + i)
        half = width // 2
        for h in range(2):
            value = dot_tn(rows[:, h * half : (h + 1) * half], grad_rows[...])
            if more is not None:
                value = value + more[h * half : (h + 1) * half].astype(F32)
            value = value.astype(BF16)
            for j in range(4):
                at = i + ((j + core) % 2) * (ring - i)
                square[at, h, j // 2] = value[j * block : (j + 1) * block]
        give(3 + i, square.at[ring])

    def wide_grad(u):
        if u == 1:
            first[0].wait_send()
            first_sent.add(0)
        half, step = width // 2, wide_units.shape[4] // 4

        def body(i, carry):
            columns = pl.ds(pl.multiple_of(i * step, step), step)
            for h in range(2):
                value = dot_tn(
                    normed[:, h * half : (h + 1) * half], mlp_rows[1 + u, :, columns]
                ).astype(BF16)
                for j in range(4):
                    at = u + ((j + core) % 2) * (2 - u)
                    wide_units[at, h, j // 2, :, columns] = value[j * block : (j + 1) * block]
            return carry

        lax.fori_loop(0, 4, body, 0)
        give(u, wide_units.at[2])

    def tall_grad():
        rows = tall_units.shape[3]

        def body(j, carry):
            columns = pl.ds(pl.multiple_of(j * rows, rows), rows)
            value = dot_tn(mlp_rows[0, :, columns], grad_mlp[...]).astype(BF16)
            tall_units[(j + core) % 2, j // 4, (j // 2) % 2] = value
            return carry

        lax.fori_loop(0, 8, body, 0)

    first_sent, ring_units = set(), []

    outs, locals_ = [], []

    def send_rows(src_of, dst, number):
        for k, z in enumerate([far_seq, near_seq, last_seq]):
            outs.append(
                remote(src_of(z), dst, out_send.at[number, k], out_recv.at[number, k], (dp, z))
            )
        copy = pltpu.make_async_copy(src_of(seq), dst, out_local.at[number])
        copy.start()
        locals_.append(copy)

    chunk = own * text // 4
    late = slice(text, 2 * text)
    limit = counts_ref[own * seq + 1]

    def cross_pairs(first_pair, last_pair):
        def body(p, carry):
            lanes = pl.ds(pl.multiple_of(p * LANES, LANES), LANES)
            dq, dk, dv = backward_pair(
                queries[late, lanes],
                keys[:, lanes],
                values[:, lanes],
                grad_mix[:, lanes],
                cross_norms[p, 0:PAIR],
                limit,
                False,
            )
            queries[late, lanes] = dq
            keys[:, lanes] = dk
            values[:, lanes] = dv
            return carry

        lax.fori_loop(first_pair, last_pair, body, 0)

    def patch_grads():
        def body(d, total):
            at = pl.ds(pl.multiple_of(d * patch_part, patch_part), patch_part)
            value = dot_nt(keys[at, :], weights[0]) + dot_nt(values[at, :], weights[1])
            position = lax.broadcasted_iota(jnp.int32, (patch_part, 1), 0) + d * patch_part
            patch_send[at, :] = value.astype(BF16)
            valid = (position < limit).astype(F32)
            return total + jnp.sum(valid * value * value, axis=0, keepdims=True)

        add_row(9, lax.fori_loop(0, 4, body, jnp.zeros((1, width), F32)))
        send_rows(
            lambda z: patch_send.at[pl.ds(pl.multiple_of(z * patch_part, patch_part), patch_part)],
            patch_out.at[seq],
            0,
        )

    def gate_weight():
        need(got.normed, got.grad_gate)
        wide_grad(0)

    def up_weight():
        need(got.normed, got.grad_up)
        wide_grad(1)
        got.normed_one = load(hbm.normed_one, normed)

    def down_weight():
        need(got.mlp_hidden, got.grad_mlp)
        tall_grad()

    def cross_some(first_pair, last_pair):
        need(got.queries, got.keys, got.values, got.grad_mix, got.cross_norms)
        cross_pairs(first_pair, last_pair)

    def late_patches():
        need(got.c_key, got.c_value)
        patch_grads()

    def late_keys():
        need(got.patch)
        half = width // 2
        for slot, right in ((0, keys), (1, values)):
            for h in range(2):
                columns = slice(h * half, (h + 1) * half)
                weights[slot, columns] = dot_tn(patch[:, columns], right[...]).astype(BF16)
        got.grad_k = load(hbm.grad_k_early, keys)
        got.grad_v = load(hbm.grad_v_early, values)
        got.patch_early = load(hbm.patch_early, patch)

    def query_weight():
        need(got.normed_two)
        weight_grad(1, normed_two, queries)

    def key_weight():
        need(got.grad_k, got.patch_early)
        weight_grad(2, patch, keys, weights.at[0])

    def value_weight():
        need(got.grad_v, got.patch_early)
        weight_grad(3, patch, values, weights.at[1])
        got.w_query = load(w_query, weights.at[0])
        got.w_key = load(w_key, weights.at[1])

    def self_loads():
        got.self_q = load(hbm.self_q, self_q)
        got.self_k = load(hbm.self_k, self_k)
        got.self_v = load(hbm.self_v, self_v)
        got.self_mix = load(hbm.self_mix, self_mix)
        got.hidden = load(hbm.hidden, hidden)

    def out_weight():
        need(got.self_mix)
        weight_grad(4, self_mix, sbranch)

    def self_weight(i, rows):
        need(got.normed_one)
        weight_grad(i, normed, rows)

    def norm_grad(u, gain, w):
        r = lax.rsqrt(jnp.mean(u * u, axis=-1, keepdims=True) + NORM_EPS)
        gw = gain * w
        grad = r * gw - u * (r * r * r) * jnp.mean(gw * u, axis=-1, keepdims=True)
        return grad, jnp.sum(w * u * r, axis=0, keepdims=True)

    def middle(i, total):
        at = pl.ds(pl.multiple_of(i * chunk, chunk), chunk)
        w = dot_nt(queries[at, :], weights[2])
        grad, row = norm_grad(after_self[at, :], g_cross_ref[...].reshape(1, width), w)
        grad = grad_after[at, :] + grad
        grad_after[at, :] = grad
        low_grad = grad.astype(BF16)
        sbranch[at, :] = low_grad
        grad_smix[at, :] = dot_nt(low_grad, weights[3]).astype(BF16)
        return total + row

    def self_inputs():
        need(got.after_self, got.grad_after, got.c_query, got.w_out)
        add_row(1, lax.fori_loop(0, 4, middle, jnp.zeros((1, width), F32)))
        got.w_value = load(w_value, weights.at[2])

    def self_pairs(first_step, last_step):
        def body(i, carry):
            e, p = i // pairs, i % pairs
            rows = pl.ds(pl.multiple_of(e * text, text), text)
            lanes = pl.ds(pl.multiple_of(p * LANES, LANES), LANES)
            dq, dk, dv = backward_pair(
                self_q[rows, lanes],
                self_k[rows, lanes],
                self_v[rows, lanes],
                grad_smix[rows, lanes],
                self_norms[e, p, 0:PAIR],
                lengths_ref[own * seq + e],
                True,
            )
            self_q[rows, lanes] = dq
            self_k[rows, lanes] = dk
            self_v[rows, lanes] = dv
            return carry

        lax.fori_loop(first_step, last_step, body, 0)

    def self_some(first_step, last_step):
        need(got.self_q, got.self_k, got.self_v, got.self_norms)
        self_pairs(first_step, last_step)

    def last(i, carry):
        total, squares = carry
        at = pl.ds(pl.multiple_of(i * chunk, chunk), chunk)
        w = (
            dot_nt(self_q[at, :], weights[0])
            + dot_nt(self_k[at, :], weights[1])
            + dot_nt(self_v[at, :], weights[2])
        )
        grad, row = norm_grad(hidden[at, :].astype(F32), g_self_ref[...].reshape(1, width), w)
        grad = grad_after[at, :] + grad
        e, half = i // 2, i % 2
        position = lax.broadcasted_iota(jnp.int32, (chunk, 1), 0) + half * chunk
        valid = (position < lengths_ref[own * seq + e]).astype(F32)
        low_grad = grad.astype(BF16)
        for k in range(2):
            place = (2 * half + k) * own + e
            grad_mlp[pl.ds(pl.multiple_of(place * part, part), part)] = low_grad[
                k * part : (k + 1) * part
            ]
        return total + row, squares + jnp.sum(valid * grad * grad, axis=0, keepdims=True)

    def inputs_grad():
        need(got.w_query, got.w_key, got.w_value, got.hidden)
        zero = jnp.zeros((1, width), F32)
        total, squares = lax.fori_loop(0, 4, last, (zero, zero))
        add_row(0, total)
        add_row(8, squares)
        leaving = own * part
        send_rows(
            lambda z: grad_mlp.at[pl.ds(pl.multiple_of(z * leaving, leaving), leaving)],
            x_out.at[seq],
            2,
        )
        send_small(0)

    def send_small(i):
        small[i] = remote(
            small_own.at[i], small_got.at[i], small_send.at[i], small_recv.at[i], peers[i]
        )

    def add_small(i):
        small[i].wait_recv()
        small_own[i + 1] = small_own[i] + small_got[i]

    def pass_small(i):
        add_small(i)
        if i < 4:
            send_small(i + 1)

    work = {
        GATE: gate_weight,
        UP: up_weight,
        CROSS_A: lambda: cross_some(0, pairs // 2),
        CROSS_B: lambda: cross_some(pairs // 2, pairs),
        PATCHES: late_patches,
        KEYS: late_keys,
        C_QUERY: query_weight,
        C_KEY: key_weight,
        C_VALUE: value_weight,
        LOADS: self_loads,
        MIDDLE: self_inputs,
        W_OUT: out_weight,
        SELF_A: lambda: self_some(0, pairs),
        SELF_B: lambda: self_some(pairs, 2 * pairs),
        LAST: inputs_grad,
        W_QUERY: lambda: self_weight(5, self_q),
        W_KEY: lambda: self_weight(6, self_k),
        W_VALUE: lambda: self_weight(7, self_v),
    }
    exchange = {
        CORE: over_core,
        GO: leave_two,
        TWO: over_two,
        THREE: over_three,
        NEAR: over_near,
        FAR: over_far,
        SMALL: pass_small,
    }
    down_weight()
    pl.semaphore_wait(barrier, len(peers))
    give(2, tall_units.at[1])
    first[3] = remote(
        hbm.dw_c_out.at[:, :, 1 - core],
        got_core[3],
        send_sem.at[0, 3],
        recv_sem.at[0, 3],
        to_core,
    )

    for e, (dst, number) in enumerate(((layer_out, 1), (layer_late_out, 4))):
        send_rows(
            lambda z, e=e: hbm.layer.at[
                pl.ds(pl.multiple_of(e * text + z * part, part), part)
            ],
            dst.at[seq],
            number,
        )
    send_rows(lambda z: hbm.patch_grad_early.at[z], early_out.at[seq], 3)
    for step in TAIL_ORDER:
        if isinstance(step, tuple):
            exchange[step[0]](step[1])
        else:
            work[step]()
    small_out[...] = small_own[5]
    for copy in outs:
        copy.wait_recv()
    for copy in locals_:
        copy.wait()
    for u, copy in first.items():
        if u not in first_sent:
            copy.wait_send()
    for copies in (second, third, near, far, small):
        for copy in copies.values():
            copy.wait_send()
    for copy in outs:
        copy.wait_send()


def finish_kernel(groups, ff_width, *refs):
    narrow_ref, wide_ref, small_ref, patch_first, patch_rest, patch_late = refs[:6]
    layer_early, layer_late, x_in = refs[6:9]
    layer_out, x_out, patch_out, gain_self, gain_cross, gain_mlp, rms_out = refs[9:16]
    out_refs = refs[16:]
    step = pl.program_id(0)
    split = patch_first.shape[1]
    x_out[...] = x_in[...].astype(F32)
    patch_out[0, :split] = patch_first[0].astype(F32)
    patch_out[0, split:] = patch_rest[0].astype(F32)
    patch_out[1] = patch_late[0].astype(F32)
    layer_out[0] = layer_early[0].astype(F32)
    layer_out[1] = layer_late[0].astype(F32)

    @pl.when(step == 0)
    def sums():
        for buffer, row, rows, members in groups:
            total = (narrow_ref, wide_ref)[buffer][row : row + rows]
            part = total.shape[1] // 2
            if len(members) == 2:
                out_refs[members[0]][...] = total[:, :part]
                out_refs[members[1]][...] = total[:, part:]
            else:
                out_refs[members[0]][0:rows] = total[:, :part]
                out_refs[members[0]][rows:] = total[:, part:]
        small = small_ref[...]
        width = small.shape[1]
        piece = width // 8
        for i, gain in enumerate((gain_self, gain_cross, gain_mlp)):
            for d in range(8):
                value = small[i : i + 1, d * piece : (d + 1) * piece]
                pl.when(lax.axis_index("dp") == d)(partial(store, gain, value))
        squares = jnp.sum(small, axis=1, keepdims=True)
        row = lax.broadcasted_iota(jnp.int32, squares.shape, 0)
        texts, patch_count = small[10:11, 0:1], small[10:11, 1:2]
        count = jnp.where(
            row == 9, patch_count * width, jnp.where(row == 7, texts * ff_width, texts * width)
        )
        rms_out[...] = jnp.sqrt(squares / count)


def store(ref, value):
    ref[...] = value


def takes_kernel(width, n_dp, n_seq, own):
    return (
        n_dp == 8
        and n_seq == 4
        and own == 2
        and width // n_dp % 32 == 0
        and width % (2 * LANES) == 0
    )


def backward_tail(lengths, counts, g_self, g_cross, small, state, weights):
    n_square, n_late = 8, 4
    own, pairs, _, text = state.self_norms.shape
    count, width = state.self_q.shape
    ff_width = state.mlp_hidden.shape[1]
    block, tall = width // 8, ff_width // 8
    tops = ((n_square // 2 * block + tall // 2, width // 2), (block, ff_width // 2))
    state = state._replace(dw_c_out=state.dw_c_out.reshape(2, 2, 2, block, width))
    slots = state.k_late.shape[0]
    vmem = pl.BlockSpec(memory_space=pltpu.VMEM)
    anywhere = pl.BlockSpec(memory_space=pl.ANY)
    smem = pl.BlockSpec(memory_space=pltpu.SMEM)

    def low(*shape):
        return pltpu.VMEM(shape, BF16)

    def wide(*shape):
        return pltpu.VMEM(shape, F32)

    units = n_square + 3
    n_groups = n_square // 2 + 2
    return pl.pallas_call(
        tail_kernel,
        out_shape=tuple(jax.ShapeDtypeStruct(t, F32) for t in tops + (small.shape,))
        + (
            jax.ShapeDtypeStruct(state.patch_grad_early.shape, BF16),
            jax.ShapeDtypeStruct((4, slots // 4, width), BF16),
            jax.ShapeDtypeStruct((4, count // 4, width), BF16),
            jax.ShapeDtypeStruct((4, text // 4, width), BF16),
            jax.ShapeDtypeStruct((4, text // 4, width), BF16),
        ),
        in_specs=[smem] * 2 + [vmem] * 3 + [anywhere] * (len(state) + len(weights)),
        out_specs=(vmem,) * 3 + (anywhere,) * 5,
        scratch_shapes=[
            wide(count, width),
            wide(count, width),
            low(count, width),
            low(count, width),
            low(count, width),
            low(3, count, ff_width),
            low(count, width),
            low(4 * slots, width),
            low(text, width),
            wide(*state.cross_norms.shape),
            wide(*state.self_norms.shape),
            low(4, width, width),
            low(3, 2, 2, block, ff_width),
            low(2, 2, 2, tall, width),
            low(2, 2, 2, block, ff_width),
            low(2, 2, tall, width),
            low(2, 2, block, ff_width),
            low(2, tall, width),
            low(2, block, ff_width),
            low(tall, width),
            low(n_square + 2, 2, 2, block, width),
            low(n_square, 2, 2, block, width),
            low(n_square, 2, block, width),
            low(n_square, block, width),
            low(2, 2, *tops[0]),
            low(2, *tops[0]),
            low(*tops[0]),
            low(2, 2, *tops[1]),
            low(2, *tops[1]),
            low(*tops[1]),
            wide(6, *small.shape),
            wide(5, *small.shape),
            pltpu.SemaphoreType.DMA((32,)),
            pltpu.SemaphoreType.DMA((3, units)),
            pltpu.SemaphoreType.DMA((3, units)),
            pltpu.SemaphoreType.DMA((5,)),
            pltpu.SemaphoreType.DMA((5,)),
            pltpu.SemaphoreType.DMA((2, n_groups)),
            pltpu.SemaphoreType.DMA((2, n_groups)),
            pltpu.SemaphoreType.DMA((5, 3)),
            pltpu.SemaphoreType.DMA((5, 3)),
            pltpu.SemaphoreType.DMA((5,)),
        ],
        compiler_params=pltpu.CompilerParams(
            collective_id=0, has_side_effects=True, vmem_limit_bytes=TAIL_VMEM
        ),
    )(lengths, counts, g_self, g_cross, small, *state, *weights)


def finish(narrow, wide_total, total, patches, layers, x_rows):
    n_square = 8
    parts, patch_part, width = patches[2].shape
    part = layers[0].shape[1]
    examples = 2 * parts
    block, ff_width = width // 8, 2 * wide_total.shape[1]
    tall = 2 * (narrow.shape[0] - n_square // 2 * block)
    groups = [(1, 0, block, (0, 1)), (0, n_square // 2 * block, tall // 2, (2,))]
    groups += [(0, i * block, block, (3 + 2 * i, 4 + 2 * i)) for i in range(n_square // 2)]
    shapes = [(block, ff_width // 4)] * 2 + [(tall, width // 4)] + [(block, width // 4)] * n_square

    def whole(shape):
        return pl.BlockSpec(shape, lambda e: (0,) * len(shape))

    def one(rows):
        return pl.BlockSpec((1, rows, width), lambda e: (e, 0, 0))

    def both(rows):
        return pl.BlockSpec((2, rows, width), lambda e: (e, 0, 0))

    outs = [
        ((examples, part, width), both(part)),
        ((examples, part, width), both(part)),
        ((examples, patch_part, width), both(patch_part)),
        ((1, block), whole((1, block))),
        ((1, block), whole((1, block))),
        ((1, block), whole((1, block))),
        ((total.shape[0], 1), whole((total.shape[0], 1))),
    ] + [(s, whole(s)) for s in shapes]
    results = pl.pallas_call(
        partial(finish_kernel, groups, ff_width),
        grid=(parts,),
        out_shape=tuple(jax.ShapeDtypeStruct(s, F32) for s, _ in outs),
        in_specs=[whole(narrow.shape), whole(wide_total.shape), whole(total.shape)]
        + [one(p.shape[1]) for p in patches]
        + [one(part)] * 2
        + [both(part)],
        out_specs=tuple(spec for _, spec in outs),
        compiler_params=pltpu.CompilerParams(vmem_limit_bytes=TAIL_VMEM),
    )(narrow, wide_total, total, *patches, *layers, x_rows)
    gains = [g[0] for g in results[3:6]]
    return results[:3], gains, results[6][3:10, 0], results[7:]


def norm_forward(u, gain):
    r = lax.rsqrt(jnp.mean(u * u, axis=-1, keepdims=True) + NORM_EPS)
    return (u * r * gain).astype(BF16)


def norm_backward(u, gain, w):
    r = lax.rsqrt(jnp.mean(u * u, axis=-1, keepdims=True) + NORM_EPS)
    gw = gain * w
    grad = r * gw - u * (r * r * r) * jnp.mean(gw * u, axis=-1, keepdims=True)
    return grad, jnp.sum(w * u * r, axis=0, keepdims=True)


def to_examples(rows):
    n = lax.axis_size("seq")
    examples, part, width = rows.shape
    parts = lax.all_to_all(rows.reshape(n, examples // n, part, width), "seq", 0, 0)
    return parts.transpose(1, 0, 2, 3).reshape(examples // n, n * part, width)


def to_positions(rows):
    n = lax.axis_size("seq")
    own, positions, width = rows.shape
    parts = rows.reshape(own, n, positions // n, width).transpose(1, 0, 2, 3)
    return lax.all_to_all(parts, "seq", 0, 0).reshape(n * own, positions // n, width)


def halve_over_dp(matrix, bits):
    n = lax.axis_size("dp")
    count = n.bit_length() - 1
    rows, width = matrix.shape[0] // n, matrix.shape[1]
    place = lax.axis_index("dp")
    left = list(range(count))[::-1]
    current = matrix.reshape((2,) * count + (rows, width))
    for bit in bits:
        axis = left.index(bit)
        mine = (place >> bit) & 1
        keep = lax.dynamic_index_in_dim(current, mine, axis, keepdims=False)
        give = lax.dynamic_index_in_dim(current, 1 - mine, axis, keepdims=False)
        got = lax.ppermute(give, "dp", [(i, i ^ (1 << bit)) for i in range(n)])
        current = (keep.astype(F32) + got.astype(F32)).astype(BF16)
        left.remove(bit)
    return current


def scatter_over_seq(matrix):
    n = lax.axis_size("seq")
    rows, width = matrix.shape
    parts = matrix.reshape(rows, n, width // n).transpose(1, 0, 2)
    return jnp.sum(lax.all_to_all(parts, "seq", 0, 0).astype(F32), axis=0)


def reduce_grad(matrix, order):
    n = lax.axis_size("dp")
    bits = list(range(n.bit_length() - 1))
    if order:
        bits = bits[:1] + bits[1:][::-1]
    return scatter_over_seq(halve_over_dp(matrix, bits))


def local(
    hidden_in,
    patches,
    text_lengths,
    patch_counts,
    cotangent,
    g_self,
    g_cross,
    g_mlp,
    w_query,
    w_key,
    w_value,
    w_out,
    c_query,
    c_key,
    c_value,
    c_out,
    w_gate,
    w_up,
    w_down,
):
    n_seq = lax.axis_size("seq")
    n_dp = lax.axis_size("dp")
    seq_place = lax.axis_index("seq")
    dp_place = lax.axis_index("dp")
    width = hidden_in.shape[2]
    ff_width = w_gate.shape[1]
    own = hidden_in.shape[0] // n_seq
    if takes_kernel(width, n_dp, n_seq, own):
        small, patch_early, state = forward_head(
            text_lengths[0],
            patch_counts,
            (g_self, g_cross, g_mlp),
            (hidden_in, patches, cotangent),
            (
                w_query,
                w_key,
                w_value,
                w_out,
                c_query,
                c_key,
                c_value,
                c_out,
                w_gate,
                w_up,
                w_down,
            ),
        )
        narrow, wide, total, patch_rest, patch_late, x_out, *layers = backward_tail(
            text_lengths[0],
            patch_counts,
            g_self,
            g_cross,
            small,
            state,
            (c_key, c_value, c_query, w_out, w_query, w_key, w_value),
        )
        rows, gains, rms_values, grads = finish(
            narrow,
            wide,
            total,
            (patch_early, patch_rest, patch_late),
            layers,
            x_out.reshape(hidden_in.shape),
        )
        gate, up, down, c_o, c_q, c_k, c_v, w_o, w_q, w_k, w_v = grads
        return (
            *rows,
            *gains,
            w_q,
            w_k,
            w_v,
            w_o,
            c_q,
            c_k,
            c_v,
            c_o,
            gate,
            up,
            down,
            rms_values,
        )
    else:
        lengths = lax.dynamic_slice_in_dim(text_lengths[0], seq_place * own, own)
        counts = lax.dynamic_slice_in_dim(patch_counts, seq_place * own, own)

        hidden = to_examples(hidden_in)
        patch = to_examples(patches)
        text = hidden.shape[1]
        slots = patch.shape[1]
        text_valid = (jnp.arange(text)[None, :] < lengths[:, None]).astype(F32).reshape(-1, 1)
        patch_valid = (jnp.arange(slots)[None, :] < counts[:, None]).astype(F32).reshape(-1, 1)
        x = hidden.reshape(-1, width).astype(F32)
        patch = patch.reshape(-1, width)
        self_flops = 4 * own * text * text * width
        cross_flops = 4 * own * text * slots * width

        normed_one = norm_forward(x, g_self)
        self_q = dot_nn(normed_one, w_query).astype(BF16)
        self_k = dot_nn(normed_one, w_key).astype(BF16)
        self_v = dot_nn(normed_one, w_value).astype(BF16)
        self_mix, self_norms = attend(
            self_forward_kernel, lengths, (self_q, self_k, self_v), None, own, self_flops
        )
        cot = to_examples(cotangent)
        self_branch = dot_nn(self_mix, w_out)
        after_self = x + self_branch
        normed_two = norm_forward(after_self, g_cross)
        cross_q = dot_nn(normed_two, c_query).astype(BF16)
        cross_k = dot_nn(patch, c_key).astype(BF16)
        cross_v = dot_nn(patch, c_value).astype(BF16)
        cross_mix, cross_norms = attend(
            cross_forward_kernel, counts, (cross_q, cross_k, cross_v), None, own, cross_flops
        )
        cross_branch = dot_nn(cross_mix, c_out)
        after_cross = after_self + cross_branch
        normed_three = norm_forward(after_cross, g_mlp)
        gate = dot_nn(normed_three, w_gate)
        up = dot_nn(normed_three, w_up)
        tanh_part = jnp.tanh(GELU_CURVE * (gate + 0.044715 * gate * gate * gate))
        gelu = 0.5 * gate * (1.0 + tanh_part)
        gelu_slope = 0.5 * (1.0 + tanh_part) + 0.5 * gate * (1.0 - tanh_part * tanh_part) * (
            GELU_CURVE * (1.0 + 3.0 * 0.044715 * gate * gate)
        )
        hidden_value = gelu * up
        hidden_low = hidden_value.astype(BF16)
        mlp_branch = dot_nn(hidden_low, w_down)
        layer_rows = after_cross + mlp_branch

        grad_y = cot.reshape(-1, width).astype(F32) * text_valid
        grad_mlp = grad_y.astype(BF16)
        grad_hidden = dot_nt(grad_mlp, w_down)
        grad_gate = (grad_hidden * up * gelu_slope).astype(BF16)
        grad_up = (grad_hidden * gelu).astype(BF16)
        grad_mlp_rows = (
            dot_tn(normed_three, grad_gate).astype(BF16),
            dot_tn(normed_three, grad_up).astype(BF16),
            dot_tn(hidden_low, grad_mlp).astype(BF16),
        )
        grad_three = dot_nt(grad_gate, w_gate) + dot_nt(grad_up, w_up)
        norm_grad, grad_g_mlp = norm_backward(after_cross, g_mlp, grad_three)
        grad_after_cross = grad_y + norm_grad
        grad_cbranch = grad_after_cross.astype(BF16)
        grad_cmix = dot_nt(grad_cbranch, c_out).astype(BF16)

        def square_row(valid, value):
            return jnp.sum(valid * value * value, axis=0, keepdims=True)

        lane = jnp.arange(LANES)
        valid_row = jnp.where(
            lane == 0, jnp.sum(lengths), jnp.where(lane == 1, jnp.sum(counts), 0)
        ).astype(F32)
        layer_low = layer_rows.astype(BF16)
        grad_cq, grad_ck, grad_cv = attend(
            cross_backward_kernel,
            counts,
            (cross_q, cross_k, cross_v, grad_cmix),
            cross_norms,
            own,
            cross_flops * 5 // 2,
        )
        grad_patch_rows = dot_nt(grad_ck, c_key) + dot_nt(grad_cv, c_value)
        grad_two = dot_nt(grad_cq, c_query)
        norm_grad, grad_g_cross = norm_backward(after_self, g_cross, grad_two)
        grad_after_self = grad_after_cross + norm_grad
        grad_sbranch = grad_after_self.astype(BF16)
        grad_smix = dot_nt(grad_sbranch, w_out).astype(BF16)
        grad_sq, grad_sk, grad_sv = attend(
            self_backward_kernel,
            lengths,
            (self_q, self_k, self_v, grad_smix),
            self_norms,
            own,
            self_flops * 5 // 2,
        )
        grad_one = dot_nt(grad_sq, w_query) + dot_nt(grad_sk, w_key) + dot_nt(grad_sv, w_value)
        norm_grad, grad_g_self = norm_backward(x, g_self, grad_one)
        grad_x_rows = grad_after_self + norm_grad
        layer_out = to_positions(layer_low.reshape(own, text, width))
        patch_out = to_positions(grad_patch_rows.astype(BF16).reshape(own, slots, width))
        x_out = to_positions(grad_x_rows.astype(BF16).reshape(own, text, width))
        grads = [
            dot_tn(rows, grad_rows).astype(BF16)
            for rows, grad_rows in (
                (normed_one, grad_sq),
                (normed_one, grad_sk),
                (normed_one, grad_sv),
                (self_mix, grad_sbranch),
                (normed_two, grad_cq),
                (patch, grad_ck),
                (patch, grad_cv),
                (cross_mix, grad_cbranch),
            )
        ]
        grads += grad_mlp_rows
        summed = tuple(reduce_grad(g, u % 2) for u, g in enumerate(grads))
        vectors = [
            grad_g_self,
            grad_g_cross,
            grad_g_mlp,
            square_row(text_valid, layer_rows),
            square_row(text_valid, self_branch),
            square_row(text_valid, cross_branch),
            square_row(text_valid, mlp_branch),
            square_row(text_valid, hidden_value),
            square_row(text_valid, grad_x_rows),
            square_row(patch_valid, grad_patch_rows),
            valid_row[None],
        ]
        folded = [
            sum(
                jnp.pad(p, ((0, 0), (0, width - p.shape[1])))
                for p in jnp.split(v, list(range(width, v.shape[1], width)), axis=1)
            )
            for v in vectors
        ]
        total = lax.psum(jnp.concatenate(folded), ("dp", "seq"))
    part = width // n_dp
    gains = [lax.dynamic_slice(total, (i, dp_place * part), (1, part))[0] for i in range(3)]
    squares = jnp.sum(total[3:10], axis=1)
    place = jnp.arange(7)
    texts, patch_count = total[10, 0], total[10, 1]
    per_value = jnp.where(
        place == 6, patch_count * width, jnp.where(place == 4, texts * ff_width, texts * width)
    )
    rms_values = jnp.sqrt(squares / per_value)
    return (
        layer_out.astype(F32),
        x_out.astype(F32),
        patch_out.astype(F32),
        gains[0],
        gains[1],
        gains[2],
        *summed,
        rms_values,
    )


def solution(mesh):
    rows = P("dp", "seq", None)
    tile = P("dp", "seq")
    in_specs = (rows, rows, P("dp", None), P("dp"), rows) + (P(),) * 14
    out_specs = (rows,) * 3 + (P("dp"),) * 3 + (tile,) * 11 + (P(),)
    return jax.shard_map(local, mesh=mesh, in_specs=in_specs, out_specs=out_specs, check_vma=False)
```

```python
from functools import partial
from types import SimpleNamespace
from typing import Any, NamedTuple

import jax
import jax.numpy as jnp
from jax import lax
from jax.experimental import pallas as pl
from jax.experimental.pallas import tpu as pltpu
from jax.sharding import PartitionSpec as P

HEAD_DIM = 64
LANES = 128
PAIR = LANES // HEAD_DIM
NORM_EPS = 1e-06
NEG_FILL = -1e30
GELU_CURVE = 0.7978845608028654
F32 = jnp.float32
BF16 = jnp.bfloat16
MESH = pl.DeviceIdType.MESH
VMEM_LIMIT = 48 * 1024 * 1024
TAIL_VMEM = 63 * 1024 * 1024
HELD_BACK = 2


def dot_nn(a, b):
    return lax.dot_general(a, b, (((1,), (0,)), ((), ())), preferred_element_type=F32)


def dot_nt(a, b):
    return lax.dot_general(a, b, (((1,), (1,)), ((), ())), preferred_element_type=F32)


def dot_tn(a, b):
    return lax.dot_general(a, b, (((0,), (0,)), ((), ())), preferred_element_type=F32)


def head_mask(h, dtype):
    lane = lax.broadcasted_iota(jnp.int32, (1, LANES), 1)
    return ((lane // HEAD_DIM) == h).astype(F32).astype(dtype)


def masked(scores, limit, causal):
    if limit is None:
        return scores
    key_pos = lax.broadcasted_iota(jnp.int32, scores.shape, 0)
    allowed = key_pos < limit
    if causal:
        queries = scores.shape[1] // PAIR
        query_pos = lax.broadcasted_iota(jnp.int32, scores.shape, 1)
        query_pos = jnp.where(query_pos < queries, query_pos, query_pos - queries)
        allowed = allowed & (key_pos <= query_pos)
    return jnp.where(allowed, scores, NEG_FILL)


def stacked(rows, factor):
    return jnp.concatenate([rows * (head_mask(h, BF16) * factor) for h in range(PAIR)], axis=0)


def own_rows(value, queries):
    parts = [
        value[h * HEAD_DIM : (h + 1) * HEAD_DIM, h * queries : (h + 1) * queries]
        for h in range(PAIR)
    ]
    return jnp.concatenate(parts, axis=0).T.astype(BF16)


def forward_pair(q, k, v, limit, causal):
    queries = q.shape[0]
    scores = masked(dot_nt(k, stacked(q, 0.125)), limit, causal)
    top = jnp.max(scores, axis=0, keepdims=True)
    exps = jnp.exp(scores - top)
    total = jnp.sum(exps, axis=0, keepdims=True)
    mixed = dot_nn(v.T, exps.astype(BF16)) / total
    norms = top + jnp.log(total)
    norms = jnp.concatenate([norms[:, :queries], norms[:, queries:]], axis=0)
    return own_rows(mixed, queries), norms


def backward_pair(q, k, v, grad_mix, norms, limit, causal):
    queries = q.shape[0]
    q_both, grad_both = stacked(q, 0.125), stacked(grad_mix, 1.0)
    norm_row = jnp.concatenate([norms[h : h + 1] for h in range(PAIR)], axis=1)
    probs = jnp.exp(masked(dot_nt(k, q_both), limit, causal) - norm_row)
    grad_v = dot_nn(probs.astype(BF16), grad_both)
    grad_p = dot_nt(v, grad_both)
    inner = jnp.sum(probs * grad_p, axis=0, keepdims=True)
    grad_s = (probs * (grad_p - inner)).astype(BF16)
    grad_k = dot_nn(grad_s, q_both)
    grad_q = dot_nn(k.T * 0.125, grad_s)
    return own_rows(grad_q, queries), grad_k.astype(BF16), grad_v.astype(BF16)


def self_forward_kernel(limit_ref, q_ref, k_ref, v_ref, mix_ref, norm_ref):
    limit = limit_ref[pl.program_id(0)]
    mix, norms = forward_pair(q_ref[...], k_ref[...], v_ref[...], limit, True)
    mix_ref[...] = mix
    norm_ref[0, 0, 0:PAIR] = norms


def self_backward_kernel(
    limit_ref, q_ref, k_ref, v_ref, grad_ref, norm_ref, dq_ref, dk_ref, dv_ref
):
    limit = limit_ref[pl.program_id(0)]
    dq, dk, dv = backward_pair(
        q_ref[...], k_ref[...], v_ref[...], grad_ref[...], norm_ref[0, 0, 0:PAIR], limit, True
    )
    dq_ref[...] = dq
    dk_ref[...] = dk
    dv_ref[...] = dv


def cross_forward_kernel(limit_ref, q_ref, k_ref, v_ref, mix_ref, norm_ref):
    limit = limit_ref[pl.program_id(0)]
    keys = k_ref.shape[0]
    short = keys // 4

    def run(count):
        mix, norms = forward_pair(q_ref[...], k_ref[0:count], v_ref[0:count], None, False)
        mix_ref[...] = mix
        norm_ref[0, 0, 0:PAIR] = norms

    pl.when(limit > short)(lambda: run(keys))
    pl.when(limit <= short)(lambda: run(short))


def cross_backward_kernel(
    limit_ref, q_ref, k_ref, v_ref, grad_ref, norm_ref, dq_ref, dk_ref, dv_ref
):
    limit = limit_ref[pl.program_id(0)]
    keys = k_ref.shape[0]
    short = keys // 4

    def run(count):
        dq, dk, dv = backward_pair(
            q_ref[...],
            k_ref[0:count],
            v_ref[0:count],
            grad_ref[...],
            norm_ref[0, 0, 0:PAIR],
            None,
            False,
        )
        dq_ref[...] = dq
        dk_ref[0:count] = dk
        dv_ref[0:count] = dv
        if count < keys:
            dk_ref[count:] = jnp.zeros((keys - count, LANES), BF16)
            dv_ref[count:] = jnp.zeros((keys - count, LANES), BF16)

    pl.when(limit > short)(lambda: run(keys))
    pl.when(limit <= short)(lambda: run(short))


def attend(kernel, limits, arrays, norms, examples, flops):
    width = arrays[0].shape[1]
    pairs = width // LANES
    queries = arrays[0].shape[0] // examples

    def rows_spec(array):
        return pl.BlockSpec((array.shape[0] // examples, LANES), lambda e, p: (e, p))

    norm_spec = pl.BlockSpec((1, 1, 8, queries), lambda e, p: (e, p, 0, 0))
    norm_shape = jax.ShapeDtypeStruct((examples, pairs, 8, queries), F32)
    in_specs = [pl.BlockSpec(memory_space=pltpu.SMEM)] + [rows_spec(a) for a in arrays]
    args = (limits,) + tuple(arrays)
    if norms is None:
        out_shape = (jax.ShapeDtypeStruct(arrays[0].shape, BF16), norm_shape)
        out_specs = (rows_spec(arrays[0]), norm_spec)
    else:
        in_specs.append(norm_spec)
        args = args + (norms,)
        out_shape = tuple(jax.ShapeDtypeStruct(a.shape, BF16) for a in arrays[:3])
        out_specs = tuple(rows_spec(a) for a in arrays[:3])
    return pl.pallas_call(
        kernel,
        grid=(examples, pairs),
        in_specs=in_specs,
        out_specs=out_specs,
        out_shape=out_shape,
        compiler_params=pltpu.CompilerParams(vmem_limit_bytes=VMEM_LIMIT),
        cost_estimate=pl.CostEstimate(
            flops=flops, bytes_accessed=sum(a.size * 2 for a in arrays), transcendentals=0
        ),
    )(*args)


class HeadState(NamedTuple):
    self_q: Any
    self_k: Any
    self_v: Any
    self_mix: Any
    normed_one: Any
    hidden: Any
    after_self: Any
    grad_after_cross: Any
    queries: Any
    normed_two: Any
    normed_three: Any
    grad_mlp: Any
    mlp_hidden: Any
    grad_gate: Any
    grad_up: Any
    self_norms: Any
    grad_mix: Any
    cross_norms: Any
    grad_k_early: Any
    grad_v_early: Any
    patch_early: Any
    k_late: Any
    v_late: Any
    patch_rows_late: Any
    layer: Any
    patch_grad_early: Any
    dw_c_out: Any


def head_kernel(*refs):
    lengths_ref, counts_ref, g_self_ref, g_cross_ref, g_mlp_ref = refs[:5]
    hidden_in, patches_in, cot_in = refs[5:8]
    weights_in = refs[8:19]
    refs = refs[19:]
    small, patch_out = refs[:2]
    n_state = len(HeadState._fields)
    kept = HeadState(*refs[2 : 2 + n_state])
    (
        hidden,
        cot,
        patch,
        normed_one,
        self_rows,
        after_self,
        normed_two,
        queries,
        keys,
        values,
        cmix,
        normed_three,
        mlp_rows,
        grad_after,
        cbranch,
        grad_mix,
        patch_send,
        layer,
        after_cross,
        mlp_sum,
        grad_three,
        squares,
        w_gate,
        w_up,
        w_down,
        self_norms,
        cross_norms,
        weight_sem,
        in_send,
        in_recv,
        in_local,
        out_send,
        out_recv,
        out_local,
        keep_sem,
    ) = refs[2 + n_state :]
    own = 2
    rows, width = hidden.shape
    text = rows // own
    slots = patch.shape[0] // own
    part, patch_part = text // 4, slots // 4
    pairs = width // LANES
    dp = lax.axis_index("dp")
    seq = lax.axis_index("seq")
    near_seq = seq + 1 - 2 * (seq % 2)
    far_seq = seq + 2 - 4 * (seq // 2)
    seq_peers = [far_seq, near_seq, 3 - seq]
    lengths = [lengths_ref[own * seq + e] for e in range(own)]
    counts = [counts_ref[own * seq + e] for e in range(own)]

    barrier = pltpu.get_barrier_semaphore()
    for z in seq_peers:
        pl.semaphore_signal(barrier, inc=1, device_id=(dp, z), device_id_type=MESH)
    pl.semaphore_wait(barrier, len(seq_peers))

    incoming = {}

    def receive(number, src, dst, size, e):
        first = pl.multiple_of(e * 4 * size + seq * size, size)
        copies = []
        for k, z in enumerate(seq_peers):
            copy = pltpu.make_async_remote_copy(
                src_ref=src.at[own * z + e],
                dst_ref=dst.at[pl.ds(first, size)],
                send_sem=in_send.at[number, k],
                recv_sem=in_recv.at[number, k],
                device_id=(dp, z),
                device_id_type=MESH,
            )
            copy.start()
            copies.append(copy)
        local_copy = pltpu.make_async_copy(
            src.at[own * seq + e], dst.at[pl.ds(first, size)], in_local.at[number]
        )
        local_copy.start()
        incoming[number] = (copies, local_copy)

    def arrived(number):
        copies, local_copy = incoming[number]
        local_copy.wait()
        for copy in copies:
            copy.wait_recv()

    receive(0, hidden_in, hidden, part, 0)
    receive(1, hidden_in, hidden, part, 1)
    receive(2, patches_in, patch, patch_part, 0)

    loads = []
    targets = [squares.at[i] for i in range(8)] + [w_gate, w_up, w_down]
    for i, (src, dst) in enumerate(zip(weights_in, targets)):
        copy = pltpu.make_async_copy(src, dst, weight_sem.at[i])
        copy.start()
        loads.append(copy)
    WQ, WK, WV, WO, CQ, CK, CV, CO = range(8)

    keeping = []

    def keep(dst, src):
        copy = pltpu.make_async_copy(src, dst, keep_sem.at[len(keeping)])
        copy.start()
        keeping.append(copy)

    small[...] = jnp.zeros(small.shape, F32)
    lane = lax.broadcasted_iota(jnp.int32, (1, width), 1)
    small[10:11] = jnp.where(
        lane == 0, lengths[0] + lengths[1], jnp.where(lane == 1, counts[0] + counts[1], 0)
    ).astype(F32)

    def add_row(i, value):
        small[i : i + 1, 0 : value.shape[1]] += value

    def valid_rows(e):
        position = lax.broadcasted_iota(jnp.int32, (text, 1), 0)
        return (position < lengths[e]).astype(F32)

    def squared(valid, value):
        return jnp.sum(valid * value * value, axis=0, keepdims=True)

    def norm(u, gain):
        r = lax.rsqrt(jnp.mean(u * u, axis=-1, keepdims=True) + NORM_EPS)
        return (u * r * gain).astype(BF16)

    arrived(0)
    arrived(1)
    for i in (WQ, WK, WV):
        loads[i].wait()
    for e in range(own):
        at = slice(e * text, (e + 1) * text)
        normed_one[at] = norm(hidden[at].astype(F32), g_self_ref[...].reshape(1, width))
        for i in (WQ, WK, WV):
            self_rows[i, at] = dot_nn(normed_one[at], squares[i]).astype(BF16)

    def self_pair(step, carry):
        e, p = step // pairs, step % pairs
        at = pl.ds(pl.multiple_of(e * text, text), text)
        lanes = pl.ds(pl.multiple_of(p * LANES, LANES), LANES)
        limit = lengths_ref[own * seq + e]
        mix, norms = forward_pair(
            self_rows[0, at, lanes], self_rows[1, at, lanes], self_rows[2, at, lanes], limit, True
        )
        self_rows[3, at, lanes] = mix
        self_norms[e, p, 0:PAIR] = norms
        return carry

    lax.fori_loop(0, own * pairs, self_pair, 0)
    receive(4, cot_in, cot, part, 0)
    receive(3, patches_in, patch, patch_part, 1)
    loads[WO].wait()
    loads[CQ].wait()
    for e in range(own):
        at = slice(e * text, (e + 1) * text)
        branch = dot_nn(self_rows[3, at], squares[WO])
        add_row(4, squared(valid_rows(e), branch))
        after = hidden[at].astype(F32) + branch
        after_self[at] = after
        normed_two[at] = norm(after, g_cross_ref[...].reshape(1, width))
        queries[at] = dot_nn(normed_two[at], squares[CQ]).astype(BF16)
    for i, dst in enumerate((kept.self_q, kept.self_k, kept.self_v, kept.self_mix)):
        keep(dst, self_rows.at[i])
    keep(kept.normed_one, normed_one)
    keep(kept.hidden, hidden)
    keep(kept.after_self, after_self)
    keep(kept.self_norms, self_norms)

    def project_patches(e):
        def body(i, carry):
            at = pl.ds(pl.multiple_of(e * slots + i * patch_part, patch_part), patch_part)
            keys[at] = dot_nn(patch[at], squares[CK]).astype(BF16)
            values[at] = dot_nn(patch[at], squares[CV]).astype(BF16)
            return carry

        lax.fori_loop(0, 4, body, 0)

    def cross_forward(e):
        at, key_at = slice(e * text, (e + 1) * text), slice(e * slots, (e + 1) * slots)

        def body(p, carry):
            lanes = pl.ds(pl.multiple_of(p * LANES, LANES), LANES)
            mix, norms = forward_pair(
                queries[at, lanes], keys[key_at, lanes], values[key_at, lanes], counts[e], False
            )
            cmix[at, lanes] = mix
            cross_norms[e, p, 0:PAIR] = norms
            return carry

        lax.fori_loop(0, pairs, body, 0)

    def feed_forward(e):
        at = slice(e * text, (e + 1) * text)
        valid = valid_rows(e)
        branch = dot_nn(cmix[at], squares[CO])
        add_row(5, squared(valid, branch))
        after = after_self[at] + branch
        after_cross[...] = after
        normed_three[at] = norm(after, g_mlp_ref[...].reshape(1, width))
        arrived(4 + e)
        cot[at] = (cot[at].astype(F32) * valid).astype(BF16)
        mlp_sum[...] = jnp.zeros((text, width), F32)
        grad_three[...] = jnp.zeros((text, width), F32)
        step = w_gate.shape[1] // 4

        def body(i, total):
            columns = pl.ds(pl.multiple_of(i * step, step), step)
            gate = dot_nn(normed_three[at], w_gate[:, columns])
            up = dot_nn(normed_three[at], w_up[:, columns])
            tanh_part = jnp.tanh(GELU_CURVE * (gate + 0.044715 * gate * gate * gate))
            gelu = 0.5 * gate * (1.0 + tanh_part)
            slope = 0.5 * (1.0 + tanh_part) + 0.5 * gate * (1.0 - tanh_part * tanh_part) * (
                GELU_CURVE * (1.0 + 3.0 * 0.044715 * gate * gate)
            )
            value = gelu * up
            low_value = value.astype(BF16)
            mlp_rows[0, at, columns] = low_value
            mlp_sum[...] += dot_nn(low_value, w_down[columns, :])
            grad_value = dot_nt(cot[at], w_down[columns, :])
            grad_gate = (grad_value * up * slope).astype(BF16)
            grad_up = (grad_value * gelu).astype(BF16)
            mlp_rows[1, at, columns] = grad_gate
            mlp_rows[2, at, columns] = grad_up
            grad_three[...] += dot_nt(grad_gate, w_gate[:, columns]) + dot_nt(
                grad_up, w_up[:, columns]
            )
            return total + squared(valid, value)

        add_row(7, lax.fori_loop(0, 4, body, jnp.zeros((1, step), F32)))
        mlp_branch = mlp_sum[...]
        add_row(6, squared(valid, mlp_branch))
        after = after_cross[...]
        out = after + mlp_branch
        add_row(3, squared(valid, out))
        layer[at] = out.astype(BF16)
        w = grad_three[...]
        r = lax.rsqrt(jnp.mean(after * after, axis=-1, keepdims=True) + NORM_EPS)
        gw = g_mlp_ref[...].reshape(1, width) * w
        add_row(2, jnp.sum(w * after * r, axis=0, keepdims=True))
        grad = r * gw - after * (r * r * r) * jnp.mean(gw * after, axis=-1, keepdims=True)
        grad = cot[at].astype(F32) + grad
        grad_after[at] = grad
        cbranch[at] = grad.astype(BF16)
        grad_mix[at] = dot_nt(cbranch[at], squares[CO]).astype(BF16)

    def cross_backward(e):
        at, key_at = slice(e * text, (e + 1) * text), slice(e * slots, (e + 1) * slots)

        def body(p, carry):
            lanes = pl.ds(pl.multiple_of(p * LANES, LANES), LANES)
            dq, dk, dv = backward_pair(
                queries[at, lanes],
                keys[key_at, lanes],
                values[key_at, lanes],
                grad_mix[at, lanes],
                cross_norms[e, p, 0:PAIR],
                counts[e],
                False,
            )
            queries[at, lanes] = dq
            keys[key_at, lanes] = dk
            values[key_at, lanes] = dv
            return carry

        lax.fori_loop(0, pairs, body, 0)

    def patch_grads(e):
        def body(d, total):
            first = pl.multiple_of(d * patch_part, patch_part)
            at = pl.ds(e * slots + first, patch_part)
            value = dot_nt(keys[at], squares[CK]) + dot_nt(values[at], squares[CV])
            position = lax.broadcasted_iota(jnp.int32, (patch_part, 1), 0) + first
            patch_send[d] = value.astype(BF16)
            return total + squared((position < counts[e]).astype(F32), value)

        add_row(9, lax.fori_loop(0, 4, body, jnp.zeros((1, width), F32)))

    def keep_rows(e):
        at = pl.ds(e * text, text)
        for i, dst in enumerate((kept.mlp_hidden, kept.grad_gate, kept.grad_up)):
            keep(dst.at[at], mlp_rows.at[i, at])
        for dst, src in (
            (kept.grad_mlp, cot),
            (kept.normed_three, normed_three),
            (kept.grad_after_cross, grad_after),
            (kept.layer, layer),
        ):
            keep(dst.at[at], src.at[at])

    outgoing = []

    def send_rows(src_of, dst, number):
        for k, z in enumerate(seq_peers):
            copy = pltpu.make_async_remote_copy(
                src_ref=src_of(z),
                dst_ref=dst.at[seq],
                send_sem=out_send.at[number, k],
                recv_sem=out_recv.at[number, k],
                device_id=(dp, z),
                device_id_type=MESH,
            )
            copy.start()
            outgoing.append(copy)
        local_copy = pltpu.make_async_copy(src_of(seq), dst.at[seq], out_local.at[number])
        local_copy.start()
        keeping.append(local_copy)

    arrived(2)
    for copy in loads[CK:]:
        copy.wait()
    project_patches(0)
    cross_forward(0)
    feed_forward(0)
    keep_rows(0)
    cross_backward(0)
    receive(5, cot_in, cot, part, 1)
    patch_grads(0)
    split = patch_part - patch_part // HELD_BACK
    keep(kept.patch_grad_early, patch_send.at[:, split:patch_part])
    keep(kept.grad_k_early, keys.at[0:slots])
    keep(kept.grad_v_early, values.at[0:slots])
    keep(kept.patch_early, patch.at[0:slots])
    keep(kept.normed_two, normed_two)
    arrived(3)
    send_rows(lambda z: patch_send.at[z, 0:split], patch_out, 0)
    project_patches(1)
    keep(kept.k_late, keys.at[slots : 2 * slots])
    keep(kept.v_late, values.at[slots : 2 * slots])
    keep(kept.patch_rows_late, patch.at[slots : 2 * slots])
    cross_forward(1)
    keep(kept.queries, queries)
    keep(kept.cross_norms, cross_norms.at[1])
    feed_forward(1)
    keep_rows(1)
    keep(kept.grad_mix, grad_mix.at[text : 2 * text])

    for i in range(2):
        columns = slice(i * (width // 2), (i + 1) * (width // 2))
        squares[0, columns] = dot_tn(cmix[:, columns], cbranch[...]).astype(BF16)
    keep(kept.dw_c_out, squares.at[0])
    for copies, local_copy in incoming.values():
        for copy in copies:
            copy.wait_send()
    for copy in outgoing:
        copy.wait()
    for copy in keeping:
        copy.wait()


def forward_head(lengths, counts, gains, rows, weights):
    examples, part, width = rows[0].shape
    patch_part = rows[1].shape[1]
    own = examples // 4
    text, slots = 4 * part, 4 * patch_part
    count, key_count = own * text, own * slots
    ff_width = weights[8].shape[1]
    pairs = width // LANES
    norms = (own, pairs, 8, text)
    vmem = pl.BlockSpec(memory_space=pltpu.VMEM)
    anywhere = pl.BlockSpec(memory_space=pl.ANY)
    smem = pl.BlockSpec(memory_space=pltpu.SMEM)
    rows_low = jax.ShapeDtypeStruct((count, width), BF16)
    rows_wide = jax.ShapeDtypeStruct((count, width), F32)
    rows_ff = jax.ShapeDtypeStruct((count, ff_width), BF16)
    keys_low = jax.ShapeDtypeStruct((slots, width), BF16)
    late_low = jax.ShapeDtypeStruct((text, width), BF16)
    state = HeadState(*[rows_low] * len(HeadState._fields))._replace(
        after_self=rows_wide,
        grad_after_cross=rows_wide,
        mlp_hidden=rows_ff,
        grad_gate=rows_ff,
        grad_up=rows_ff,
        self_norms=jax.ShapeDtypeStruct(norms, F32),
        cross_norms=jax.ShapeDtypeStruct(norms[1:], F32),
        grad_k_early=keys_low,
        grad_v_early=keys_low,
        patch_early=keys_low,
        k_late=keys_low,
        v_late=keys_low,
        patch_rows_late=keys_low,
        grad_mix=late_low,
        dw_c_out=jax.ShapeDtypeStruct((width, width), BF16),
        patch_grad_early=jax.ShapeDtypeStruct((4, patch_part // HELD_BACK, width), BF16),
    )

    def low(*shape):
        return pltpu.VMEM(shape, BF16)

    def wide(*shape):
        return pltpu.VMEM(shape, F32)

    outs = pl.pallas_call(
        head_kernel,
        out_shape=(
            jax.ShapeDtypeStruct((16, width), F32),
            jax.ShapeDtypeStruct((4, patch_part - patch_part // HELD_BACK, width), BF16),
            *state,
        ),
        in_specs=[smem] * 2 + [vmem] * 3 + [anywhere] * 14,
        out_specs=(vmem,) + (anywhere,) * (1 + len(state)),
        scratch_shapes=[
            low(count, width),
            low(count, width),
            low(key_count, width),
            low(count, width),
            low(4, count, width),
            wide(count, width),
            low(count, width),
            low(count, width),
            low(key_count, width),
            low(key_count, width),
            low(count, width),
            low(count, width),
            low(3, count, ff_width),
            wide(count, width),
            low(count, width),
            low(count, width),
            low(4, patch_part, width),
            low(count, width),
            wide(text, width),
            wide(text, width),
            wide(text, width),
            low(8, width, width),
            low(width, ff_width),
            low(width, ff_width),
            low(ff_width, width),
            wide(*norms),
            wide(*norms),
            pltpu.SemaphoreType.DMA((11,)),
            pltpu.SemaphoreType.DMA((6, 3)),
            pltpu.SemaphoreType.DMA((6, 3)),
            pltpu.SemaphoreType.DMA((6,)),
            pltpu.SemaphoreType.DMA((1, 3)),
            pltpu.SemaphoreType.DMA((1, 3)),
            pltpu.SemaphoreType.DMA((1,)),
            pltpu.SemaphoreType.DMA((len(state) + 9,)),
        ],
        compiler_params=pltpu.CompilerParams(
            collective_id=1, has_side_effects=True, vmem_limit_bytes=TAIL_VMEM
        ),
    )(lengths, counts, *gains, *rows, *weights)
    return outs[0], outs[1], HeadState(*outs[2:])


(
    GATE,
    UP,
    CROSS_A,
    CROSS_B,
    PATCHES,
    KEYS,
    C_QUERY,
    C_KEY,
    C_VALUE,
    LOADS,
    MIDDLE,
    W_OUT,
    SELF_A,
    SELF_B,
    LAST,
    W_QUERY,
    W_KEY,
    W_VALUE,
) = range(18)
CORE, GO, TWO, THREE, NEAR, FAR, SMALL = range(7)
TAIL_ORDER = (
    GATE, (CORE, 3), UP, (GO, 3), (CORE, 2), (GO, 2), CROSS_A, (CORE, 0), (GO, 0), CROSS_B, C_QUERY,
    LOADS, (CORE, 1), (GO, 1), MIDDLE, (CORE, 4), (GO, 4), PATCHES, SELF_A, (TWO, 2), SELF_B, (TWO, 3),
    (TWO, 4), (TWO, 0), W_QUERY, W_KEY, W_VALUE, (TWO, 1), KEYS, W_OUT, (CORE, 8), (THREE, 1),
    (CORE, 10), (CORE, 7), (GO, 7), (GO, 8), C_KEY, (GO, 10), (THREE, 2), C_VALUE, (CORE, 9), (NEAR, 1),
    (CORE, 5), (GO, 9), (GO, 5), (THREE, 0), (NEAR, 2), (CORE, 6), (GO, 6), LAST, (TWO, 8), (TWO, 7),
    (TWO, 9), (SMALL, 0), (NEAR, 0), (TWO, 10), (TWO, 6), (SMALL, 1), (TWO, 5), (THREE, 4), (THREE, 5),
    (SMALL, 2), (THREE, 3), (NEAR, 4), (NEAR, 5), (SMALL, 3), (FAR, 0), (NEAR, 3), (FAR, 1), (FAR, 4),
    (FAR, 5), (FAR, 2), (FAR, 3), (SMALL, 4),
)
Y_FIRST = (1, 2, 6, 8, 9)


def tail_kernel(lengths_ref, counts_ref, g_self_ref, g_cross_ref, small_in, *refs):
    n_state = len(HeadState._fields)
    hbm = HeadState(*refs[:n_state])
    c_key, c_value, c_query, w_out, w_query, w_key, w_value = refs[n_state : n_state + 7]
    refs = refs[n_state + 7 :]
    narrow, wide, small_out, early_out, patch_out, x_out, layer_out, layer_late_out = refs[:8]
    (
        after_self,
        grad_after,
        queries,
        normed,
        normed_two,
        mlp_rows,
        grad_mlp,
        big,
        grad_mix,
        cross_norms,
        self_norms,
        weights,
        wide_units,
        tall_units,
        wide_core,
        tall_core,
        wide_two,
        tall_two,
        wide_three,
        tall_three,
        square,
        square_core,
        square_two,
        square_three,
        cut_narrow,
        near_narrow,
        far_narrow,
        cut_wide,
        near_wide,
        far_wide,
        small_own,
        small_got,
        load_sem,
        send_sem,
        recv_sem,
        small_send,
        small_recv,
        cut_send,
        cut_recv,
        out_send,
        out_recv,
        out_local,
    ) = refs[8:]
    width = queries.shape[1]
    block = width // 8
    text = self_norms.shape[3]
    own = 2
    pairs = width // LANES
    part = text // 4

    dp = lax.axis_index("dp")
    seq = lax.axis_index("seq")
    core, x, y = dp % 2, (dp // 2) % 2, dp // 4
    low, high = seq % 2, seq // 2
    to_core = (dp + 1 - 2 * core, seq)
    to_x = (dp + 2 - 4 * x, seq)
    to_y = (dp + 4 - 8 * y, seq)
    near_seq = seq + 1 - 2 * low
    far_seq = seq + 2 - 4 * high
    last_seq = 3 - seq
    seq_peers = [near_seq, far_seq, last_seq]
    to_near, to_far = (dp, near_seq), (dp, far_seq)
    peers = [to_core, to_x, to_y, to_near, to_far, (dp, last_seq)]

    barrier = pltpu.get_barrier_semaphore()
    for peer in peers:
        pl.semaphore_signal(barrier, inc=1, device_id=peer, device_id_type=MESH)

    got, waited = SimpleNamespace(count=0), set()

    def need(*copies):
        for copy in copies:
            if id(copy) not in waited:
                copy.wait()
                waited.add(id(copy))

    def load(src, dst):
        copy = pltpu.make_async_copy(src, dst, load_sem.at[got.count])
        copy.start()
        got.count += 1
        return copy

    slots = big.shape[0] // 4
    patch_part = slots // 4
    keys, values, patch, patch_send = (big.at[i * slots : (i + 1) * slots] for i in range(4))
    self_q, self_k, self_v, self_mix, hidden, sbranch = (
        mlp_rows.at[i // 2, :, i % 2 * width : (i % 2 + 1) * width] for i in range(6)
    )
    grad_smix = normed_two
    got.mlp_hidden = load(hbm.mlp_hidden, mlp_rows.at[0])
    got.grad_mlp = load(hbm.grad_mlp, grad_mlp)
    got.normed = load(hbm.normed_three, normed)
    got.grad_gate = load(hbm.grad_gate, mlp_rows.at[1])
    got.grad_up = load(hbm.grad_up, mlp_rows.at[2])
    got.dw_c_out = load(hbm.dw_c_out.at[:, :, core], square.at[0])
    got.queries = load(hbm.queries, queries)
    got.keys = load(hbm.k_late, keys)
    got.values = load(hbm.v_late, values)
    got.grad_mix = load(hbm.grad_mix, grad_mix)
    got.cross_norms = load(hbm.cross_norms, cross_norms)
    got.c_key = load(c_key, weights.at[0])
    got.c_value = load(c_value, weights.at[1])
    got.patch = load(hbm.patch_rows_late, patch)
    got.normed_two = load(hbm.normed_two, normed_two)
    got.after_self = load(hbm.after_self, after_self)
    got.grad_after = load(hbm.grad_after_cross, grad_after)
    got.c_query = load(c_query, weights.at[2])
    got.w_out = load(w_out, weights.at[3])
    got.self_norms = load(hbm.self_norms, self_norms)

    small_own[0] = small_in[...]

    def add_row(i, value):
        small_own[0, i : i + 1] += value

    def remote(src, dst, send, recv, device):
        copy = pltpu.make_async_remote_copy(
            src_ref=src,
            dst_ref=dst,
            send_sem=send,
            recv_sem=recv,
            device_id=device,
            device_id_type=MESH,
        )
        copy.start()
        return copy

    n_square = square_core.shape[0]
    y_first = Y_FIRST
    first, second, third, near, far, small = {}, {}, {}, {}, {}, {}
    got_core = [wide_core.at[0], wide_core.at[1], tall_core]
    got_core += [square_core.at[i] for i in range(n_square)]
    got_two = [wide_two.at[0], wide_two.at[1], tall_two]
    got_two += [square_two.at[i] for i in range(n_square)]
    got_three = [wide_three.at[0], wide_three.at[1], tall_three]
    got_three += [square_three.at[i] for i in range(n_square)]
    current = [wide_units.at[0], wide_units.at[1], tall_units.at[0]]
    current += [square.at[i] for i in range(n_square)]
    def add(out, got):
        rows = out.shape[0]
        step = 32

        def body(i, carry):
            at = pl.ds(pl.multiple_of(i * step, step), step)
            out[at, :] = (out[at, :].astype(F32) + got[at, :].astype(F32)).astype(BF16)
            return carry

        lax.fori_loop(0, rows // step, body, 0)

    def over_core(u):
        if u == 3:
            need(got.dw_c_out)
        first[u].wait_recv()
        for i in range(2):
            for j in range(2):
                add(current[u].at[i, j], got_core[u].at[i, j])

    def leave_two(u):
        cur = current[u]
        src, device = (cur.at[1 - y], to_y) if u in y_first else (cur.at[:, 1 - x], to_x)
        second[u] = remote(src, got_two[u], send_sem.at[1, u], recv_sem.at[1, u], device)

    def over_two(u):
        second[u].wait_recv()
        cur = current[u]
        for i in range(2):
            add(cur.at[y, i] if u in y_first else cur.at[i, x], got_two[u].at[i])
        src, device = (cur.at[y, 1 - x], to_x) if u in y_first else (cur.at[1 - y, x], to_y)
        third[u] = remote(src, got_three[u], send_sem.at[2, u], recv_sem.at[2, u], device)

    groups = [(1, 0, block, (0, 1)), (0, n_square // 2 * block, tall_three.shape[0] // 2, (2,))]
    groups += [(0, i * block, block, (3 + 2 * i, 4 + 2 * i)) for i in range(n_square // 2)]
    cut, got_near, got_far = (cut_narrow, cut_wide), (near_narrow, near_wide), (far_narrow, far_wide)
    totals = (narrow, wide)

    def over_three(g):
        buffer, row, rows, members = groups[g]
        for u in members:
            third[u].wait_recv()
        halves = [current[u][y, x].astype(F32) + got_three[u][...].astype(F32) for u in members]
        if len(members) == 1:
            halves = [halves[0][:rows], halves[0][rows:]]
        piece = halves[0].shape[1] // 4
        at = pl.ds(row, rows)
        for z in range(4):
            columns = [h[:, z * piece : (z + 1) * piece] for h in halves]
            cut[buffer][z // 2, z % 2, at] = jnp.concatenate(columns, axis=1).astype(BF16)
        near[g] = remote(
            cut[buffer].at[:, 1 - low, at],
            got_near[buffer].at[:, at],
            cut_send.at[0, g],
            cut_recv.at[0, g],
            to_near,
        )

    def over_near(g):
        buffer, row, rows, _ = groups[g]
        near[g].wait_recv()
        at = pl.ds(row, rows)
        for i in range(2):
            add(cut[buffer].at[i, low, at], got_near[buffer].at[i, at])
        far[g] = remote(
            cut[buffer].at[1 - high, low, at],
            got_far[buffer].at[at],
            cut_send.at[1, g],
            cut_recv.at[1, g],
            to_far,
        )

    def over_far(g):
        buffer, row, rows, _ = groups[g]
        far[g].wait_recv()
        at = pl.ds(row, rows)
        totals[buffer][at] = cut[buffer][high, low, at].astype(F32) + got_far[buffer][at].astype(F32)

    def give(u, src):
        first[u] = remote(src, got_core[u], send_sem.at[0, u], recv_sem.at[0, u], to_core)

    def weight_grad(i, rows, grad_rows, more=None):
        ring = n_square + len(ring_units) % 2
        if len(ring_units) >= 2:
            first[ring_units[-2]].wait_send()
            first_sent.add(ring_units[-2])
        ring_units.append(3 + i)
        half = width // 2
        for h in range(2):
            value = dot_tn(rows[:, h * half : (h + 1) * half], grad_rows[...])
            if more is not None:
                value = value + more[h * half : (h + 1) * half].astype(F32)
            value = value.astype(BF16)
            for j in range(4):
                at = i + ((j + core) % 2) * (ring - i)
                square[at, h, j // 2] = value[j * block : (j + 1) * block]
        give(3 + i, square.at[ring])

    def wide_grad(u):
        if u == 1:
            first[0].wait_send()
            first_sent.add(0)
        half, step = width // 2, wide_units.shape[4] // 4

        def body(i, carry):
            columns = pl.ds(pl.multiple_of(i * step, step), step)
            for h in range(2):
                value = dot_tn(
                    normed[:, h * half : (h + 1) * half], mlp_rows[1 + u, :, columns]
                ).astype(BF16)
                for j in range(4):
                    at = u + ((j + core) % 2) * (2 - u)
                    wide_units[at, h, j // 2, :, columns] = value[j * block : (j + 1) * block]
            return carry

        lax.fori_loop(0, 4, body, 0)
        give(u, wide_units.at[2])

    def tall_grad():
        rows = tall_units.shape[3]

        def body(j, carry):
            columns = pl.ds(pl.multiple_of(j * rows, rows), rows)
            value = dot_tn(mlp_rows[0, :, columns], grad_mlp[...]).astype(BF16)
            tall_units[(j + core) % 2, j // 4, (j // 2) % 2] = value
            return carry

        lax.fori_loop(0, 8, body, 0)

    first_sent, ring_units = set(), []

    outs, locals_ = [], []

    def send_rows(src_of, dst, number):
        for k, z in enumerate([far_seq, near_seq, last_seq]):
            outs.append(
                remote(src_of(z), dst, out_send.at[number, k], out_recv.at[number, k], (dp, z))
            )
        copy = pltpu.make_async_copy(src_of(seq), dst, out_local.at[number])
        copy.start()
        locals_.append(copy)

    chunk = own * text // 4
    late = slice(text, 2 * text)
    limit = counts_ref[own * seq + 1]

    def cross_pairs(first_pair, last_pair):
        def body(p, carry):
            lanes = pl.ds(pl.multiple_of(p * LANES, LANES), LANES)
            dq, dk, dv = backward_pair(
                queries[late, lanes],
                keys[:, lanes],
                values[:, lanes],
                grad_mix[:, lanes],
                cross_norms[p, 0:PAIR],
                limit,
                False,
            )
            queries[late, lanes] = dq
            keys[:, lanes] = dk
            values[:, lanes] = dv
            return carry

        lax.fori_loop(first_pair, last_pair, body, 0)

    def patch_grads():
        def body(d, total):
            at = pl.ds(pl.multiple_of(d * patch_part, patch_part), patch_part)
            value = dot_nt(keys[at, :], weights[0]) + dot_nt(values[at, :], weights[1])
            position = lax.broadcasted_iota(jnp.int32, (patch_part, 1), 0) + d * patch_part
            patch_send[at, :] = value.astype(BF16)
            valid = (position < limit).astype(F32)
            return total + jnp.sum(valid * value * value, axis=0, keepdims=True)

        add_row(9, lax.fori_loop(0, 4, body, jnp.zeros((1, width), F32)))
        send_rows(
            lambda z: patch_send.at[pl.ds(pl.multiple_of(z * patch_part, patch_part), patch_part)],
            patch_out.at[seq],
            0,
        )

    def gate_weight():
        need(got.normed, got.grad_gate)
        wide_grad(0)

    def up_weight():
        need(got.normed, got.grad_up)
        wide_grad(1)
        got.normed_one = load(hbm.normed_one, normed)

    def down_weight():
        need(got.mlp_hidden, got.grad_mlp)
        tall_grad()

    def cross_some(first_pair, last_pair):
        need(got.queries, got.keys, got.values, got.grad_mix, got.cross_norms)
        cross_pairs(first_pair, last_pair)

    def late_patches():
        need(got.c_key, got.c_value)
        patch_grads()

    def late_keys():
        need(got.patch)
        half = width // 2
        for slot, right in ((0, keys), (1, values)):
            for h in range(2):
                columns = slice(h * half, (h + 1) * half)
                weights[slot, columns] = dot_tn(patch[:, columns], right[...]).astype(BF16)
        got.grad_k = load(hbm.grad_k_early, keys)
        got.grad_v = load(hbm.grad_v_early, values)
        got.patch_early = load(hbm.patch_early, patch)

    def query_weight():
        need(got.normed_two)
        weight_grad(1, normed_two, queries)

    def key_weight():
        need(got.grad_k, got.patch_early)
        weight_grad(2, patch, keys, weights.at[0])

    def value_weight():
        need(got.grad_v, got.patch_early)
        weight_grad(3, patch, values, weights.at[1])
        got.w_query = load(w_query, weights.at[0])
        got.w_key = load(w_key, weights.at[1])

    def self_loads():
        got.self_q = load(hbm.self_q, self_q)
        got.self_k = load(hbm.self_k, self_k)
        got.self_v = load(hbm.self_v, self_v)
        got.self_mix = load(hbm.self_mix, self_mix)
        got.hidden = load(hbm.hidden, hidden)

    def out_weight():
        need(got.self_mix)
        weight_grad(4, self_mix, sbranch)

    def self_weight(i, rows):
        need(got.normed_one)
        weight_grad(i, normed, rows)

    def norm_grad(u, gain, w):
        r = lax.rsqrt(jnp.mean(u * u, axis=-1, keepdims=True) + NORM_EPS)
        gw = gain * w
        grad = r * gw - u * (r * r * r) * jnp.mean(gw * u, axis=-1, keepdims=True)
        return grad, jnp.sum(w * u * r, axis=0, keepdims=True)

    def middle(i, total):
        at = pl.ds(pl.multiple_of(i * chunk, chunk), chunk)
        w = dot_nt(queries[at, :], weights[2])
        grad, row = norm_grad(after_self[at, :], g_cross_ref[...].reshape(1, width), w)
        grad = grad_after[at, :] + grad
        grad_after[at, :] = grad
        low_grad = grad.astype(BF16)
        sbranch[at, :] = low_grad
        grad_smix[at, :] = dot_nt(low_grad, weights[3]).astype(BF16)
        return total + row

    def self_inputs():
        need(got.after_self, got.grad_after, got.c_query, got.w_out)
        add_row(1, lax.fori_loop(0, 4, middle, jnp.zeros((1, width), F32)))
        got.w_value = load(w_value, weights.at[2])

    def self_pairs(first_step, last_step):
        def body(i, carry):
            e, p = i // pairs, i % pairs
            rows = pl.ds(pl.multiple_of(e * text, text), text)
            lanes = pl.ds(pl.multiple_of(p * LANES, LANES), LANES)
            dq, dk, dv = backward_pair(
                self_q[rows, lanes],
                self_k[rows, lanes],
                self_v[rows, lanes],
                grad_smix[rows, lanes],
                self_norms[e, p, 0:PAIR],
                lengths_ref[own * seq + e],
                True,
            )
            self_q[rows, lanes] = dq
            self_k[rows, lanes] = dk
            self_v[rows, lanes] = dv
            return carry

        lax.fori_loop(first_step, last_step, body, 0)

    def self_some(first_step, last_step):
        need(got.self_q, got.self_k, got.self_v, got.self_norms)
        self_pairs(first_step, last_step)

    def last(i, carry):
        total, squares = carry
        at = pl.ds(pl.multiple_of(i * chunk, chunk), chunk)
        w = (
            dot_nt(self_q[at, :], weights[0])
            + dot_nt(self_k[at, :], weights[1])
            + dot_nt(self_v[at, :], weights[2])
        )
        grad, row = norm_grad(hidden[at, :].astype(F32), g_self_ref[...].reshape(1, width), w)
        grad = grad_after[at, :] + grad
        e, half = i // 2, i % 2
        position = lax.broadcasted_iota(jnp.int32, (chunk, 1), 0) + half * chunk
        valid = (position < lengths_ref[own * seq + e]).astype(F32)
        low_grad = grad.astype(BF16)
        for k in range(2):
            place = (2 * half + k) * own + e
            grad_mlp[pl.ds(pl.multiple_of(place * part, part), part)] = low_grad[
                k * part : (k + 1) * part
            ]
        return total + row, squares + jnp.sum(valid * grad * grad, axis=0, keepdims=True)

    def inputs_grad():
        need(got.w_query, got.w_key, got.w_value, got.hidden)
        zero = jnp.zeros((1, width), F32)
        total, squares = lax.fori_loop(0, 4, last, (zero, zero))
        add_row(0, total)
        add_row(8, squares)
        leaving = own * part
        send_rows(
            lambda z: grad_mlp.at[pl.ds(pl.multiple_of(z * leaving, leaving), leaving)],
            x_out.at[seq],
            2,
        )
        send_small(0)

    def send_small(i):
        small[i] = remote(
            small_own.at[i], small_got.at[i], small_send.at[i], small_recv.at[i], peers[i]
        )

    def add_small(i):
        small[i].wait_recv()
        small_own[i + 1] = small_own[i] + small_got[i]

    def pass_small(i):
        add_small(i)
        if i < 4:
            send_small(i + 1)

    work = {
        GATE: gate_weight,
        UP: up_weight,
        CROSS_A: lambda: cross_some(0, pairs // 2),
        CROSS_B: lambda: cross_some(pairs // 2, pairs),
        PATCHES: late_patches,
        KEYS: late_keys,
        C_QUERY: query_weight,
        C_KEY: key_weight,
        C_VALUE: value_weight,
        LOADS: self_loads,
        MIDDLE: self_inputs,
        W_OUT: out_weight,
        SELF_A: lambda: self_some(0, pairs),
        SELF_B: lambda: self_some(pairs, 2 * pairs),
        LAST: inputs_grad,
        W_QUERY: lambda: self_weight(5, self_q),
        W_KEY: lambda: self_weight(6, self_k),
        W_VALUE: lambda: self_weight(7, self_v),
    }
    exchange = {
        CORE: over_core,
        GO: leave_two,
        TWO: over_two,
        THREE: over_three,
        NEAR: over_near,
        FAR: over_far,
        SMALL: pass_small,
    }
    pl.semaphore_wait(barrier, len(peers))
    first[3] = remote(
        hbm.dw_c_out.at[:, :, 1 - core],
        got_core[3],
        send_sem.at[0, 3],
        recv_sem.at[0, 3],
        to_core,
    )

    for e, (dst, number) in enumerate(((layer_out, 1), (layer_late_out, 4))):
        send_rows(
            lambda z, e=e: hbm.layer.at[
                pl.ds(pl.multiple_of(e * text + z * part, part), part)
            ],
            dst.at[seq],
            number,
        )
    send_rows(lambda z: hbm.patch_grad_early.at[z], early_out.at[seq], 3)
    down_weight()
    give(2, tall_units.at[1])
    for step in TAIL_ORDER:
        if isinstance(step, tuple):
            exchange[step[0]](step[1])
        else:
            work[step]()
    small_out[...] = small_own[5]
    for copy in outs:
        copy.wait_recv()
    for copy in locals_:
        copy.wait()
    for u, copy in first.items():
        if u not in first_sent:
            copy.wait_send()
    for copies in (second, third, near, far, small):
        for copy in copies.values():
            copy.wait_send()
    for copy in outs:
        copy.wait_send()


def finish_kernel(groups, ff_width, *refs):
    narrow_ref, wide_ref, small_ref, patch_first, patch_rest, patch_late = refs[:6]
    layer_early, layer_late, x_in = refs[6:9]
    layer_out, x_out, patch_out, gain_self, gain_cross, gain_mlp, rms_out = refs[9:16]
    out_refs = refs[16:]
    step = pl.program_id(0)
    split = patch_first.shape[1]
    x_out[...] = x_in[...].astype(F32)
    patch_out[0, :split] = patch_first[0].astype(F32)
    patch_out[0, split:] = patch_rest[0].astype(F32)
    patch_out[1] = patch_late[0].astype(F32)
    layer_out[0] = layer_early[0].astype(F32)
    layer_out[1] = layer_late[0].astype(F32)

    @pl.when(step == 0)
    def sums():
        for buffer, row, rows, members in groups:
            total = (narrow_ref, wide_ref)[buffer][row : row + rows]
            part = total.shape[1] // 2
            if len(members) == 2:
                out_refs[members[0]][...] = total[:, :part]
                out_refs[members[1]][...] = total[:, part:]
            else:
                out_refs[members[0]][0:rows] = total[:, :part]
                out_refs[members[0]][rows:] = total[:, part:]
        small = small_ref[...]
        width = small.shape[1]
        piece = width // 8
        for i, gain in enumerate((gain_self, gain_cross, gain_mlp)):
            for d in range(8):
                value = small[i, d * piece : (d + 1) * piece]
                pl.when(lax.axis_index("dp") == d)(partial(store, gain, value))
        squares = jnp.sum(small, axis=1, keepdims=True)
        row = lax.broadcasted_iota(jnp.int32, (small.shape[0], LANES), 0)
        lane = lax.broadcasted_iota(jnp.int32, (small.shape[0], LANES), 1)
        squares = jnp.sum(jnp.where(row == lane + 3, squares, 0.0), axis=0, keepdims=True)
        lane = lane[0:1]
        texts, patch_count = small[10:11, 0:1], small[10:11, 1:2]
        count = jnp.where(
            lane == 6, patch_count * width, jnp.where(lane == 4, texts * ff_width, texts * width)
        )
        rms_out[...] = jnp.sqrt(squares / count)[0, 0 : rms_out.shape[0]]


def store(ref, value):
    ref[...] = value


def takes_kernel(width, n_dp, n_seq, own):
    return (
        n_dp == 8
        and n_seq == 4
        and own == 2
        and width // n_dp % 32 == 0
        and width % (2 * LANES) == 0
    )


def backward_tail(lengths, counts, g_self, g_cross, small, state, weights):
    n_square, n_late = 8, 4
    own, pairs, _, text = state.self_norms.shape
    count, width = state.self_q.shape
    ff_width = state.mlp_hidden.shape[1]
    block, tall = width // 8, ff_width // 8
    tops = ((n_square // 2 * block + tall // 2, width // 2), (block, ff_width // 2))
    state = state._replace(dw_c_out=state.dw_c_out.reshape(2, 2, 2, block, width))
    slots = state.k_late.shape[0]
    vmem = pl.BlockSpec(memory_space=pltpu.VMEM)
    anywhere = pl.BlockSpec(memory_space=pl.ANY)
    smem = pl.BlockSpec(memory_space=pltpu.SMEM)

    def low(*shape):
        return pltpu.VMEM(shape, BF16)

    def wide(*shape):
        return pltpu.VMEM(shape, F32)

    units = n_square + 3
    n_groups = n_square // 2 + 2
    return pl.pallas_call(
        tail_kernel,
        out_shape=tuple(jax.ShapeDtypeStruct(t, F32) for t in tops + (small.shape,))
        + (
            jax.ShapeDtypeStruct(state.patch_grad_early.shape, BF16),
            jax.ShapeDtypeStruct((4, slots // 4, width), BF16),
            jax.ShapeDtypeStruct((4, count // 4, width), BF16),
            jax.ShapeDtypeStruct((4, text // 4, width), BF16),
            jax.ShapeDtypeStruct((4, text // 4, width), BF16),
        ),
        in_specs=[smem] * 2 + [vmem] * 3 + [anywhere] * (len(state) + len(weights)),
        out_specs=(vmem,) * 3 + (anywhere,) * 5,
        scratch_shapes=[
            wide(count, width),
            wide(count, width),
            low(count, width),
            low(count, width),
            low(count, width),
            low(3, count, ff_width),
            low(count, width),
            low(4 * slots, width),
            low(text, width),
            wide(*state.cross_norms.shape),
            wide(*state.self_norms.shape),
            low(4, width, width),
            low(3, 2, 2, block, ff_width),
            low(2, 2, 2, tall, width),
            low(2, 2, 2, block, ff_width),
            low(2, 2, tall, width),
            low(2, 2, block, ff_width),
            low(2, tall, width),
            low(2, block, ff_width),
            low(tall, width),
            low(n_square + 2, 2, 2, block, width),
            low(n_square, 2, 2, block, width),
            low(n_square, 2, block, width),
            low(n_square, block, width),
            low(2, 2, *tops[0]),
            low(2, *tops[0]),
            low(*tops[0]),
            low(2, 2, *tops[1]),
            low(2, *tops[1]),
            low(*tops[1]),
            wide(6, *small.shape),
            wide(5, *small.shape),
            pltpu.SemaphoreType.DMA((32,)),
            pltpu.SemaphoreType.DMA((3, units)),
            pltpu.SemaphoreType.DMA((3, units)),
            pltpu.SemaphoreType.DMA((5,)),
            pltpu.SemaphoreType.DMA((5,)),
            pltpu.SemaphoreType.DMA((2, n_groups)),
            pltpu.SemaphoreType.DMA((2, n_groups)),
            pltpu.SemaphoreType.DMA((5, 3)),
            pltpu.SemaphoreType.DMA((5, 3)),
            pltpu.SemaphoreType.DMA((5,)),
        ],
        compiler_params=pltpu.CompilerParams(
            collective_id=0, has_side_effects=True, vmem_limit_bytes=TAIL_VMEM
        ),
    )(lengths, counts, g_self, g_cross, small, *state, *weights)


def finish(narrow, wide_total, total, patches, layers, x_rows):
    n_square = 8
    parts, patch_part, width = patches[2].shape
    part = layers[0].shape[1]
    examples = 2 * parts
    block, ff_width = width // 8, 2 * wide_total.shape[1]
    tall = 2 * (narrow.shape[0] - n_square // 2 * block)
    groups = [(1, 0, block, (0, 1)), (0, n_square // 2 * block, tall // 2, (2,))]
    groups += [(0, i * block, block, (3 + 2 * i, 4 + 2 * i)) for i in range(n_square // 2)]
    shapes = [(block, ff_width // 4)] * 2 + [(tall, width // 4)] + [(block, width // 4)] * n_square

    def whole(shape):
        return pl.BlockSpec(shape, lambda e: (0,) * len(shape))

    def one(rows):
        return pl.BlockSpec((1, rows, width), lambda e: (e, 0, 0))

    def both(rows):
        return pl.BlockSpec((2, rows, width), lambda e: (e, 0, 0))

    outs = [
        ((examples, part, width), both(part)),
        ((examples, part, width), both(part)),
        ((examples, patch_part, width), both(patch_part)),
        ((block,), whole((block,))),
        ((block,), whole((block,))),
        ((block,), whole((block,))),
        ((7,), whole((7,))),
    ] + [(s, whole(s)) for s in shapes]
    results = pl.pallas_call(
        partial(finish_kernel, groups, ff_width),
        grid=(parts,),
        out_shape=tuple(jax.ShapeDtypeStruct(s, F32) for s, _ in outs),
        in_specs=[whole(narrow.shape), whole(wide_total.shape), whole(total.shape)]
        + [one(p.shape[1]) for p in patches]
        + [one(part)] * 2
        + [both(part)],
        out_specs=tuple(spec for _, spec in outs),
        compiler_params=pltpu.CompilerParams(vmem_limit_bytes=TAIL_VMEM),
    )(narrow, wide_total, total, *patches, *layers, x_rows)
    return results[:3], results[3:6], results[6], results[7:]


def norm_forward(u, gain):
    r = lax.rsqrt(jnp.mean(u * u, axis=-1, keepdims=True) + NORM_EPS)
    return (u * r * gain).astype(BF16)


def norm_backward(u, gain, w):
    r = lax.rsqrt(jnp.mean(u * u, axis=-1, keepdims=True) + NORM_EPS)
    gw = gain * w
    grad = r * gw - u * (r * r * r) * jnp.mean(gw * u, axis=-1, keepdims=True)
    return grad, jnp.sum(w * u * r, axis=0, keepdims=True)


def to_examples(rows):
    n = lax.axis_size("seq")
    examples, part, width = rows.shape
    parts = lax.all_to_all(rows.reshape(n, examples // n, part, width), "seq", 0, 0)
    return parts.transpose(1, 0, 2, 3).reshape(examples // n, n * part, width)


def to_positions(rows):
    n = lax.axis_size("seq")
    own, positions, width = rows.shape
    parts = rows.reshape(own, n, positions // n, width).transpose(1, 0, 2, 3)
    return lax.all_to_all(parts, "seq", 0, 0).reshape(n * own, positions // n, width)


def halve_over_dp(matrix, bits):
    n = lax.axis_size("dp")
    count = n.bit_length() - 1
    rows, width = matrix.shape[0] // n, matrix.shape[1]
    place = lax.axis_index("dp")
    left = list(range(count))[::-1]
    current = matrix.reshape((2,) * count + (rows, width))
    for bit in bits:
        axis = left.index(bit)
        mine = (place >> bit) & 1
        keep = lax.dynamic_index_in_dim(current, mine, axis, keepdims=False)
        give = lax.dynamic_index_in_dim(current, 1 - mine, axis, keepdims=False)
        got = lax.ppermute(give, "dp", [(i, i ^ (1 << bit)) for i in range(n)])
        current = (keep.astype(F32) + got.astype(F32)).astype(BF16)
        left.remove(bit)
    return current


def scatter_over_seq(matrix):
    n = lax.axis_size("seq")
    rows, width = matrix.shape
    parts = matrix.reshape(rows, n, width // n).transpose(1, 0, 2)
    return jnp.sum(lax.all_to_all(parts, "seq", 0, 0).astype(F32), axis=0)


def reduce_grad(matrix, order):
    n = lax.axis_size("dp")
    bits = list(range(n.bit_length() - 1))
    if order:
        bits = bits[:1] + bits[1:][::-1]
    return scatter_over_seq(halve_over_dp(matrix, bits))


def local(
    hidden_in,
    patches,
    text_lengths,
    patch_counts,
    cotangent,
    g_self,
    g_cross,
    g_mlp,
    w_query,
    w_key,
    w_value,
    w_out,
    c_query,
    c_key,
    c_value,
    c_out,
    w_gate,
    w_up,
    w_down,
):
    n_seq = lax.axis_size("seq")
    n_dp = lax.axis_size("dp")
    seq_place = lax.axis_index("seq")
    dp_place = lax.axis_index("dp")
    width = hidden_in.shape[2]
    ff_width = w_gate.shape[1]
    own = hidden_in.shape[0] // n_seq
    if takes_kernel(width, n_dp, n_seq, own):
        small, patch_early, state = forward_head(
            text_lengths[0],
            patch_counts,
            (g_self, g_cross, g_mlp),
            (hidden_in, patches, cotangent),
            (
                w_query,
                w_key,
                w_value,
                w_out,
                c_query,
                c_key,
                c_value,
                c_out,
                w_gate,
                w_up,
                w_down,
            ),
        )
        narrow, wide, total, patch_rest, patch_late, x_out, *layers = backward_tail(
            text_lengths[0],
            patch_counts,
            g_self,
            g_cross,
            small,
            state,
            (c_key, c_value, c_query, w_out, w_query, w_key, w_value),
        )
        rows, gains, rms_values, grads = finish(
            narrow,
            wide,
            total,
            (patch_early, patch_rest, patch_late),
            layers,
            x_out.reshape(hidden_in.shape),
        )
        gate, up, down, c_o, c_q, c_k, c_v, w_o, w_q, w_k, w_v = grads
        return (
            *rows,
            *gains,
            w_q,
            w_k,
            w_v,
            w_o,
            c_q,
            c_k,
            c_v,
            c_o,
            gate,
            up,
            down,
            rms_values,
        )
    else:
        lengths = lax.dynamic_slice_in_dim(text_lengths[0], seq_place * own, own)
        counts = lax.dynamic_slice_in_dim(patch_counts, seq_place * own, own)

        hidden = to_examples(hidden_in)
        patch = to_examples(patches)
        text = hidden.shape[1]
        slots = patch.shape[1]
        text_valid = (jnp.arange(text)[None, :] < lengths[:, None]).astype(F32).reshape(-1, 1)
        patch_valid = (jnp.arange(slots)[None, :] < counts[:, None]).astype(F32).reshape(-1, 1)
        x = hidden.reshape(-1, width).astype(F32)
        patch = patch.reshape(-1, width)
        self_flops = 4 * own * text * text * width
        cross_flops = 4 * own * text * slots * width

        normed_one = norm_forward(x, g_self)
        self_q = dot_nn(normed_one, w_query).astype(BF16)
        self_k = dot_nn(normed_one, w_key).astype(BF16)
        self_v = dot_nn(normed_one, w_value).astype(BF16)
        self_mix, self_norms = attend(
            self_forward_kernel, lengths, (self_q, self_k, self_v), None, own, self_flops
        )
        cot = to_examples(cotangent)
        self_branch = dot_nn(self_mix, w_out)
        after_self = x + self_branch
        normed_two = norm_forward(after_self, g_cross)
        cross_q = dot_nn(normed_two, c_query).astype(BF16)
        cross_k = dot_nn(patch, c_key).astype(BF16)
        cross_v = dot_nn(patch, c_value).astype(BF16)
        cross_mix, cross_norms = attend(
            cross_forward_kernel, counts, (cross_q, cross_k, cross_v), None, own, cross_flops
        )
        cross_branch = dot_nn(cross_mix, c_out)
        after_cross = after_self + cross_branch
        normed_three = norm_forward(after_cross, g_mlp)
        gate = dot_nn(normed_three, w_gate)
        up = dot_nn(normed_three, w_up)
        tanh_part = jnp.tanh(GELU_CURVE * (gate + 0.044715 * gate * gate * gate))
        gelu = 0.5 * gate * (1.0 + tanh_part)
        gelu_slope = 0.5 * (1.0 + tanh_part) + 0.5 * gate * (1.0 - tanh_part * tanh_part) * (
            GELU_CURVE * (1.0 + 3.0 * 0.044715 * gate * gate)
        )
        hidden_value = gelu * up
        hidden_low = hidden_value.astype(BF16)
        mlp_branch = dot_nn(hidden_low, w_down)
        layer_rows = after_cross + mlp_branch

        grad_y = cot.reshape(-1, width).astype(F32) * text_valid
        grad_mlp = grad_y.astype(BF16)
        grad_hidden = dot_nt(grad_mlp, w_down)
        grad_gate = (grad_hidden * up * gelu_slope).astype(BF16)
        grad_up = (grad_hidden * gelu).astype(BF16)
        grad_mlp_rows = (
            dot_tn(normed_three, grad_gate).astype(BF16),
            dot_tn(normed_three, grad_up).astype(BF16),
            dot_tn(hidden_low, grad_mlp).astype(BF16),
        )
        grad_three = dot_nt(grad_gate, w_gate) + dot_nt(grad_up, w_up)
        norm_grad, grad_g_mlp = norm_backward(after_cross, g_mlp, grad_three)
        grad_after_cross = grad_y + norm_grad
        grad_cbranch = grad_after_cross.astype(BF16)
        grad_cmix = dot_nt(grad_cbranch, c_out).astype(BF16)

        def square_row(valid, value):
            return jnp.sum(valid * value * value, axis=0, keepdims=True)

        lane = jnp.arange(LANES)
        valid_row = jnp.where(
            lane == 0, jnp.sum(lengths), jnp.where(lane == 1, jnp.sum(counts), 0)
        ).astype(F32)
        layer_low = layer_rows.astype(BF16)
        grad_cq, grad_ck, grad_cv = attend(
            cross_backward_kernel,
            counts,
            (cross_q, cross_k, cross_v, grad_cmix),
            cross_norms,
            own,
            cross_flops * 5 // 2,
        )
        grad_patch_rows = dot_nt(grad_ck, c_key) + dot_nt(grad_cv, c_value)
        grad_two = dot_nt(grad_cq, c_query)
        norm_grad, grad_g_cross = norm_backward(after_self, g_cross, grad_two)
        grad_after_self = grad_after_cross + norm_grad
        grad_sbranch = grad_after_self.astype(BF16)
        grad_smix = dot_nt(grad_sbranch, w_out).astype(BF16)
        grad_sq, grad_sk, grad_sv = attend(
            self_backward_kernel,
            lengths,
            (self_q, self_k, self_v, grad_smix),
            self_norms,
            own,
            self_flops * 5 // 2,
        )
        grad_one = dot_nt(grad_sq, w_query) + dot_nt(grad_sk, w_key) + dot_nt(grad_sv, w_value)
        norm_grad, grad_g_self = norm_backward(x, g_self, grad_one)
        grad_x_rows = grad_after_self + norm_grad
        layer_out = to_positions(layer_low.reshape(own, text, width))
        patch_out = to_positions(grad_patch_rows.astype(BF16).reshape(own, slots, width))
        x_out = to_positions(grad_x_rows.astype(BF16).reshape(own, text, width))
        grads = [
            dot_tn(rows, grad_rows).astype(BF16)
            for rows, grad_rows in (
                (normed_one, grad_sq),
                (normed_one, grad_sk),
                (normed_one, grad_sv),
                (self_mix, grad_sbranch),
                (normed_two, grad_cq),
                (patch, grad_ck),
                (patch, grad_cv),
                (cross_mix, grad_cbranch),
            )
        ]
        grads += grad_mlp_rows
        summed = tuple(reduce_grad(g, u % 2) for u, g in enumerate(grads))
        vectors = [
            grad_g_self,
            grad_g_cross,
            grad_g_mlp,
            square_row(text_valid, layer_rows),
            square_row(text_valid, self_branch),
            square_row(text_valid, cross_branch),
            square_row(text_valid, mlp_branch),
            square_row(text_valid, hidden_value),
            square_row(text_valid, grad_x_rows),
            square_row(patch_valid, grad_patch_rows),
            valid_row[None],
        ]
        folded = [
            sum(
                jnp.pad(p, ((0, 0), (0, width - p.shape[1])))
                for p in jnp.split(v, list(range(width, v.shape[1], width)), axis=1)
            )
            for v in vectors
        ]
        total = lax.psum(jnp.concatenate(folded), ("dp", "seq"))
    part = width // n_dp
    gains = [lax.dynamic_slice(total, (i, dp_place * part), (1, part))[0] for i in range(3)]
    squares = jnp.sum(total[3:10], axis=1)
    place = jnp.arange(7)
    texts, patch_count = total[10, 0], total[10, 1]
    per_value = jnp.where(
        place == 6, patch_count * width, jnp.where(place == 4, texts * ff_width, texts * width)
    )
    rms_values = jnp.sqrt(squares / per_value)
    return (
        layer_out.astype(F32),
        x_out.astype(F32),
        patch_out.astype(F32),
        gains[0],
        gains[1],
        gains[2],
        *summed,
        rms_values,
    )


def solution(mesh):
    rows = P("dp", "seq", None)
    tile = P("dp", "seq")
    in_specs = (rows, rows, P("dp", None), P("dp"), rows) + (P(),) * 14
    out_specs = (rows,) * 3 + (P("dp"),) * 3 + (tile,) * 11 + (P(),)
    return jax.shard_map(local, mesh=mesh, in_specs=in_specs, out_specs=out_specs, check_vma=False)
```
